512 devices in a mesh: space: 64 (over x, z), tile: 8 (over y, core).
Axes of the slice: x: 4, y: 4, z: 16, core: 2. Of those that a mesh axis runs over, the one named last changes fastest.
Arguments:
- features: bfloat16 [512, 64, 8, 128], P('space', 'tile'), may hold values from -6 to 6
- occupancy: int32 [512, 64, 8], P('space', 'tile'), may hold values 0 or 1
- kernel: bfloat16 [27, 128, 128], replicated, may hold values from -0.109375 to 0.109375
- cotangent: bfloat16 [512, 64, 8, 128], P('space', 'tile'), may hold values from -6 to 6
Outputs:
- outputs: bfloat16 [512, 64, 8, 128], P('space', 'tile')
- feature_grad: bfloat16 [512, 64, 8, 128], P('space', 'tile')
- kernel_grad: float32 [27, 128, 128], replicated
The draws below stay inside these ranges and needn't reach their ends.
All inputs are finite; a program needn't handle non-finite values. No bound on the sum of `occupancy` on one device may be relied on, other than what follows from the above.
Results may differ from the reference program's by a relative error of at most 0.001.
Values may be sent and summed in bfloat16 or wider, within the bound.
A program may use at most 64 MiB of HBM per device.

```python
import math
import jax
import jax.numpy as jnp
from jax import lax

C = 128
NX = 512
NY = 64
NZ = 8


def touch_ends(array, key, least, top_value):
    shape = array.shape
    place = [jax.random.randint(jax.random.fold_in(key, axis), (), 0, shape[axis]) for axis in range(len(shape))]
    array = array.at[tuple(place)].set(least)
    longest = shape.index(max(shape))
    place[longest] = (place[longest] + 1) % shape[longest]
    return array.at[tuple(place)].set(top_value)


def shard_levels(own_key, dims, cuts, smallest, high):
    level, own = 1.0, jax.random.fold_in(own_key, 6)
    for position, shards_of in cuts:
        draws = jnp.exp(jax.random.uniform(jax.random.fold_in(own, position), (shards_of,), jnp.float32, smallest / len(cuts), high / len(cuts)))
        level = level * jnp.repeat(draws, dims[position] // shards_of).reshape([-1 if axis == position else 1 for axis in range(len(dims))])
    return level


def noise(stream_key, extent, scale, bound, cuts=(), dtype=jnp.bfloat16):
    loudness = shard_levels(stream_key, extent, cuts, -0.22, 0.18) if cuts else 1.0
    entries = jax.random.normal(stream_key, extent, jnp.float32) * scale * loudness
    return jnp.minimum(jnp.maximum(entries, -bound), bound).astype(dtype)


def setup_inputs(seed: int = 0) -> dict:
    key_list = jax.random.split(jax.random.key(seed), 5)
    features = noise(key_list[0], (NX, NY, NZ, C), 1.0, 6.0, ((0, 64), (1, 8)))
    occupancy = touch_ends((jax.random.randint(key_list[1], (NX, NY, NZ), 0, 2) < 1).astype(jnp.int32), jax.random.fold_in(key_list[1], 1), 0, 1)
    kernel = noise(key_list[2], (27, C, C), (27 * C) ** -0.5, 0.109375)
    cotangent = noise(key_list[3], (NX, NY, NZ, C), 1.0, 6.0, ((0, 64), (1, 8)))
    return {"features": features, "occupancy": occupancy, "kernel": kernel, "cotangent": cotangent}


def convolve(padded, weight):
    size_x = padded.shape[0] - 2
    size_y = padded.shape[1] - 2
    size_z = padded.shape[2] - 2
    width_out = weight.shape[2]
    total = jnp.zeros((size_x * size_y * size_z, width_out), jnp.float32)
    for shift_x in range(3):
        for shift_y in range(3):
            stacked = jnp.concatenate([padded[shift_x:shift_x + size_x, shift_y:shift_y + size_y, shift_z:shift_z + size_z, :] for shift_z in range(3)], axis=-1)
            stacked = stacked.reshape(size_x * size_y * size_z, -1)
            first = 9 * shift_x + 3 * shift_y
            total = total + jnp.dot(stacked, weight[first:first + 3].reshape(-1, width_out), preferred_element_type=jnp.float32)
    return total.reshape(size_x, size_y, size_z, width_out)

def kernel_terms(padded, grads):
    size_x, size_y, size_z, width = grads.shape
    flat_grads = grads.reshape(size_x * size_y * size_z, width)
    pieces = []
    for shift_x in range(3):
        for shift_y in range(3):
            stacked = jnp.concatenate([padded[shift_x:shift_x + size_x, shift_y:shift_y + size_y, shift_z:shift_z + size_z, :] for shift_z in range(3)], axis=-1)
            stacked = stacked.reshape(size_x * size_y * size_z, -1)
            product = lax.dot_general(stacked, flat_grads, (((0,), (0,)), ((), ())), preferred_element_type=jnp.float32)
            pieces.append(product.reshape(3, width, width))
    return jnp.concatenate(pieces, axis=0)

def reference(features, occupancy, kernel, cotangent):
    mask_low = occupancy.astype(jnp.bfloat16)[..., None]
    mask_full = occupancy.astype(jnp.float32)[..., None]
    masked = features * mask_low
    masked_grad = cotangent * mask_low
    widths = ((1, 1), (1, 1), (1, 1), (0, 0))
    padded = jnp.pad(masked, widths)
    padded_grad = jnp.pad(masked_grad, widths)
    outputs = (convolve(padded, kernel) * mask_full).astype(jnp.bfloat16)
    flipped = jnp.transpose(kernel[::-1], (0, 2, 1))
    feature_grad = (convolve(padded_grad, flipped) * mask_full).astype(jnp.bfloat16)
    scale = 1.0 / math.sqrt(NX * NY * NZ)
    kernel_grad = kernel_terms(padded, masked_grad) * scale
    return (outputs, feature_grad, kernel_grad)
```

```python
import functools
import math

import jax
import jax.numpy as jnp
from jax import lax
from jax.experimental import pallas as pl
from jax.experimental.pallas import tpu as pltpu
from jax.sharding import PartitionSpec as P

MESH = pl.DeviceIdType.MESH
CHIPS = (4, 4, 16)
C = 128
DIRS = ((1, 0), (-1, 0), (0, 1), (0, -1), (1, 1), (1, -1), (-1, 1), (-1, -1))
F32 = jnp.float32
BF16 = jnp.bfloat16


def dot(a, b):
    return jnp.dot(a, b, preferred_element_type=F32)


def kernel(
    chips,
    scale,
    feat_hbm,
    occ_hbm,
    kern_hbm,
    cot_hbm,
    out_hbm,
    fgrad_hbm,
    kgrad_hbm,
    feat_v,
    cot_v,
    occ_v,
    kern_v,
    kern_t,
    mask_v,
    features_t,
    padded,
    wide_f,
    wide_g,
    send_face,
    send_corner,
    recv_face,
    recv_corner,
    part,
    pair_buf,
    first_buf,
    second_buf,
    tiles,
    z_buf,
    total,
    out_v,
    fgrad_v,
    in_sem,
    out_sem,
    halo_send,
    halo_recv,
    pair_send,
    pair_recv,
    first_send,
    first_recv,
    second_send,
    second_recv,
    z_send,
    z_recv,
    zg_send,
    zg_recv,
    sg_send,
    sg_recv,
    fg_send,
    fg_recv,
    pg_send,
    pg_recv,
):
    nx, ny, nz = chips
    n_space, n_tile = nx * nz, ny * 2
    space, tile = lax.axis_index("space"), lax.axis_index("tile")
    x, z = space // nz, space % nz
    y, core = tile // 2, tile % 2
    block = C // nx
    block_y = C // ny
    rows = C // (nx * ny)
    per_owner = -(-14 // nz)
    owners = 14 // per_owner

    def at(px, py, pz, pc):
        return {"space": px * nz + pz, "tile": py * 2 + pc}

    def x_peer(d):
        return (x + d) % nx

    def y_peer(d):
        return (y + d) % ny

    def z_peer(d):
        return (z + d) % nz

    def halo_peer(i):
        ds, dt = DIRS[i]
        return {
            "space": (space + ds + n_space) % n_space,
            "tile": (tile + dt + n_tile) % n_tile,
        }

    sibling = at(x, y, z, 1 - core)

    barrier = pltpu.get_barrier_semaphore()

    def greet(device):
        pl.semaphore_signal(barrier, inc=1, device_id=device, device_id_type=MESH)

    for i in range(8):
        greet(halo_peer(i))
    greet(sibling)
    for d in range(1, nx):
        greet(at(x_peer(d), y, z, core))
    for d in range(1, ny):
        greet(at(x, y_peer(d), z, core))

    def greet_z(d, carry):
        greet(at(x, y, z_peer(d), core))
        return carry

    lax.fori_loop(1, nz, greet_z, 0)

    loads = [
        pltpu.make_async_copy(src, dst, in_sem.at[i])
        for i, (src, dst) in enumerate(
            ((occ_hbm, occ_v), (cot_hbm, cot_v), (feat_hbm, feat_v), (kern_hbm, kern_v))
        )
    ]
    for load in loads:
        load.start()

    loads[0].wait()
    cells = occ_v[...].reshape(64, 8).astype(F32).astype(BF16)
    pick = lax.broadcasted_iota(jnp.int32, (512, 64), 0) // 8
    pick = (pick == lax.broadcasted_iota(jnp.int32, (512, 64), 1)).astype(F32)
    spread = dot(pick.astype(BF16), cells)
    own = lax.broadcasted_iota(jnp.int32, (512, 8), 0) % 8
    own = own == lax.broadcasted_iota(jnp.int32, (512, 8), 1)
    column = jnp.sum(jnp.where(own, spread, 0.0), axis=1, keepdims=True)
    mask_v[...] = jnp.broadcast_to(column, (512, C)).reshape(8, 8, 8, C)

    def masked_of(source):
        return source[...].astype(F32) * mask_v[...]

    def fill_halo(which, value):
        edge_x = {1: value[7], -1: value[0]}
        edge_y = {1: value[:, 7], -1: value[:, 0]}
        for i in range(2):
            send_face[which, i] = edge_x[DIRS[i][0]].reshape(64, C).astype(BF16)
        for i in range(2, 4):
            send_face[which, i] = edge_y[DIRS[i][1]].reshape(64, C).astype(BF16)
        for i in range(4, 8):
            corner = edge_x[DIRS[i][0]][7 if DIRS[i][1] == 1 else 0]
            send_corner[which, i - 4] = jnp.concatenate([corner, corner], axis=0).astype(BF16)

    def halo_copies(which):
        copies = []
        for i in range(8):
            if i < 4:
                source, target = send_face.at[which, i], recv_face.at[which, i]
            else:
                source, target = send_corner.at[which, i - 4], recv_corner.at[which, i - 4]
            copies.append(
                pltpu.make_async_remote_copy(
                    src_ref=source,
                    dst_ref=target,
                    send_sem=halo_send.at[which, i],
                    recv_sem=halo_recv.at[which, i],
                    device_id=halo_peer(i),
                    device_id_type=MESH,
                )
            )
        return copies

    inside = {
        (0, 1): (space > 0).astype(F32),
        (0, -1): (space < n_space - 1).astype(F32),
        (1, 1): (tile > 0).astype(F32),
        (1, -1): (tile < n_tile - 1).astype(F32),
    }

    def place_halo(which):
        for i in range(8):
            ds, dt = DIRS[i]
            valid = 1.0
            if ds:
                valid = valid * inside[0, ds]
            if dt:
                valid = valid * inside[1, dt]
            row, col = {1: 0, -1: 9}.get(ds), {1: 0, -1: 9}.get(dt)
            if i < 4:
                value = recv_face[which, i].astype(F32).reshape(8, 8, C) * valid
            else:
                value = recv_corner[which, i - 4].astype(F32)[0:8] * valid
            if ds == 0:
                padded[1:9, col] = value
            elif dt == 0:
                padded[row, 1:9] = value
            else:
                padded[row, col] = value

    z_place = lax.broadcasted_iota(jnp.int32, (10, 8, C), 1)

    def widen(target):
        def slab(i, carry):
            value = padded[i]
            before = jnp.where(z_place == 0, 0.0, pltpu.roll(value, 1, 1))
            after = jnp.where(z_place == 7, 0.0, pltpu.roll(value, 7, 1))
            start = pl.multiple_of(i * 64, 64)
            for sy in range(3):
                for sz, shifted in enumerate((before, value, after)):
                    column = (3 * sy + sz) * C
                    target[pl.ds(start, 64), column : column + C] = (
                        shifted[sy : sy + 8].reshape(64, C).astype(BF16)
                    )
            return carry

        lax.fori_loop(0, 10, slab, 0)

    loads[1].wait()
    masked_grad = masked_of(cot_v)
    padded[1:9, 1:9] = masked_grad
    fill_halo(0, masked_grad)
    pl.semaphore_wait(barrier, 8 + 1 + (nx - 1) + (ny - 1) + (nz - 1))
    halo_g = halo_copies(0)
    for copy in halo_g:
        copy.start()
    loads[2].wait()
    masked = masked_of(feat_v)
    fill_halo(1, masked)
    halo_f = halo_copies(1)
    for copy in halo_f:
        copy.start()
    features_t[...] = jnp.transpose(masked.reshape(512, C)).astype(BF16)

    loads[3].wait()

    def flip(s, carry):
        start = pl.multiple_of(s * C, C)
        kern_t[pl.ds(start, C), :] = jnp.transpose(kern_v[26 - s].astype(F32)).astype(BF16)
        return carry

    lax.fori_loop(0, 27, flip, 0)

    for copy in halo_g:
        copy.wait_recv()
    place_halo(0)
    widen(wide_g)

    def terms(sx, first, last):
        for q in range(first, last, 2):
            end = min(q + 2, last)
            result = dot(features_t[...], wide_g[sx * 64 : sx * 64 + 512, q * C : end * C])
            for j in range(q, end):
                part[26 - (9 * sx + j)] = result[:, (j - q) * C : (j - q + 1) * C]

    mine = core * 14
    theirs = (1 - core) * 14

    def pair_copy(half):
        return pltpu.make_async_remote_copy(
            src_ref=part.at[pl.ds(theirs + 7 * half, 7)],
            dst_ref=pair_buf.at[pl.ds(7 * half, 7)],
            send_sem=pair_send.at[half],
            recv_sem=pair_recv.at[half],
            device_id=sibling,
            device_id_type=MESH,
        )

    part[27] = jnp.zeros((C, C), F32)
    terms(1, 4, 9)
    terms(2, 0, 2)
    terms(0, 0, 6)
    pair = {1: pair_copy(1)}
    pair[1].start()
    terms(2, 2, 9)
    terms(0, 6, 9)
    terms(1, 0, 4)
    pair[0] = pair_copy(0)
    pair[0].start()

    first_size = {0: nx, 1: ny}
    second_size = {0: ny, 1: nx}
    first_block = {0: block, 1: block_y}
    first_place = {0: x * block, 1: y * block_y}
    second_place = {0: x * block + y * rows, 1: y * block_y + x * rows}

    def first_peer(half, d):
        return (x_peer(d), y) if half == 0 else (x, y_peer(d))

    def second_peer(half, d):
        return (x, y_peer(d)) if half == 0 else (x_peer(d), y)

    def first_copies(half):
        copies = []
        for d in range(1, first_size[half]):
            px, py = first_peer(half, d)
            index = px if half == 0 else py
            start = pl.multiple_of(index * first_block[half], 8)
            copies.append(
                pltpu.make_async_remote_copy(
                    src_ref=part.at[pl.ds(mine + 7 * half, 7), pl.ds(start, first_block[half])],
                    dst_ref=first_buf.at[half, d - 1],
                    send_sem=first_send.at[half, d - 1],
                    recv_sem=first_recv.at[half, d - 1],
                    device_id=at(px, py, z, core),
                    device_id_type=MESH,
                )
            )
        return copies

    def second_copies(half):
        copies = []
        base = first_place[half]
        for d in range(1, second_size[half]):
            px, py = second_peer(half, d)
            index = py if half == 0 else px
            start = pl.multiple_of(base + index * rows, 8)
            copies.append(
                pltpu.make_async_remote_copy(
                    src_ref=part.at[pl.ds(mine + 7 * half, 7), pl.ds(start, rows)],
                    dst_ref=second_buf.at[half, d - 1],
                    send_sem=second_send.at[half, d - 1],
                    recv_sem=second_recv.at[half, d - 1],
                    device_id=at(px, py, z, core),
                    device_id_type=MESH,
                )
            )
        return copies

    def add_pair(half):
        pair[half].wait_recv()

        def one(i, carry):
            part[mine + 7 * half + i] = part[mine + 7 * half + i] + pair_buf[7 * half + i]
            return carry

        lax.fori_loop(0, 7, one, 0)

    def add_first(half, copies):
        for copy in copies:
            copy.wait_recv()
        where = pl.ds(pl.multiple_of(first_place[half], 8), first_block[half])
        value = part[pl.ds(mine + 7 * half, 7), where]
        for d in range(1, first_size[half]):
            value = value + first_buf[half, d - 1]
        part[pl.ds(mine + 7 * half, 7), where] = value

    def add_second(half, copies):
        for copy in copies:
            copy.wait_recv()
        where = pl.ds(pl.multiple_of(second_place[half], 8), rows)
        value = part[pl.ds(mine + 7 * half, 7), where]
        for d in range(1, second_size[half]):
            value = value + second_buf[half, d - 1]
        tiles[7 * half : 7 * half + 7] = value

    firsts, seconds = {}, {}
    for half in (1, 0):
        add_pair(half)
        firsts[half] = first_copies(half)
        for copy in firsts[half]:
            copy.start()

    padded[1:9, 1:9] = masked_of(feat_v)
    for copy in halo_f:
        copy.wait_recv()
    place_halo(1)
    widen(wide_f)

    def convolved(wide, weight, target):
        value = dot(wide[0:512, :], weight(0))
        value = value + dot(wide[64:576, :], weight(1))
        value = value + dot(wide[128:640, :], weight(2))
        value = value.reshape(8, 8, 8, C) * mask_v[...]
        target[...] = value.astype(BF16)

    convolved(wide_f, lambda a: kern_v[9 * a : 9 * a + 9].reshape(9 * C, C), out_v)
    out_copy = pltpu.make_async_copy(out_v, out_hbm, out_sem.at[0])
    out_copy.start()

    for half in (1, 0):
        add_first(half, firsts[half])
        seconds[half] = second_copies(half)
        for copy in seconds[half]:
            copy.start()
    for half in (1, 0):
        add_second(half, seconds[half])

    def z_copy(d, target):
        return pltpu.make_async_remote_copy(
            src_ref=tiles.at[pl.ds(target * per_owner, per_owner)],
            dst_ref=z_buf.at[d - 1],
            send_sem=z_send.at[d - 1],
            recv_sem=z_recv.at[d - 1],
            device_id=at(x, y, target, core),
            device_id_type=MESH,
        )

    def z_start(d, carry):
        @pl.when(z_peer(d) < owners)
        def _():
            z_copy(d, z_peer(d)).start()

        return carry

    lax.fori_loop(1, nz, z_start, 0)

    convolved(wide_g, lambda a: kern_t[a * 9 * C : (a + 1) * 9 * C, :], fgrad_v)
    fgrad_copy = pltpu.make_async_copy(fgrad_v, fgrad_hbm, out_sem.at[1])
    fgrad_copy.start()

    def tile_at(owner):
        second_half = (owner * per_owner) // 7
        row = second_place[0] + second_half * (second_place[1] - second_place[0])
        return total.at[pl.ds(mine + owner * per_owner, per_owner), pl.ds(pl.multiple_of(row, 8), rows)]

    def zg_copy(d, owner):
        return pltpu.make_async_remote_copy(
            src_ref=tile_at(owner),
            dst_ref=tile_at(owner),
            send_sem=zg_send.at[d - 1],
            recv_sem=zg_recv.at[d - 1],
            device_id=at(x, y, z_peer(d), core),
            device_id_type=MESH,
        )

    @pl.when(z < owners)
    def _():
        def z_wait(d, carry):
            z_copy(d, z).wait_recv()
            return carry

        lax.fori_loop(1, nz, z_wait, 0)
        value = tiles[pl.ds(z * per_owner, per_owner)]
        for d in range(1, nz):
            value = value + z_buf[d - 1]
        tile_at(z)[...] = value * scale

        def zg_start(d, carry):
            zg_copy(d, z).start()
            return carry

        lax.fori_loop(1, nz, zg_start, 0)

    def zg_wait(d, carry):
        sender = (z - d + nz) % nz

        @pl.when(sender < owners)
        def _():
            zg_copy(d, sender).wait_recv()

        return carry

    lax.fori_loop(1, nz, zg_wait, 0)

    def gathered(half, offsets, row, size):
        return total.at[pl.ds(offsets + 7 * half, 7), pl.ds(pl.multiple_of(row, 8), size)]

    def back(half, level, d, row, size, px, py):
        sends, receives = ((sg_send, sg_recv), (fg_send, fg_recv))[level]
        return pltpu.make_async_remote_copy(
            src_ref=gathered(half, mine, row, size),
            dst_ref=gathered(half, mine, row, size),
            send_sem=sends.at[half, d - 1],
            recv_sem=receives.at[half, d - 1],
            device_id=at(px, py, z, core),
            device_id_type=MESH,
        )

    def pair_back(half, d, offsets, index):
        size = first_block[half]
        return pltpu.make_async_remote_copy(
            src_ref=gathered(half, offsets, index * size, size),
            dst_ref=gathered(half, offsets, index * size, size),
            send_sem=pg_send.at[half, d],
            recv_sem=pg_recv.at[half, d],
            device_id=sibling,
            device_id_type=MESH,
        )

    sent = []
    for half in (1, 0):
        for d in range(1, second_size[half]):
            copy = back(half, 0, d, second_place[half], rows, *second_peer(half, d))
            copy.start()
            sent.append(copy)
    for half in (1, 0):
        mine_at = x if half == 0 else y
        for d in range(1, second_size[half]):
            n = second_size[half]
            from_index = ((y if half == 0 else x) - d + n) % n
            back(half, 0, d, first_place[half] + from_index * rows, rows, x, y).wait_recv()
        for d in range(1, first_size[half]):
            copy = back(half, 1, d, first_place[half], first_block[half], *first_peer(half, d))
            copy.start()
            sent.append(copy)
        copy = pair_back(half, 0, mine, mine_at)
        copy.start()
        sent.append(copy)
    for d in range(1, max(nx, ny)):
        for half in (1, 0):
            n = first_size[half]
            if d < n:
                mine_at = x if half == 0 else y
                from_index = (mine_at - d + n) % n
                back(half, 1, d, from_index * first_block[half], first_block[half], x, y).wait_recv()
                copy = pair_back(half, d, mine, from_index)
                copy.start()
                sent.append(copy)
    for d in range(0, max(nx, ny)):
        for half in (1, 0):
            n = first_size[half]
            if d < n:
                mine_at = x if half == 0 else y
                pair_back(half, d, theirs, (mine_at - d + n) % n).wait_recv()

    kgrad_copy = pltpu.make_async_copy(total.at[0:27], kgrad_hbm, out_sem.at[2])
    kgrad_copy.start()

    for copy in halo_g + halo_f + [pair[0], pair[1]] + sent:
        copy.wait_send()
    for half in (1, 0):
        for copy in firsts[half] + seconds[half]:
            copy.wait_send()

    def z_sent(d, carry):
        @pl.when(z_peer(d) < owners)
        def _():
            z_copy(d, z_peer(d)).wait_send()

        @pl.when(z < owners)
        def _():
            zg_copy(d, z).wait_send()

        return carry

    lax.fori_loop(1, nz, z_sent, 0)
    out_copy.wait()
    fgrad_copy.wait()
    kgrad_copy.wait()


def shards(chips, features, occupancy, weights, cotangent):
    nx, ny, nz = chips
    voxels = 512 * nx * ny * nz * 2
    scale = 1.0 / math.sqrt(voxels)
    rows = C // (nx * ny)
    per_owner = -(-14 // nz)
    most = max(nx, ny)
    dma = pltpu.SemaphoreType.DMA
    return pl.pallas_call(
        functools.partial(kernel, chips, scale),
        out_shape=(
            jax.ShapeDtypeStruct((8, 8, 8, C), BF16),
            jax.ShapeDtypeStruct((8, 8, 8, C), BF16),
            jax.ShapeDtypeStruct((27, C, C), F32),
        ),
        in_specs=[pl.BlockSpec(memory_space=pl.ANY)] * 4,
        out_specs=[pl.BlockSpec(memory_space=pl.ANY)] * 3,
        scratch_shapes=[
            pltpu.VMEM((8, 8, 8, C), BF16),
            pltpu.VMEM((8, 8, 8, C), BF16),
            pltpu.VMEM((8, 8, 8), jnp.int32),
            pltpu.VMEM((27, C, C), BF16),
            pltpu.VMEM((27 * C, C), BF16),
            pltpu.VMEM((8, 8, 8, C), F32),
            pltpu.VMEM((C, 512), BF16),
            pltpu.VMEM((10, 10, 8, C), F32),
            pltpu.VMEM((640, 9 * C), BF16),
            pltpu.VMEM((640, 9 * C), BF16),
            pltpu.VMEM((2, 4, 64, C), BF16),
            pltpu.VMEM((2, 4, 16, C), BF16),
            pltpu.VMEM((2, 4, 64, C), BF16),
            pltpu.VMEM((2, 4, 16, C), BF16),
            pltpu.VMEM((28, C, C), F32),
            pltpu.VMEM((14, C, C), F32),
            pltpu.VMEM((2, most - 1, 7, C // nx, C), F32),
            pltpu.VMEM((2, most - 1, 7, rows, C), F32),
            pltpu.VMEM((14, rows, C), F32),
            pltpu.VMEM((nz - 1, per_owner, rows, C), F32),
            pltpu.VMEM((28, C, C), F32),
            pltpu.VMEM((8, 8, 8, C), BF16),
            pltpu.VMEM((8, 8, 8, C), BF16),
            dma((4,)),
            dma((3,)),
            dma((2, 8)),
            dma((2, 8)),
            dma((2,)),
            dma((2,)),
            dma((2, most - 1)),
            dma((2, most - 1)),
            dma((2, most - 1)),
            dma((2, most - 1)),
            dma((nz - 1,)),
            dma((nz - 1,)),
            dma((nz - 1,)),
            dma((nz - 1,)),
            dma((2, most - 1)),
            dma((2, most - 1)),
            dma((2, most - 1)),
            dma((2, most - 1)),
            dma((2, most)),
            dma((2, most)),
        ],
        compiler_params=pltpu.CompilerParams(
            collective_id=0, has_side_effects=True, vmem_limit_bytes=48 * 1024 * 1024
        ),
        cost_estimate=pl.CostEstimate(
            flops=3 * 2 * 512 * 27 * C * C, bytes_accessed=4_000_000, transcendentals=0
        ),
    )(features, occupancy, weights, cotangent)


def solution(mesh, chips=CHIPS):
    in_specs = (
        P("space", "tile", None, None),
        P("space", "tile", None),
        P(),
        P("space", "tile", None, None),
    )
    out_specs = (P("space", "tile", None, None), P("space", "tile", None, None), P())
    return jax.shard_map(
        functools.partial(shards, chips),
        mesh=mesh,
        in_specs=in_specs,
        out_specs=out_specs,
        check_vma=False,
    )
```

```python
import functools
import math

import jax
import jax.numpy as jnp
from jax import lax
from jax.experimental import pallas as pl
from jax.experimental.pallas import tpu as pltpu
from jax.sharding import PartitionSpec as P

MESH = pl.DeviceIdType.MESH
CHIPS = (4, 4, 16)
C = 128
DIRS = ((1, 0), (-1, 0), (0, 1), (0, -1), (1, 1), (1, -1), (-1, 1), (-1, -1))
F32 = jnp.float32
BF16 = jnp.bfloat16


def dot(a, b):
    return jnp.dot(a, b, preferred_element_type=F32)


def kernel(
    chips,
    scale,
    feat_hbm,
    occ_hbm,
    kern_hbm,
    cot_hbm,
    out_ref,
    fgrad_ref,
    total,
    feat_v,
    cot_v,
    occ_v,
    kern_v,
    kern_t,
    mask_v,
    features_t,
    padded,
    wide_f,
    wide_g,
    send_face,
    send_corner,
    recv_face,
    recv_corner,
    part,
    pair_buf,
    first_buf,
    second_buf,
    tiles,
    z_buf,
    z_all,
    out_v,
    fgrad_v,
    in_sem,
    out_sem,
    own_sem,
    halo_send,
    halo_recv,
    pair_send,
    pair_recv,
    first_send,
    first_recv,
    second_send,
    second_recv,
    z_send,
    z_recv,
    zg_send,
    zg_recv,
    sg_send,
    sg_recv,
    fg_send,
    fg_recv,
    pg_send,
    pg_recv,
):
    nx, ny, nz = chips
    n_space, n_tile = nx * nz, ny * 2
    space, tile = lax.axis_index("space"), lax.axis_index("tile")
    x, z = space // nz, space % nz
    y, core = tile // 2, tile % 2
    block = C // nx
    block_y = C // ny
    rows = C // (nx * ny)
    per_owner = -(-14 // nz)
    slots = nz * per_owner

    def at(px, py, pz, pc):
        return {"space": px * nz + pz, "tile": py * 2 + pc}

    def x_peer(d):
        return (x + d) % nx

    def y_peer(d):
        return (y + d) % ny

    def z_peer(d):
        return (z + d) % nz

    def halo_peer(i):
        ds, dt = DIRS[i]
        return {
            "space": (space + ds + n_space) % n_space,
            "tile": (tile + dt + n_tile) % n_tile,
        }

    sibling = at(x, y, z, 1 - core)

    barrier = pltpu.get_barrier_semaphore()

    def greet(device):
        pl.semaphore_signal(barrier, inc=1, device_id=device, device_id_type=MESH)

    for i in range(8):
        greet(halo_peer(i))
    greet(sibling)
    for d in range(1, nx):
        greet(at(x_peer(d), y, z, core))
    for d in range(1, ny):
        greet(at(x, y_peer(d), z, core))

    def greet_z(d, carry):
        greet(at(x, y, z_peer(d), core))
        return carry

    lax.fori_loop(1, nz, greet_z, 0)

    loads = [
        pltpu.make_async_copy(src, dst, in_sem.at[i])
        for i, (src, dst) in enumerate(
            ((occ_hbm, occ_v), (cot_hbm, cot_v), (feat_hbm, feat_v), (kern_hbm, kern_v))
        )
    ]
    for load in loads:
        load.start()

    loads[0].wait()
    cells = occ_v[...].reshape(64, 8).astype(F32).astype(BF16)
    pick = lax.broadcasted_iota(jnp.int32, (512, 64), 0) // 8
    pick = (pick == lax.broadcasted_iota(jnp.int32, (512, 64), 1)).astype(F32)
    spread = dot(pick.astype(BF16), cells)
    own = lax.broadcasted_iota(jnp.int32, (512, 8), 0) % 8
    own = own == lax.broadcasted_iota(jnp.int32, (512, 8), 1)
    column = jnp.sum(jnp.where(own, spread, 0.0), axis=1, keepdims=True)
    mask_v[...] = jnp.broadcast_to(column, (512, C)).reshape(8, 8, 8, C)

    def masked_of(source):
        return source[...].astype(F32) * mask_v[...]

    def fill_halo(which, value):
        edge_x = {1: value[7], -1: value[0]}
        edge_y = {1: value[:, 7], -1: value[:, 0]}
        for i in range(2):
            send_face[which, i] = edge_x[DIRS[i][0]].reshape(64, C).astype(BF16)
        for i in range(2, 4):
            send_face[which, i] = edge_y[DIRS[i][1]].reshape(64, C).astype(BF16)
        for i in range(4, 8):
            corner = edge_x[DIRS[i][0]][7 if DIRS[i][1] == 1 else 0]
            send_corner[which, i - 4] = jnp.concatenate([corner, corner], axis=0).astype(BF16)

    def halo_copies(which):
        copies = []
        for i in range(8):
            if i < 4:
                source, target = send_face.at[which, i], recv_face.at[which, i]
            else:
                source, target = send_corner.at[which, i - 4], recv_corner.at[which, i - 4]
            copies.append(
                pltpu.make_async_remote_copy(
                    src_ref=source,
                    dst_ref=target,
                    send_sem=halo_send.at[which, i],
                    recv_sem=halo_recv.at[which, i],
                    device_id=halo_peer(i),
                    device_id_type=MESH,
                )
            )
        return copies

    inside = {
        (0, 1): (space > 0).astype(F32),
        (0, -1): (space < n_space - 1).astype(F32),
        (1, 1): (tile > 0).astype(F32),
        (1, -1): (tile < n_tile - 1).astype(F32),
    }

    def place_halo(which):
        for i in range(8):
            ds, dt = DIRS[i]
            valid = 1.0
            if ds:
                valid = valid * inside[0, ds]
            if dt:
                valid = valid * inside[1, dt]
            row, col = {1: 0, -1: 9}.get(ds), {1: 0, -1: 9}.get(dt)
            if i < 4:
                value = recv_face[which, i].astype(F32).reshape(8, 8, C) * valid
            else:
                value = recv_corner[which, i - 4].astype(F32)[0:8] * valid
            if ds == 0:
                padded[1:9, col] = value
            elif dt == 0:
                padded[row, 1:9] = value
            else:
                padded[row, col] = value

    z_place = lax.broadcasted_iota(jnp.int32, (10, 8, C), 1)

    def widen(target):
        def slab(i, carry):
            value = padded[i]
            before = jnp.where(z_place == 0, 0.0, pltpu.roll(value, 1, 1))
            after = jnp.where(z_place == 7, 0.0, pltpu.roll(value, 7, 1))
            start = pl.multiple_of(i * 64, 64)
            for sy in range(3):
                for sz, shifted in enumerate((before, value, after)):
                    column = (3 * sy + sz) * C
                    target[pl.ds(start, 64), column : column + C] = (
                        shifted[sy : sy + 8].reshape(64, C).astype(BF16)
                    )
            return carry

        lax.fori_loop(0, 10, slab, 0)

    loads[1].wait()
    masked_grad = masked_of(cot_v)
    padded[1:9, 1:9] = masked_grad
    fill_halo(0, masked_grad)
    pl.semaphore_wait(barrier, 8 + 1 + (nx - 1) + (ny - 1) + (nz - 1))
    halo_g = halo_copies(0)
    for copy in halo_g:
        copy.start()
    loads[2].wait()
    masked = masked_of(feat_v)
    fill_halo(1, masked)
    halo_f = halo_copies(1)
    for copy in halo_f:
        copy.start()
    features_t[...] = jnp.transpose(masked.reshape(512, C)).astype(BF16)

    for copy in halo_g:
        copy.wait_recv()
    place_halo(0)
    widen(wide_g)

    def terms(sx, first, last):
        for q in range(first, last, 2):
            end = min(q + 2, last)
            result = dot(features_t[...], wide_g[sx * 64 : sx * 64 + 512, q * C : end * C])
            for j in range(q, end):
                part[26 - (9 * sx + j)] = result[:, (j - q) * C : (j - q + 1) * C]

    mine = core * 14
    theirs = (1 - core) * 14

    def pair_copy(half):
        return pltpu.make_async_remote_copy(
            src_ref=part.at[pl.ds(theirs + 7 * half, 7)],
            dst_ref=pair_buf.at[pl.ds(7 * half, 7)],
            send_sem=pair_send.at[half],
            recv_sem=pair_recv.at[half],
            device_id=sibling,
            device_id_type=MESH,
        )

    part[27] = jnp.zeros((C, C), F32)
    if slots > 14:
        tiles[14:slots] = jnp.zeros((slots - 14, rows, C), F32)
    terms(1, 4, 9)
    terms(2, 0, 2)
    terms(0, 0, 6)
    pair = {1: pair_copy(1)}
    pair[1].start()
    terms(2, 2, 9)
    terms(0, 6, 9)
    terms(1, 0, 4)
    pair[0] = pair_copy(0)
    pair[0].start()

    first_size = {0: nx, 1: ny}
    second_size = {0: ny, 1: nx}
    first_block = {0: block, 1: block_y}
    first_place = {0: x * block, 1: y * block_y}
    second_place = {0: x * block + y * rows, 1: y * block_y + x * rows}

    def first_index(half, d):
        return x_peer(d + nx) if half == 0 else y_peer(d + ny)

    def first_device(half, d):
        if half == 0:
            return at(x_peer(d + nx), y, z, core)
        return at(x, y_peer(d + ny), z, core)

    def second_peer(half, d):
        return (x, y_peer(d)) if half == 0 else (x_peer(d), y)

    def first_copy(half, slot):
        sign = 1 if slot % 2 == 0 else -1
        upper = {0: 0, 1: 1, 2: 1, 3: 0, 4: 0, 5: 1}[slot]
        target = first_index(half, 2 if slot < 2 else sign)
        size = first_block[half] // 2
        start = pl.multiple_of(target * first_block[half] + upper * size, 8)
        return pltpu.make_async_remote_copy(
            src_ref=part.at[pl.ds(mine + 7 * half, 7), pl.ds(start, size)],
            dst_ref=first_buf.at[half, slot, :, 0:size],
            send_sem=first_send.at[half, slot],
            recv_sem=first_recv.at[half, slot],
            device_id=first_device(half, sign),
            device_id_type=MESH,
        )

    def first_start(half):
        ring = first_size[half] > 2
        firsts[half] = {slot: first_copy(half, slot) for slot in ((0, 1, 2, 3) if ring else (2, 3))}
        for copy in firsts[half].values():
            copy.start()

    def first_relay(half):
        if first_size[half] == 2:
            return
        size = first_block[half] // 2
        for slot in (0, 1):
            firsts[half][slot].wait_recv()
            target = first_index(half, 1 if slot == 0 else -1)
            where = pl.ds(pl.multiple_of(target * first_block[half] + slot * size, 8), size)
            part[pl.ds(mine + 7 * half, 7), where] = (
                part[pl.ds(mine + 7 * half, 7), where] + first_buf[half, slot, :, 0:size]
            )
            firsts[half][slot + 4] = first_copy(half, slot + 4)
            firsts[half][slot + 4].start()

    def second_copies(half):
        copies = []
        base = first_place[half]
        for d in range(1, second_size[half]):
            px, py = second_peer(half, d)
            index = py if half == 0 else px
            start = pl.multiple_of(base + index * rows, 8)
            copies.append(
                pltpu.make_async_remote_copy(
                    src_ref=part.at[pl.ds(mine + 7 * half, 7), pl.ds(start, rows)],
                    dst_ref=second_buf.at[half, d - 1],
                    send_sem=second_send.at[half, d - 1],
                    recv_sem=second_recv.at[half, d - 1],
                    device_id=at(px, py, z, core),
                    device_id_type=MESH,
                )
            )
        return copies

    def add_pair(half):
        pair[half].wait_recv()

        def one(i, carry):
            part[mine + 7 * half + i] = part[mine + 7 * half + i] + pair_buf[7 * half + i]
            return carry

        lax.fori_loop(0, 7, one, 0)

    def add_first(half):
        size = first_block[half] // 2
        for upper, slots_of in ((0, (3, 4)), (1, (2, 5))):
            where = pl.ds(pl.multiple_of(first_place[half] + upper * size, 8), size)
            value = part[pl.ds(mine + 7 * half, 7), where]
            for slot in slots_of:
                if slot in firsts[half]:
                    firsts[half][slot].wait_recv()
                    value = value + first_buf[half, slot, :, 0:size]
            part[pl.ds(mine + 7 * half, 7), where] = value

    def add_second(half, copies):
        for copy in copies:
            copy.wait_recv()
        where = pl.ds(pl.multiple_of(second_place[half], 8), rows)
        value = part[pl.ds(mine + 7 * half, 7), where]
        for d in range(1, second_size[half]):
            value = value + second_buf[half, d - 1]
        tiles[7 * half : 7 * half + 7] = value

    firsts, seconds = {}, {}
    for half in (1, 0):
        add_pair(half)
        first_start(half)

    padded[1:9, 1:9] = masked_of(feat_v)
    for copy in halo_f:
        copy.wait_recv()
    place_halo(1)
    widen(wide_f)
    for half in (1, 0):
        first_relay(half)

    def convolved(wide, weight, target):
        value = dot(wide[0:512, :], weight(0))
        value = value + dot(wide[64:576, :], weight(1))
        value = value + dot(wide[128:640, :], weight(2))
        value = value.reshape(8, 8, 8, C) * mask_v[...]
        target[...] = value.astype(BF16)

    loads[3].wait()
    convolved(wide_f, lambda a: kern_v[9 * a : 9 * a + 9].reshape(9 * C, C), out_v)
    out_copy = pltpu.make_async_copy(out_v, out_ref, out_sem.at[0])
    out_copy.start()

    for half in (1, 0):
        add_first(half)
        seconds[half] = second_copies(half)
        for copy in seconds[half]:
            copy.start()
    for half in (1, 0):
        add_second(half, seconds[half])

    def z_part(ref, index):
        return ref.at[pl.ds(index * per_owner, per_owner)]

    def z_copy(d):
        return pltpu.make_async_remote_copy(
            src_ref=z_part(tiles, z_peer(d)),
            dst_ref=z_part(z_buf, d - 1),
            send_sem=z_send,
            recv_sem=z_recv,
            device_id=at(x, y, z_peer(d), core),
            device_id_type=MESH,
        )

    def zg_copy(d):
        return pltpu.make_async_remote_copy(
            src_ref=z_part(z_all, z),
            dst_ref=z_part(z_all, z),
            send_sem=zg_send,
            recv_sem=zg_recv,
            device_id=at(x, y, z_peer(d), core),
            device_id_type=MESH,
        )

    z_whole = pltpu.make_async_remote_copy(
        src_ref=tiles.at[0 : slots - per_owner],
        dst_ref=z_buf,
        send_sem=z_send,
        recv_sem=z_recv,
        device_id=sibling,
        device_id_type=MESH,
    )
    zg_whole = pltpu.make_async_remote_copy(
        src_ref=z_all.at[0 : slots - per_owner],
        dst_ref=z_all.at[0 : slots - per_owner],
        send_sem=zg_send,
        recv_sem=zg_recv,
        device_id=sibling,
        device_id_type=MESH,
    )

    def z_start(d, carry):
        z_copy(d).start()
        return carry

    lax.fori_loop(1, nz, z_start, 0)

    def flip(s, carry):
        start = pl.multiple_of(s * C, C)
        kern_t[pl.ds(start, C), :] = jnp.transpose(kern_v[26 - s].astype(F32)).astype(BF16)
        return carry

    lax.fori_loop(0, 27, flip, 0)

    z_whole.wait_recv()
    value = tiles[pl.ds(z * per_owner, per_owner)]
    for d in range(1, nz):
        value = value + z_buf[(d - 1) * per_owner : d * per_owner]
    z_all[pl.ds(z * per_owner, per_owner)] = value * scale

    def zg_start(d, carry):
        zg_copy(d).start()
        return carry

    lax.fori_loop(1, nz, zg_start, 0)

    for copy in halo_g + halo_f + [pair[0], pair[1]]:
        copy.wait_send()
    for half in (1, 0):
        for copy in list(firsts[half].values()) + seconds[half]:
            copy.wait_send()
    z_whole.wait_send()

    def gathered(half, offsets, row, size):
        return total.at[pl.ds(offsets + 7 * half, 7), pl.ds(pl.multiple_of(row, 8), size)]

    def second_back(half, d, row):
        return pltpu.make_async_remote_copy(
            src_ref=z_all.at[7 * half : 7 * half + 7],
            dst_ref=gathered(half, mine, row, rows),
            send_sem=sg_send.at[half, d - 1],
            recv_sem=sg_recv.at[half, d - 1],
            device_id=at(*second_peer(half, d), z, core),
            device_id_type=MESH,
        )

    def first_back(half, slot, target):
        sign = 1 if slot % 2 == 0 else -1
        upper = {0: 0, 1: 1, 2: 1, 3: 0, 4: 0, 5: 1}[slot]
        size = first_block[half] // 2
        row = target * first_block[half] + upper * size
        return pltpu.make_async_remote_copy(
            src_ref=gathered(half, mine, row, size),
            dst_ref=gathered(half, mine, row, size),
            send_sem=fg_send.at[half, slot],
            recv_sem=fg_recv.at[half, slot],
            device_id=first_device(half, sign),
            device_id_type=MESH,
        )

    def source_of(half, slot):
        sign = 1 if slot % 2 == 0 else -1
        return first_index(half, -sign if slot < 4 else 2)

    def pair_back(half, slot, offsets):
        size = first_block[half]
        if slot == 6:
            row = first_index(half, 0) * size
        else:
            size = size // 2
            upper = {0: 0, 1: 1, 2: 1, 3: 0, 4: 0, 5: 1}[slot]
            row = source_of(half, slot) * 2 * size + upper * size
        return pltpu.make_async_remote_copy(
            src_ref=gathered(half, offsets, row, size),
            dst_ref=gathered(half, offsets, row, size),
            send_sem=pg_send.at[half, slot],
            recv_sem=pg_recv.at[half, slot],
            device_id=sibling,
            device_id_type=MESH,
        )

    convolved(wide_g, lambda a: kern_t[a * 9 * C : (a + 1) * 9 * C, :], fgrad_v)
    fgrad_copy = pltpu.make_async_copy(fgrad_v, fgrad_ref, out_sem.at[1])
    fgrad_copy.start()

    zg_whole.wait_recv()
    sent = []
    keeps = {}
    for half in (1, 0):
        for d in range(1, second_size[half]):
            copy = second_back(half, d, second_place[half])
            copy.start()
            sent.append(copy)
        keeps[half] = pltpu.make_async_copy(
            z_all.at[7 * half : 7 * half + 7],
            gathered(half, mine, second_place[half], rows),
            own_sem.at[half],
        )
        keeps[half].start()
    for half in (1, 0):
        n = second_size[half]
        for d in range(1, n):
            from_index = ((y if half == 0 else x) - d + n) % n
            second_back(half, d, first_place[half] + from_index * rows).wait_recv()
        keeps[half].wait()
        for slot in (0, 1, 2, 3) if first_size[half] > 2 else (0, 1):
            copy = first_back(half, slot, first_index(half, 0))
            copy.start()
            sent.append(copy)
        copy = pair_back(half, 6, mine)
        copy.start()
        sent.append(copy)

    forwarded = []
    for slot in range(6):
        for half in (1, 0):
            if first_size[half] > 2 or slot < 2:
                first_back(half, slot, source_of(half, slot)).wait_recv()
                if first_size[half] > 2 and slot < 2:
                    copy = first_back(half, slot + 4, source_of(half, slot))
                    copy.start()
                    sent.append(copy)
                copy = pair_back(half, slot, mine)
                copy.start()
                forwarded.append(copy)
    zg_whole.wait_send()
    for copy in sent:
        copy.wait_send()
    out_copy.wait()
    fgrad_copy.wait()
    for slot in (6, 0, 1, 2, 3, 4, 5):
        for half in (1, 0):
            if first_size[half] > 2 or slot in (6, 0, 1):
                pair_back(half, slot, theirs).wait_recv()
    for copy in forwarded:
        copy.wait_send()


def finish(out_ref, fgrad_ref, kgrad_ref, out_final, fgrad_final, kgrad_final, sem):
    copies = [
        pltpu.make_async_copy(kgrad_ref.at[0:27], kgrad_final, sem.at[0]),
        pltpu.make_async_copy(out_ref, out_final, sem.at[1]),
        pltpu.make_async_copy(fgrad_ref, fgrad_final, sem.at[2]),
    ]
    for copy in copies:
        copy.start()
    for copy in copies:
        copy.wait()


def shards(chips, features, occupancy, weights, cotangent):
    nx, ny, nz = chips
    voxels = 512 * nx * ny * nz * 2
    scale = 1.0 / math.sqrt(voxels)
    rows = C // (nx * ny)
    per_owner = -(-14 // nz)
    most = max(nx, ny)
    dma = pltpu.SemaphoreType.DMA
    results = pl.pallas_call(
        functools.partial(kernel, chips, scale),
        out_shape=(
            jax.ShapeDtypeStruct((8, 8, 8, C), BF16),
            jax.ShapeDtypeStruct((8, 8, 8, C), BF16),
            jax.ShapeDtypeStruct((28, C, C), F32),
        ),
        in_specs=[pl.BlockSpec(memory_space=pltpu.HBM)] * 4,
        out_specs=[pl.BlockSpec(memory_space=pl.ANY)] * 3,
        scratch_shapes=[
            pltpu.VMEM((8, 8, 8, C), BF16),
            pltpu.VMEM((8, 8, 8, C), BF16),
            pltpu.VMEM((8, 8, 8), jnp.int32),
            pltpu.VMEM((27, C, C), BF16),
            pltpu.VMEM((27 * C, C), BF16),
            pltpu.VMEM((8, 8, 8, C), F32),
            pltpu.VMEM((C, 512), BF16),
            pltpu.VMEM((10, 10, 8, C), F32),
            pltpu.VMEM((640, 9 * C), BF16),
            pltpu.VMEM((640, 9 * C), BF16),
            pltpu.VMEM((2, 4, 64, C), BF16),
            pltpu.VMEM((2, 4, 16, C), BF16),
            pltpu.VMEM((2, 4, 64, C), BF16),
            pltpu.VMEM((2, 4, 16, C), BF16),
            pltpu.VMEM((28, C, C), F32),
            pltpu.VMEM((14, C, C), F32),
            pltpu.VMEM((2, 6, 7, C // (2 * min(nx, ny)), C), F32),
            pltpu.VMEM((2, most - 1, 7, rows, C), F32),
            pltpu.VMEM((nz * per_owner, rows, C), F32),
            pltpu.VMEM(((nz - 1) * per_owner, rows, C), F32),
            pltpu.VMEM((nz * per_owner, rows, C), F32),
            pltpu.VMEM((8, 8, 8, C), BF16),
            pltpu.VMEM((8, 8, 8, C), BF16),
            dma((4,)),
            dma((2,)),
            dma((2,)),
            dma((2, 8)),
            dma((2, 8)),
            dma((2,)),
            dma((2,)),
            dma((2, 6)),
            dma((2, 6)),
            dma((2, most - 1)),
            dma((2, most - 1)),
            dma,
            dma,
            dma,
            dma,
            dma((2, most - 1)),
            dma((2, most - 1)),
            dma((2, 6)),
            dma((2, 6)),
            dma((2, 7)),
            dma((2, 7)),
        ],
        compiler_params=pltpu.CompilerParams(
            collective_id=0, has_side_effects=True, vmem_limit_bytes=48 * 1024 * 1024
        ),
        cost_estimate=pl.CostEstimate(
            flops=3 * 2 * 512 * 27 * C * C, bytes_accessed=4_000_000, transcendentals=0
        ),
    )(*(pltpu.with_memory_space_constraint(a, pltpu.HBM) for a in (features, occupancy, weights, cotangent)))
    return pl.pallas_call(
        finish,
        out_shape=(
            jax.ShapeDtypeStruct((8, 8, 8, C), BF16),
            jax.ShapeDtypeStruct((8, 8, 8, C), BF16),
            jax.ShapeDtypeStruct((27, C, C), F32),
        ),
        in_specs=[pl.BlockSpec(memory_space=pltpu.VMEM)] * 3,
        out_specs=[pl.BlockSpec(memory_space=pl.ANY)] * 3,
        scratch_shapes=[dma((3,))],
    )(*results)


def solution(mesh, chips=CHIPS):
    in_specs = (
        P("space", "tile", None, None),
        P("space", "tile", None),
        P(),
        P("space", "tile", None, None),
    )
    out_specs = (P("space", "tile", None, None), P("space", "tile", None, None), P())
    return jax.shard_map(
        functools.partial(shards, chips),
        mesh=mesh,
        in_specs=in_specs,
        out_specs=out_specs,
        check_vma=False,
    )
```

```python
import functools
import math

import jax
import jax.numpy as jnp
from jax import lax
from jax.experimental import pallas as pl
from jax.experimental.pallas import tpu as pltpu
from jax.sharding import PartitionSpec as P

MESH = pl.DeviceIdType.MESH
CHIPS = (4, 4, 16)
C = 128
DIRS = ((1, 0), (-1, 0), (0, 1), (0, -1), (1, 1), (1, -1), (-1, 1), (-1, -1))
F32 = jnp.float32
BF16 = jnp.bfloat16


def dot(a, b):
    return jnp.dot(a, b, preferred_element_type=F32)


def kernel(
    chips,
    scale,
    feat_hbm,
    occ_hbm,
    kern_hbm,
    cot_hbm,
    out_ref,
    fgrad_ref,
    total,
    feat_v,
    cot_v,
    occ_v,
    kern_v,
    kern_t,
    mask_v,
    features_t,
    padded,
    wide_f,
    wide_g,
    send_face,
    send_corner,
    recv_face,
    recv_corner,
    part,
    pair_buf,
    first_buf,
    second_buf,
    tiles,
    z_buf,
    z_all,
    out_v,
    fgrad_v,
    in_sem,
    out_sem,
    own_sem,
    known,
    halo_send,
    halo_recv,
    pair_send,
    pair_recv,
    first_send,
    first_recv,
    second_send,
    second_recv,
    z_send,
    z_recv,
    zg_send,
    zg_recv,
    sg_send,
    sg_recv,
    fg_send,
    fg_recv,
    pg_send,
    pg_recv,
):
    nx, ny, nz = chips
    n_space, n_tile = nx * nz, ny * 2
    space, tile = lax.axis_index("space"), lax.axis_index("tile")
    x, z = space // nz, space % nz
    y, core = tile // 2, tile % 2
    block = C // nx
    block_y = C // ny
    rows = C // (nx * ny)
    per_owner = -(-14 // nz)
    slots = nz * per_owner

    def at(px, py, pz, pc):
        return {"space": px * nz + pz, "tile": py * 2 + pc}

    def x_peer(d):
        return (x + d) % nx

    def y_peer(d):
        return (y + d) % ny

    def z_peer(d):
        return (z + d) % nz

    def halo_peer(i):
        ds, dt = DIRS[i]
        return {
            "space": (space + ds + n_space) % n_space,
            "tile": (tile + dt + n_tile) % n_tile,
        }

    sibling = at(x, y, z, 1 - core)

    loads = [
        pltpu.make_async_copy(src, dst, in_sem.at[i])
        for i, (src, dst) in enumerate(
            ((occ_hbm, occ_v), (cot_hbm, cot_v), (feat_hbm, feat_v), (kern_hbm, kern_v))
        )
    ]
    for load in loads:
        load.start()

    barrier = pltpu.get_barrier_semaphore()

    def greet(device):
        pl.semaphore_signal(barrier, inc=1, device_id=device, device_id_type=MESH)

    for i in range(8):
        greet(halo_peer(i))
    greet(sibling)
    for d in range(1, nx):
        greet(at(x_peer(d), y, z, core))
    for d in range(1, ny):
        greet(at(x, y_peer(d), z, core))

    for d in (1, -1):
        greet(at(x, y, z_peer(d + nz), core))

    def tell(step):
        d = 2**step
        if d < nz // 2:
            for side in (d, -d):
                pl.semaphore_signal(
                    known.at[step],
                    inc=1,
                    device_id=at(x, y, z_peer(side + nz), core),
                    device_id_type=MESH,
                )

    def hear(step):
        if 2**step < nz // 2:
            pl.semaphore_wait(known.at[step], 2)

    loads[0].wait()
    cells = occ_v[...].reshape(64, 8).astype(F32).astype(BF16)
    pick = lax.broadcasted_iota(jnp.int32, (512, 64), 0) // 8
    pick = (pick == lax.broadcasted_iota(jnp.int32, (512, 64), 1)).astype(F32)
    spread = dot(pick.astype(BF16), cells)
    own = lax.broadcasted_iota(jnp.int32, (512, 8), 0) % 8
    own = own == lax.broadcasted_iota(jnp.int32, (512, 8), 1)
    column = jnp.sum(jnp.where(own, spread, 0.0), axis=1, keepdims=True)
    mask_v[...] = jnp.broadcast_to(column, (512, C)).reshape(8, 8, 8, C)

    def masked_of(source):
        return source[...].astype(F32) * mask_v[...]

    def fill_halo(which, value):
        edge_x = {1: value[7], -1: value[0]}
        edge_y = {1: value[:, 7], -1: value[:, 0]}
        for i in range(2):
            send_face[which, i] = edge_x[DIRS[i][0]].reshape(64, C).astype(BF16)
        for i in range(2, 4):
            send_face[which, i] = edge_y[DIRS[i][1]].reshape(64, C).astype(BF16)
        for i in range(4, 8):
            corner = edge_x[DIRS[i][0]][7 if DIRS[i][1] == 1 else 0]
            send_corner[which, i - 4] = jnp.concatenate([corner, corner], axis=0).astype(BF16)

    def halo_copies(which):
        copies = []
        for i in range(8):
            if i < 4:
                source, target = send_face.at[which, i], recv_face.at[which, i]
            else:
                source, target = send_corner.at[which, i - 4], recv_corner.at[which, i - 4]
            copies.append(
                pltpu.make_async_remote_copy(
                    src_ref=source,
                    dst_ref=target,
                    send_sem=halo_send.at[which, i],
                    recv_sem=halo_recv.at[which, i],
                    device_id=halo_peer(i),
                    device_id_type=MESH,
                )
            )
        return copies

    inside = {
        (0, 1): (space > 0).astype(F32),
        (0, -1): (space < n_space - 1).astype(F32),
        (1, 1): (tile > 0).astype(F32),
        (1, -1): (tile < n_tile - 1).astype(F32),
    }

    def place_halo(which):
        for i in range(8):
            ds, dt = DIRS[i]
            valid = 1.0
            if ds:
                valid = valid * inside[0, ds]
            if dt:
                valid = valid * inside[1, dt]
            row, col = {1: 0, -1: 9}.get(ds), {1: 0, -1: 9}.get(dt)
            if i < 4:
                value = recv_face[which, i].astype(F32).reshape(8, 8, C) * valid
            else:
                value = recv_corner[which, i - 4].astype(F32)[0:8] * valid
            if ds == 0:
                padded[1:9, col] = value
            elif dt == 0:
                padded[row, 1:9] = value
            else:
                padded[row, col] = value

    z_place = lax.broadcasted_iota(jnp.int32, (10, 8, C), 1)

    def widen(target):
        def slab(i, carry):
            value = padded[i]
            before = jnp.where(z_place == 0, 0.0, pltpu.roll(value, 1, 1))
            after = jnp.where(z_place == 7, 0.0, pltpu.roll(value, 7, 1))
            start = pl.multiple_of(i * 64, 64)
            for sy in range(3):
                for sz, shifted in enumerate((before, value, after)):
                    column = (3 * sy + sz) * C
                    target[pl.ds(start, 64), column : column + C] = (
                        shifted[sy : sy + 8].reshape(64, C).astype(BF16)
                    )
            return carry

        lax.fori_loop(0, 10, slab, 0)

    loads[1].wait()
    masked_grad = masked_of(cot_v)
    padded[1:9, 1:9] = masked_grad
    fill_halo(0, masked_grad)
    pl.semaphore_wait(barrier, 8 + 1 + (nx - 1) + (ny - 1) + 2)
    halo_g = halo_copies(0)
    for copy in halo_g:
        copy.start()
    tell(0)
    loads[2].wait()
    masked = masked_of(feat_v)
    fill_halo(1, masked)
    halo_f = halo_copies(1)
    for copy in halo_f:
        copy.start()
    hear(0)
    tell(1)
    features_t[...] = jnp.transpose(masked.reshape(512, C)).astype(BF16)

    for copy in halo_g:
        copy.wait_recv()
    place_halo(0)
    widen(wide_g)

    def terms(sx, first, last):
        for q in range(first, last, 2):
            end = min(q + 2, last)
            result = dot(features_t[...], wide_g[sx * 64 : sx * 64 + 512, q * C : end * C])
            for j in range(q, end):
                part[26 - (9 * sx + j)] = result[:, (j - q) * C : (j - q + 1) * C]

    mine = core * 14
    theirs = (1 - core) * 14

    def pair_copy(half):
        return pltpu.make_async_remote_copy(
            src_ref=part.at[pl.ds(theirs + 7 * half, 7)],
            dst_ref=pair_buf.at[pl.ds(7 * half, 7)],
            send_sem=pair_send.at[half],
            recv_sem=pair_recv.at[half],
            device_id=sibling,
            device_id_type=MESH,
        )

    hear(1)
    tell(2)

    part[27] = jnp.zeros((C, C), F32)
    if slots > 14:
        tiles[14:slots] = jnp.zeros((slots - 14, rows, C), F32)
    terms(1, 4, 9)
    terms(2, 0, 2)
    terms(0, 0, 6)
    pair = {1: pair_copy(1)}
    pair[1].start()
    terms(2, 2, 9)
    terms(0, 6, 9)
    terms(1, 0, 4)
    pair[0] = pair_copy(0)
    pair[0].start()

    first_size = {0: nx, 1: ny}
    second_size = {0: ny, 1: nx}
    first_block = {0: block, 1: block_y}
    first_place = {0: x * block, 1: y * block_y}
    second_place = {0: x * block + y * rows, 1: y * block_y + x * rows}

    def first_index(half, d):
        return x_peer(d + nx) if half == 0 else y_peer(d + ny)

    def first_device(half, d):
        if half == 0:
            return at(x_peer(d + nx), y, z, core)
        return at(x, y_peer(d + ny), z, core)

    def second_peer(half, d):
        return (x, y_peer(d)) if half == 0 else (x_peer(d), y)

    def first_copy(half, slot):
        sign = 1 if slot % 2 == 0 else -1
        upper = {0: 0, 1: 1, 2: 1, 3: 0, 4: 0, 5: 1}[slot]
        target = first_index(half, 2 if slot < 2 else sign)
        size = first_block[half] // 2
        start = pl.multiple_of(target * first_block[half] + upper * size, 8)
        return pltpu.make_async_remote_copy(
            src_ref=part.at[pl.ds(mine + 7 * half, 7), pl.ds(start, size)],
            dst_ref=first_buf.at[half, slot, :, 0:size],
            send_sem=first_send.at[half, slot],
            recv_sem=first_recv.at[half, slot],
            device_id=first_device(half, sign),
            device_id_type=MESH,
        )

    def first_start(half):
        ring = first_size[half] > 2
        firsts[half] = {slot: first_copy(half, slot) for slot in ((0, 1, 2, 3) if ring else (2, 3))}
        for copy in firsts[half].values():
            copy.start()

    def first_relay(half):
        if first_size[half] == 2:
            return
        size = first_block[half] // 2
        for slot in (0, 1):
            firsts[half][slot].wait_recv()
            target = first_index(half, 1 if slot == 0 else -1)
            where = pl.ds(pl.multiple_of(target * first_block[half] + slot * size, 8), size)
            part[pl.ds(mine + 7 * half, 7), where] = (
                part[pl.ds(mine + 7 * half, 7), where] + first_buf[half, slot, :, 0:size]
            )
            firsts[half][slot + 4] = first_copy(half, slot + 4)
            firsts[half][slot + 4].start()

    def second_copies(half):
        copies = []
        base = first_place[half]
        for d in range(1, second_size[half]):
            px, py = second_peer(half, d)
            index = py if half == 0 else px
            start = pl.multiple_of(base + index * rows, 8)
            copies.append(
                pltpu.make_async_remote_copy(
                    src_ref=part.at[pl.ds(mine + 7 * half, 7), pl.ds(start, rows)],
                    dst_ref=second_buf.at[half, d - 1],
                    send_sem=second_send.at[half, d - 1],
                    recv_sem=second_recv.at[half, d - 1],
                    device_id=at(px, py, z, core),
                    device_id_type=MESH,
                )
            )
        return copies

    def add_pair(half):
        pair[half].wait_recv()

        def one(i, carry):
            part[mine + 7 * half + i] = part[mine + 7 * half + i] + pair_buf[7 * half + i]
            return carry

        lax.fori_loop(0, 7, one, 0)

    def add_first(half):
        size = first_block[half] // 2
        for upper, slots_of in ((0, (3, 4)), (1, (2, 5))):
            where = pl.ds(pl.multiple_of(first_place[half] + upper * size, 8), size)
            value = part[pl.ds(mine + 7 * half, 7), where]
            for slot in slots_of:
                if slot in firsts[half]:
                    firsts[half][slot].wait_recv()
                    value = value + first_buf[half, slot, :, 0:size]
            part[pl.ds(mine + 7 * half, 7), where] = value

    def add_second(half, copies):
        for copy in copies:
            copy.wait_recv()
        where = pl.ds(pl.multiple_of(second_place[half], 8), rows)
        value = part[pl.ds(mine + 7 * half, 7), where]
        for d in range(1, second_size[half]):
            value = value + second_buf[half, d - 1]
        tiles[7 * half : 7 * half + 7] = value

    firsts, seconds = {}, {}
    for half in (1, 0):
        add_pair(half)
        first_start(half)

    padded[1:9, 1:9] = masked_of(feat_v)
    for copy in halo_f:
        copy.wait_recv()
    place_halo(1)
    widen(wide_f)
    for half in (1, 0):
        first_relay(half)

    def convolved(wide, weight, target):
        value = dot(wide[0:512, :], weight(0))
        value = value + dot(wide[64:576, :], weight(1))
        value = value + dot(wide[128:640, :], weight(2))
        value = value.reshape(8, 8, 8, C) * mask_v[...]
        target[...] = value.astype(BF16)

    loads[3].wait()
    convolved(wide_f, lambda a: kern_v[9 * a : 9 * a + 9].reshape(9 * C, C), out_v)
    out_copy = pltpu.make_async_copy(out_v, out_ref, out_sem.at[0])
    out_copy.start()

    for half in (1, 0):
        add_first(half)
        seconds[half] = second_copies(half)
        for copy in seconds[half]:
            copy.start()
    for half in (1, 0):
        add_second(half, seconds[half])

    def z_part(ref, index):
        return ref.at[pl.ds(index * per_owner, per_owner)]

    def z_copy(d):
        return pltpu.make_async_remote_copy(
            src_ref=z_part(tiles, z_peer(d)),
            dst_ref=z_part(z_buf, d - 1),
            send_sem=z_send,
            recv_sem=z_recv,
            device_id=at(x, y, z_peer(d), core),
            device_id_type=MESH,
        )

    def zg_copy(d):
        return pltpu.make_async_remote_copy(
            src_ref=z_part(z_all, z),
            dst_ref=z_part(z_all, z),
            send_sem=zg_send,
            recv_sem=zg_recv,
            device_id=at(x, y, z_peer(d), core),
            device_id_type=MESH,
        )

    z_whole = pltpu.make_async_remote_copy(
        src_ref=tiles.at[0 : slots - per_owner],
        dst_ref=z_buf,
        send_sem=z_send,
        recv_sem=z_recv,
        device_id=sibling,
        device_id_type=MESH,
    )
    zg_whole = pltpu.make_async_remote_copy(
        src_ref=z_all.at[0 : slots - per_owner],
        dst_ref=z_all.at[0 : slots - per_owner],
        send_sem=zg_send,
        recv_sem=zg_recv,
        device_id=sibling,
        device_id_type=MESH,
    )

    def z_start(d, carry):
        z_copy(d).start()
        return carry

    hear(2)
    lax.fori_loop(1, nz, z_start, 0)

    def flip(s, carry):
        start = pl.multiple_of(s * C, C)
        kern_t[pl.ds(start, C), :] = jnp.transpose(kern_v[26 - s].astype(F32)).astype(BF16)
        return carry

    lax.fori_loop(0, 27, flip, 0)

    z_whole.wait_recv()
    value = tiles[pl.ds(z * per_owner, per_owner)]
    for d in range(1, nz):
        value = value + z_buf[(d - 1) * per_owner : d * per_owner]
    z_all[pl.ds(z * per_owner, per_owner)] = value * scale

    def zg_start(d, carry):
        zg_copy(d).start()
        return carry

    lax.fori_loop(1, nz, zg_start, 0)

    for copy in halo_g + halo_f + [pair[0], pair[1]]:
        copy.wait_send()
    for half in (1, 0):
        for copy in list(firsts[half].values()) + seconds[half]:
            copy.wait_send()
    z_whole.wait_send()

    def gathered(half, offsets, row, size):
        return total.at[pl.ds(offsets + 7 * half, 7), pl.ds(pl.multiple_of(row, 8), size)]

    def second_back(half, d, row):
        return pltpu.make_async_remote_copy(
            src_ref=z_all.at[7 * half : 7 * half + 7],
            dst_ref=gathered(half, mine, row, rows),
            send_sem=sg_send.at[half, d - 1],
            recv_sem=sg_recv.at[half, d - 1],
            device_id=at(*second_peer(half, d), z, core),
            device_id_type=MESH,
        )

    def first_back(half, slot, target):
        sign = 1 if slot % 2 == 0 else -1
        upper = {0: 0, 1: 1, 2: 1, 3: 0, 4: 0, 5: 1}[slot]
        size = first_block[half] // 2
        row = target * first_block[half] + upper * size
        return pltpu.make_async_remote_copy(
            src_ref=gathered(half, mine, row, size),
            dst_ref=gathered(half, mine, row, size),
            send_sem=fg_send.at[half, slot],
            recv_sem=fg_recv.at[half, slot],
            device_id=first_device(half, sign),
            device_id_type=MESH,
        )

    def source_of(half, slot):
        sign = 1 if slot % 2 == 0 else -1
        return first_index(half, -sign if slot < 4 else 2)

    def pair_back(half, slot, offsets):
        size = first_block[half]
        if slot == 6:
            row = first_index(half, 0) * size
        else:
            size = size // 2
            upper = {0: 0, 1: 1, 2: 1, 3: 0, 4: 0, 5: 1}[slot]
            row = source_of(half, slot) * 2 * size + upper * size
        return pltpu.make_async_remote_copy(
            src_ref=gathered(half, offsets, row, size),
            dst_ref=gathered(half, offsets, row, size),
            send_sem=pg_send.at[half, slot],
            recv_sem=pg_recv.at[half, slot],
            device_id=sibling,
            device_id_type=MESH,
        )

    convolved(wide_g, lambda a: kern_t[a * 9 * C : (a + 1) * 9 * C, :], fgrad_v)
    fgrad_copy = pltpu.make_async_copy(fgrad_v, fgrad_ref, out_sem.at[1])
    fgrad_copy.start()

    zg_whole.wait_recv()
    sent = []
    keeps = {}
    for half in (1, 0):
        for d in range(1, second_size[half]):
            copy = second_back(half, d, second_place[half])
            copy.start()
            sent.append(copy)
        keeps[half] = pltpu.make_async_copy(
            z_all.at[7 * half : 7 * half + 7],
            gathered(half, mine, second_place[half], rows),
            own_sem.at[half],
        )
        keeps[half].start()
    for half in (1, 0):
        n = second_size[half]
        for d in range(1, n):
            from_index = ((y if half == 0 else x) - d + n) % n
            second_back(half, d, first_place[half] + from_index * rows).wait_recv()
        keeps[half].wait()
        for slot in (0, 1, 2, 3) if first_size[half] > 2 else (0, 1):
            copy = first_back(half, slot, first_index(half, 0))
            copy.start()
            sent.append(copy)
        copy = pair_back(half, 6, mine)
        copy.start()
        sent.append(copy)

    forwarded = []
    for slot in range(6):
        for half in (1, 0):
            if first_size[half] > 2 or slot < 2:
                first_back(half, slot, source_of(half, slot)).wait_recv()
                if first_size[half] > 2 and slot < 2:
                    copy = first_back(half, slot + 4, source_of(half, slot))
                    copy.start()
                    sent.append(copy)
                copy = pair_back(half, slot, mine)
                copy.start()
                forwarded.append(copy)
    zg_whole.wait_send()
    for copy in sent:
        copy.wait_send()
    out_copy.wait()
    fgrad_copy.wait()
    for slot in (6, 0, 1, 2, 3, 4, 5):
        for half in (1, 0):
            if first_size[half] > 2 or slot in (6, 0, 1):
                pair_back(half, slot, theirs).wait_recv()
    for copy in forwarded:
        copy.wait_send()


def shards(chips, features, occupancy, weights, cotangent):
    nx, ny, nz = chips
    voxels = 512 * nx * ny * nz * 2
    scale = 1.0 / math.sqrt(voxels)
    rows = C // (nx * ny)
    per_owner = -(-14 // nz)
    most = max(nx, ny)
    dma = pltpu.SemaphoreType.DMA
    results = pl.pallas_call(
        functools.partial(kernel, chips, scale),
        out_shape=(
            jax.ShapeDtypeStruct((8, 8, 8, C), BF16),
            jax.ShapeDtypeStruct((8, 8, 8, C), BF16),
            jax.ShapeDtypeStruct((28, C, C), F32),
        ),
        in_specs=[pl.BlockSpec(memory_space=pltpu.HBM)] * 4,
        out_specs=[pl.BlockSpec(memory_space=pl.ANY)] * 3,
        scratch_shapes=[
            pltpu.VMEM((8, 8, 8, C), BF16),
            pltpu.VMEM((8, 8, 8, C), BF16),
            pltpu.VMEM((8, 8, 8), jnp.int32),
            pltpu.VMEM((27, C, C), BF16),
            pltpu.VMEM((27 * C, C), BF16),
            pltpu.VMEM((8, 8, 8, C), F32),
            pltpu.VMEM((C, 512), BF16),
            pltpu.VMEM((10, 10, 8, C), F32),
            pltpu.VMEM((640, 9 * C), BF16),
            pltpu.VMEM((640, 9 * C), BF16),
            pltpu.VMEM((2, 4, 64, C), BF16),
            pltpu.VMEM((2, 4, 16, C), BF16),
            pltpu.VMEM((2, 4, 64, C), BF16),
            pltpu.VMEM((2, 4, 16, C), BF16),
            pltpu.VMEM((28, C, C), F32),
            pltpu.VMEM((14, C, C), F32),
            pltpu.VMEM((2, 6, 7, C // (2 * min(nx, ny)), C), F32),
            pltpu.VMEM((2, most - 1, 7, rows, C), F32),
            pltpu.VMEM((nz * per_owner, rows, C), F32),
            pltpu.VMEM(((nz - 1) * per_owner, rows, C), F32),
            pltpu.VMEM((nz * per_owner, rows, C), F32),
            pltpu.VMEM((8, 8, 8, C), BF16),
            pltpu.VMEM((8, 8, 8, C), BF16),
            dma((4,)),
            dma((2,)),
            dma((2,)),
            pltpu.SemaphoreType.REGULAR((3,)),
            dma((2, 8)),
            dma((2, 8)),
            dma((2,)),
            dma((2,)),
            dma((2, 6)),
            dma((2, 6)),
            dma((2, most - 1)),
            dma((2, most - 1)),
            dma,
            dma,
            dma,
            dma,
            dma((2, most - 1)),
            dma((2, most - 1)),
            dma((2, 6)),
            dma((2, 6)),
            dma((2, 7)),
            dma((2, 7)),
        ],
        compiler_params=pltpu.CompilerParams(
            collective_id=0, has_side_effects=True, vmem_limit_bytes=48 * 1024 * 1024
        ),
        cost_estimate=pl.CostEstimate(
            flops=3 * 2 * 512 * 27 * C * C, bytes_accessed=4_000_000, transcendentals=0
        ),
    )(*(pltpu.with_memory_space_constraint(a, pltpu.HBM) for a in (features, occupancy, weights, cotangent)))
    return results[0], results[1], results[2][:27]


def solution(mesh, chips=CHIPS):
    in_specs = (
        P("space", "tile", None, None),
        P("space", "tile", None),
        P(),
        P("space", "tile", None, None),
    )
    out_specs = (P("space", "tile", None, None), P("space", "tile", None, None), P())
    return jax.shard_map(
        functools.partial(shards, chips),
        mesh=mesh,
        in_specs=in_specs,
        out_specs=out_specs,
        check_vma=False,
    )
```

```python
import functools
import math

import jax
import jax.numpy as jnp
from jax import lax
from jax.experimental import pallas as pl
from jax.experimental.pallas import tpu as pltpu
from jax.sharding import PartitionSpec as P

MESH = pl.DeviceIdType.MESH
CHIPS = (4, 4, 16)
C = 128
DIRS = ((1, 0), (-1, 0), (0, 1), (0, -1), (1, 1), (1, -1), (-1, 1), (-1, -1))
F32 = jnp.float32
BF16 = jnp.bfloat16


def dot(a, b):
    return jnp.dot(a, b, preferred_element_type=F32)


def kernel(
    chips,
    scale,
    feat_hbm,
    occ_hbm,
    kern_hbm,
    cot_hbm,
    out_ref,
    fgrad_ref,
    total,
    feat_v,
    cot_v,
    occ_v,
    kern_v,
    kern_t,
    mask_v,
    features_t,
    padded,
    wide_f,
    wide_g,
    send_face,
    send_corner,
    recv_face,
    recv_corner,
    part,
    pair_buf,
    first_buf,
    second_buf,
    tiles,
    z_buf,
    z_all,
    out_v,
    fgrad_v,
    in_sem,
    out_sem,
    own_sem,
    known,
    halo_send,
    halo_recv,
    pair_send,
    pair_recv,
    first_send,
    first_recv,
    second_send,
    second_recv,
    z_send,
    z_recv,
    zg_send,
    zg_recv,
    sg_send,
    sg_recv,
    fg_send,
    fg_recv,
    pg_send,
    pg_recv,
):
    nx, ny, nz = chips
    n_space, n_tile = nx * nz, ny * 2
    space, tile = lax.axis_index("space"), lax.axis_index("tile")
    x, z = space // nz, space % nz
    y, core = tile // 2, tile % 2
    block = C // nx
    block_y = C // ny
    rows = C // (nx * ny)
    per_owner = -(-14 // nz)
    slots = nz * per_owner

    def at(px, py, pz, pc):
        return {"space": px * nz + pz, "tile": py * 2 + pc}

    def x_peer(d):
        return (x + d) % nx

    def y_peer(d):
        return (y + d) % ny

    def z_peer(d):
        return (z + d) % nz

    def halo_peer(i):
        ds, dt = DIRS[i]
        return {
            "space": (space + ds + n_space) % n_space,
            "tile": (tile + dt + n_tile) % n_tile,
        }

    sibling = at(x, y, z, 1 - core)

    loads = [
        pltpu.make_async_copy(src, dst, in_sem.at[i])
        for i, (src, dst) in enumerate(
            ((occ_hbm, occ_v), (cot_hbm, cot_v), (feat_hbm, feat_v), (kern_hbm, kern_v))
        )
    ]
    for load in loads:
        load.start()

    barrier = pltpu.get_barrier_semaphore()

    def greet(device):
        pl.semaphore_signal(barrier, inc=1, device_id=device, device_id_type=MESH)

    for i in range(8):
        greet(halo_peer(i))
    greet(sibling)
    for d in range(1, nx):
        greet(at(x_peer(d), y, z, core))
    for d in range(1, ny):
        greet(at(x, y_peer(d), z, core))

    for d in (1, -1):
        greet(at(x, y, z_peer(d + nz), core))

    def tell(step):
        d = 2**step
        if d < nz // 2:
            for side in (d, -d):
                pl.semaphore_signal(
                    known.at[step],
                    inc=1,
                    device_id=at(x, y, z_peer(side + nz), core),
                    device_id_type=MESH,
                )

    def hear(step):
        if 2**step < nz // 2:
            pl.semaphore_wait(known.at[step], 2)

    loads[0].wait()
    cells = occ_v[...].reshape(64, 8).astype(F32).astype(BF16)
    pick = lax.broadcasted_iota(jnp.int32, (512, 64), 0) // 8
    pick = (pick == lax.broadcasted_iota(jnp.int32, (512, 64), 1)).astype(F32)
    spread = dot(pick.astype(BF16), cells)
    own = lax.broadcasted_iota(jnp.int32, (512, 8), 0) % 8
    own = own == lax.broadcasted_iota(jnp.int32, (512, 8), 1)
    column = jnp.sum(jnp.where(own, spread, 0.0), axis=1, keepdims=True)
    mask_v[...] = jnp.broadcast_to(column, (512, C)).reshape(8, 8, 8, C)

    def masked_of(source):
        return source[...].astype(F32) * mask_v[...]

    def fill_halo(which, value):
        edge_x = {1: value[7], -1: value[0]}
        edge_y = {1: value[:, 7], -1: value[:, 0]}
        for i in range(2):
            send_face[which, i] = edge_x[DIRS[i][0]].reshape(64, C).astype(BF16)
        for i in range(2, 4):
            send_face[which, i] = edge_y[DIRS[i][1]].reshape(64, C).astype(BF16)
        for i in range(4, 8):
            corner = edge_x[DIRS[i][0]][7 if DIRS[i][1] == 1 else 0]
            send_corner[which, i - 4] = jnp.concatenate([corner, corner], axis=0).astype(BF16)

    def halo_copies(which):
        copies = []
        for i in range(8):
            if i < 4:
                source, target = send_face.at[which, i], recv_face.at[which, i]
            else:
                source, target = send_corner.at[which, i - 4], recv_corner.at[which, i - 4]
            copies.append(
                pltpu.make_async_remote_copy(
                    src_ref=source,
                    dst_ref=target,
                    send_sem=halo_send.at[which, i],
                    recv_sem=halo_recv.at[which, i],
                    device_id=halo_peer(i),
                    device_id_type=MESH,
                )
            )
        return copies

    inside = {
        (0, 1): (space > 0).astype(F32),
        (0, -1): (space < n_space - 1).astype(F32),
        (1, 1): (tile > 0).astype(F32),
        (1, -1): (tile < n_tile - 1).astype(F32),
    }

    def place_halo(which):
        for i in range(8):
            ds, dt = DIRS[i]
            valid = 1.0
            if ds:
                valid = valid * inside[0, ds]
            if dt:
                valid = valid * inside[1, dt]
            row, col = {1: 0, -1: 9}.get(ds), {1: 0, -1: 9}.get(dt)
            if i < 4:
                value = recv_face[which, i].astype(F32).reshape(8, 8, C) * valid
            else:
                value = recv_corner[which, i - 4].astype(F32)[0:8] * valid
            if ds == 0:
                padded[1:9, col] = value
            elif dt == 0:
                padded[row, 1:9] = value
            else:
                padded[row, col] = value

    z_place = lax.broadcasted_iota(jnp.int32, (10, 8, C), 1)

    def widen(target):
        def slab(i, carry):
            value = padded[i]
            before = jnp.where(z_place == 0, 0.0, pltpu.roll(value, 1, 1))
            after = jnp.where(z_place == 7, 0.0, pltpu.roll(value, 7, 1))
            start = pl.multiple_of(i * 64, 64)
            for sy in range(3):
                for sz, shifted in enumerate((before, value, after)):
                    column = (3 * sy + sz) * C
                    target[pl.ds(start, 64), column : column + C] = (
                        shifted[sy : sy + 8].reshape(64, C).astype(BF16)
                    )
            return carry

        lax.fori_loop(0, 10, slab, 0)

    loads[1].wait()
    masked_grad = masked_of(cot_v)
    padded[1:9, 1:9] = masked_grad
    fill_halo(0, masked_grad)
    pl.semaphore_wait(barrier, 8 + 1 + (nx - 1) + (ny - 1) + 2)
    halo_g = halo_copies(0)
    for copy in halo_g:
        copy.start()
    tell(0)
    loads[2].wait()
    masked = masked_of(feat_v)
    fill_halo(1, masked)
    halo_f = halo_copies(1)
    for copy in halo_f:
        copy.start()
    hear(0)
    tell(1)
    features_t[...] = jnp.transpose(masked.reshape(512, C)).astype(BF16)

    for copy in halo_g:
        copy.wait_recv()
    place_halo(0)
    widen(wide_g)

    def terms(sx, first, last):
        for q in range(first, last, 2):
            end = min(q + 2, last)
            result = dot(features_t[...], wide_g[sx * 64 : sx * 64 + 512, q * C : end * C])
            for j in range(q, end):
                part[26 - (9 * sx + j)] = result[:, (j - q) * C : (j - q + 1) * C]

    mine = core * 14
    theirs = (1 - core) * 14

    def pair_copy(half):
        return pltpu.make_async_remote_copy(
            src_ref=part.at[pl.ds(theirs + 7 * half, 7)],
            dst_ref=pair_buf.at[pl.ds(7 * half, 7)],
            send_sem=pair_send.at[half],
            recv_sem=pair_recv.at[half],
            device_id=sibling,
            device_id_type=MESH,
        )

    hear(1)
    tell(2)

    def offset_terms(first):
        for sx in range(3):
            inside_sx = [26 - o - 9 * sx for o in range(first, min(first + 7, 27)) if (26 - o) // 9 == sx]
            if inside_sx:
                terms(sx, min(inside_sx), max(inside_sx) + 1)

    def for_core(first, second):
        @pl.when(core == 0)
        def _():
            offset_terms(first)

        @pl.when(core == 1)
        def _():
            offset_terms(second)

    part[27] = jnp.zeros((C, C), F32)
    pair = {}
    for half in (1, 0):
        for_core(14 + 7 * half, 7 * half)
        pair[half] = pair_copy(half)
        pair[half].start()

    first_size = {0: nx, 1: ny}
    second_size = {0: ny, 1: nx}
    first_block = {0: block, 1: block_y}
    first_place = {0: x * block, 1: y * block_y}
    second_place = {0: x * block + y * rows, 1: y * block_y + x * rows}

    def first_index(half, d):
        return x_peer(d + nx) if half == 0 else y_peer(d + ny)

    def first_device(half, d):
        if half == 0:
            return at(x_peer(d + nx), y, z, core)
        return at(x, y_peer(d + ny), z, core)

    def second_peer(half, d):
        return (x, y_peer(d)) if half == 0 else (x_peer(d), y)

    def first_copy(half, slot):
        sign = 1 if slot % 2 == 0 else -1
        upper = {0: 0, 1: 1, 2: 1, 3: 0, 4: 0, 5: 1}[slot]
        target = first_index(half, 2 if slot < 2 else sign)
        size = first_block[half] // 2
        start = pl.multiple_of(target * first_block[half] + upper * size, 8)
        return pltpu.make_async_remote_copy(
            src_ref=part.at[pl.ds(mine + 7 * half, 7), pl.ds(start, size)],
            dst_ref=first_buf.at[half, slot, :, 0:size],
            send_sem=first_send.at[half, slot],
            recv_sem=first_recv.at[half, slot],
            device_id=first_device(half, sign),
            device_id_type=MESH,
        )

    def first_start(half):
        ring = first_size[half] > 2
        firsts[half] = {slot: first_copy(half, slot) for slot in ((0, 1, 2, 3) if ring else (2, 3))}
        for copy in firsts[half].values():
            copy.start()

    def first_relay(half):
        if first_size[half] == 2:
            return
        size = first_block[half] // 2
        for slot in (0, 1):
            firsts[half][slot].wait_recv()
            target = first_index(half, 1 if slot == 0 else -1)
            where = pl.ds(pl.multiple_of(target * first_block[half] + slot * size, 8), size)
            part[pl.ds(mine + 7 * half, 7), where] = (
                part[pl.ds(mine + 7 * half, 7), where] + first_buf[half, slot, :, 0:size]
            )
            firsts[half][slot + 4] = first_copy(half, slot + 4)
            firsts[half][slot + 4].start()

    def second_copies(half):
        copies = []
        base = first_place[half]
        for d in range(1, second_size[half]):
            px, py = second_peer(half, d)
            index = py if half == 0 else px
            start = pl.multiple_of(base + index * rows, 8)
            copies.append(
                pltpu.make_async_remote_copy(
                    src_ref=part.at[pl.ds(mine + 7 * half, 7), pl.ds(start, rows)],
                    dst_ref=second_buf.at[half, d - 1],
                    send_sem=second_send.at[half, d - 1],
                    recv_sem=second_recv.at[half, d - 1],
                    device_id=at(px, py, z, core),
                    device_id_type=MESH,
                )
            )
        return copies

    def add_pair(half):
        pair[half].wait_recv()

        def one(i, carry):
            part[mine + 7 * half + i] = part[mine + 7 * half + i] + pair_buf[7 * half + i]
            return carry

        lax.fori_loop(0, 7, one, 0)

    def add_first(half):
        size = first_block[half] // 2
        for upper, slots_of in ((0, (3, 4)), (1, (2, 5))):
            where = pl.ds(pl.multiple_of(first_place[half] + upper * size, 8), size)
            value = part[pl.ds(mine + 7 * half, 7), where]
            for slot in slots_of:
                if slot in firsts[half]:
                    firsts[half][slot].wait_recv()
                    value = value + first_buf[half, slot, :, 0:size]
            part[pl.ds(mine + 7 * half, 7), where] = value

    def add_second(half, copies):
        for copy in copies:
            copy.wait_recv()
        where = pl.ds(pl.multiple_of(second_place[half], 8), rows)
        value = part[pl.ds(mine + 7 * half, 7), where]
        for d in range(1, second_size[half]):
            value = value + second_buf[half, d - 1]
        for i in range(7):
            tiles[i // per_owner, half, i % per_owner] = value[i]

    firsts, seconds = {}, {}
    for half in (1, 0):
        for_core(7 * half, 14 + 7 * half)
        add_pair(half)
        first_start(half)

    padded[1:9, 1:9] = masked_of(feat_v)
    for copy in halo_f:
        copy.wait_recv()
    place_halo(1)
    widen(wide_f)
    for half in (1, 0):
        first_relay(half)

    def convolved(wide, weight, target):
        value = dot(wide[0:512, :], weight(0))
        value = value + dot(wide[64:576, :], weight(1))
        value = value + dot(wide[128:640, :], weight(2))
        value = value.reshape(8, 8, 8, C) * mask_v[...]
        target[...] = value.astype(BF16)

    loads[3].wait()
    convolved(wide_f, lambda a: kern_v[9 * a : 9 * a + 9].reshape(9 * C, C), out_v)
    out_copy = pltpu.make_async_copy(out_v, out_ref, out_sem.at[0])
    out_copy.start()

    for half in (1, 0):
        add_first(half)
        seconds[half] = second_copies(half)
        for copy in seconds[half]:
            copy.start()
    def z_part(ref, owner):
        return ref.at[owner // 2, owner % 2]

    def z_copy(d):
        return pltpu.make_async_remote_copy(
            src_ref=z_part(tiles, z_peer(d)),
            dst_ref=z_buf.at[pl.ds((d - 1) * per_owner, per_owner)],
            send_sem=z_send,
            recv_sem=z_recv,
            device_id=at(x, y, z_peer(d), core),
            device_id_type=MESH,
        )

    def zg_copy(d):
        return pltpu.make_async_remote_copy(
            src_ref=z_part(z_all, z),
            dst_ref=z_part(z_all, z),
            send_sem=zg_send,
            recv_sem=zg_recv.at[z % 2],
            device_id=at(x, y, z_peer(d), core),
            device_id_type=MESH,
        )

    def z_bytes(count, sends, receives):
        return pltpu.make_async_remote_copy(
            src_ref=z_buf.at[0 : count * per_owner],
            dst_ref=z_buf.at[0 : count * per_owner],
            send_sem=sends,
            recv_sem=receives,
            device_id=sibling,
            device_id_type=MESH,
        )

    z_whole = z_bytes(nz - 1, z_send, z_recv)
    zg_whole = z_bytes(nz - 1, zg_send, zg_recv.at[0])

    def zg_arrived(half):
        @pl.when(z % 2 != half)
        def _():
            z_bytes(nz // 2, zg_send, zg_recv.at[half]).wait_recv()

        if nz > 2:

            @pl.when(z % 2 == half)
            def _():
                z_bytes(nz // 2 - 1, zg_send, zg_recv.at[half]).wait_recv()

    hear(2)
    if slots > 14:
        tiles[nz // 2 - 1] = jnp.zeros((2, per_owner, rows, C), F32)
    for half in (1, 0):
        add_second(half, seconds[half])

        def z_start(k, carry):
            d = 2 * k + (z + half) % 2

            @pl.when(d > 0)
            def _():
                z_copy(d).start()

            return carry

        lax.fori_loop(0, nz // 2, z_start, 0)

    def flip(s, carry):
        start = pl.multiple_of(s * C, C)
        kern_t[pl.ds(start, C), :] = jnp.transpose(kern_v[26 - s].astype(F32)).astype(BF16)
        return carry

    lax.fori_loop(0, 27, flip, 0)

    z_whole.wait_recv()
    value = tiles[z // 2, z % 2]
    for d in range(1, nz):
        value = value + z_buf[(d - 1) * per_owner : d * per_owner]
    z_all[z // 2, z % 2] = value * scale

    def zg_start(d, carry):
        zg_copy(d).start()
        return carry

    lax.fori_loop(1, nz, zg_start, 0)

    for copy in halo_g + halo_f + [pair[0], pair[1]]:
        copy.wait_send()
    for half in (1, 0):
        for copy in list(firsts[half].values()) + seconds[half]:
            copy.wait_send()
    z_whole.wait_send()

    def gathered(half, offsets, row, size):
        return total.at[pl.ds(offsets + 7 * half, 7), pl.ds(pl.multiple_of(row, 8), size)]

    def z_half(half):
        return z_all.at[0:7, half, 0] if per_owner == 1 else z_all.at[0, half]

    def second_back(half, d, row):
        return pltpu.make_async_remote_copy(
            src_ref=z_half(half),
            dst_ref=gathered(half, mine, row, rows),
            send_sem=sg_send.at[half, d - 1],
            recv_sem=sg_recv.at[half, d - 1],
            device_id=at(*second_peer(half, d), z, core),
            device_id_type=MESH,
        )

    def first_back(half, slot, target):
        sign = 1 if slot % 2 == 0 else -1
        upper = {0: 0, 1: 1, 2: 1, 3: 0, 4: 0, 5: 1}[slot]
        size = first_block[half] // 2
        row = target * first_block[half] + upper * size
        return pltpu.make_async_remote_copy(
            src_ref=gathered(half, mine, row, size),
            dst_ref=gathered(half, mine, row, size),
            send_sem=fg_send.at[half, slot],
            recv_sem=fg_recv.at[half, slot],
            device_id=first_device(half, sign),
            device_id_type=MESH,
        )

    def source_of(half, slot):
        sign = 1 if slot % 2 == 0 else -1
        return first_index(half, -sign if slot < 4 else 2)

    def pair_back(half, slot, offsets):
        size = first_block[half]
        if slot == 6:
            row = first_index(half, 0) * size
        else:
            size = size // 2
            upper = {0: 0, 1: 1, 2: 1, 3: 0, 4: 0, 5: 1}[slot]
            row = source_of(half, slot) * 2 * size + upper * size
        return pltpu.make_async_remote_copy(
            src_ref=gathered(half, offsets, row, size),
            dst_ref=gathered(half, offsets, row, size),
            send_sem=pg_send.at[half, slot],
            recv_sem=pg_recv.at[half, slot],
            device_id=sibling,
            device_id_type=MESH,
        )

    convolved(wide_g, lambda a: kern_t[a * 9 * C : (a + 1) * 9 * C, :], fgrad_v)
    fgrad_copy = pltpu.make_async_copy(fgrad_v, fgrad_ref, out_sem.at[1])
    fgrad_copy.start()

    sent = []
    keeps = {}
    for half in (1, 0):
        zg_arrived(half)
        for d in range(1, second_size[half]):
            copy = second_back(half, d, second_place[half])
            copy.start()
            sent.append(copy)
        keeps[half] = pltpu.make_async_copy(
            z_half(half),
            gathered(half, mine, second_place[half], rows),
            own_sem.at[half],
        )
        keeps[half].start()
    for half in (1, 0):
        n = second_size[half]
        for d in range(1, n):
            from_index = ((y if half == 0 else x) - d + n) % n
            second_back(half, d, first_place[half] + from_index * rows).wait_recv()
        keeps[half].wait()
        for slot in (0, 1, 2, 3) if first_size[half] > 2 else (0, 1):
            copy = first_back(half, slot, first_index(half, 0))
            copy.start()
            sent.append(copy)
        copy = pair_back(half, 6, mine)
        copy.start()
        sent.append(copy)

    forwarded = []
    for slot in range(6):
        for half in (1, 0):
            if first_size[half] > 2 or slot < 2:
                first_back(half, slot, source_of(half, slot)).wait_recv()
                if first_size[half] > 2 and slot < 2:
                    copy = first_back(half, slot + 4, source_of(half, slot))
                    copy.start()
                    sent.append(copy)
                copy = pair_back(half, slot, mine)
                copy.start()
                forwarded.append(copy)
    zg_whole.wait_send()
    for copy in sent:
        copy.wait_send()
    out_copy.wait()
    fgrad_copy.wait()
    for slot in (6, 0, 1, 2, 3, 4, 5):
        for half in (1, 0):
            if first_size[half] > 2 or slot in (6, 0, 1):
                pair_back(half, slot, theirs).wait_recv()
    for copy in forwarded:
        copy.wait_send()


def shards(chips, features, occupancy, weights, cotangent):
    nx, ny, nz = chips
    voxels = 512 * nx * ny * nz * 2
    scale = 1.0 / math.sqrt(voxels)
    rows = C // (nx * ny)
    per_owner = -(-14 // nz)
    most = max(nx, ny)
    dma = pltpu.SemaphoreType.DMA
    results = pl.pallas_call(
        functools.partial(kernel, chips, scale),
        out_shape=(
            jax.ShapeDtypeStruct((8, 8, 8, C), BF16),
            jax.ShapeDtypeStruct((8, 8, 8, C), BF16),
            jax.ShapeDtypeStruct((28, C, C), F32),
        ),
        in_specs=[pl.BlockSpec(memory_space=pltpu.HBM)] * 4,
        out_specs=[pl.BlockSpec(memory_space=pl.ANY)] * 3,
        scratch_shapes=[
            pltpu.VMEM((8, 8, 8, C), BF16),
            pltpu.VMEM((8, 8, 8, C), BF16),
            pltpu.VMEM((8, 8, 8), jnp.int32),
            pltpu.VMEM((27, C, C), BF16),
            pltpu.VMEM((27 * C, C), BF16),
            pltpu.VMEM((8, 8, 8, C), F32),
            pltpu.VMEM((C, 512), BF16),
            pltpu.VMEM((10, 10, 8, C), F32),
            pltpu.VMEM((640, 9 * C), BF16),
            pltpu.VMEM((640, 9 * C), BF16),
            pltpu.VMEM((2, 4, 64, C), BF16),
            pltpu.VMEM((2, 4, 16, C), BF16),
            pltpu.VMEM((2, 4, 64, C), BF16),
            pltpu.VMEM((2, 4, 16, C), BF16),
            pltpu.VMEM((28, C, C), F32),
            pltpu.VMEM((14, C, C), F32),
            pltpu.VMEM((2, 6, 7, C // (2 * min(nx, ny)), C), F32),
            pltpu.VMEM((2, most - 1, 7, rows, C), F32),
            pltpu.VMEM((nz // 2, 2, per_owner, rows, C), F32),
            pltpu.VMEM(((nz - 1) * per_owner, rows, C), F32),
            pltpu.VMEM((nz // 2, 2, per_owner, rows, C), F32),
            pltpu.VMEM((8, 8, 8, C), BF16),
            pltpu.VMEM((8, 8, 8, C), BF16),
            dma((4,)),
            dma((2,)),
            dma((2,)),
            pltpu.SemaphoreType.REGULAR((3,)),
            dma((2, 8)),
            dma((2, 8)),
            dma((2,)),
            dma((2,)),
            dma((2, 6)),
            dma((2, 6)),
            dma((2, most - 1)),
            dma((2, most - 1)),
            dma,
            dma,
            dma,
            dma((2,)),
            dma((2, most - 1)),
            dma((2, most - 1)),
            dma((2, 6)),
            dma((2, 6)),
            dma((2, 7)),
            dma((2, 7)),
        ],
        compiler_params=pltpu.CompilerParams(
            collective_id=0, has_side_effects=True, vmem_limit_bytes=48 * 1024 * 1024
        ),
        cost_estimate=pl.CostEstimate(
            flops=3 * 2 * 512 * 27 * C * C, bytes_accessed=4_000_000, transcendentals=0
        ),
    )(*(pltpu.with_memory_space_constraint(a, pltpu.HBM) for a in (features, occupancy, weights, cotangent)))
    return results[0], results[1], results[2][:27]


def solution(mesh, chips=CHIPS):
    in_specs = (
        P("space", "tile", None, None),
        P("space", "tile", None),
        P(),
        P("space", "tile", None, None),
    )
    out_specs = (P("space", "tile", None, None), P("space", "tile", None, None), P())
    return jax.shard_map(
        functools.partial(shards, chips),
        mesh=mesh,
        in_specs=in_specs,
        out_specs=out_specs,
        check_vma=False,
    )
```

```python
import functools
import math

import jax
import jax.numpy as jnp
from jax import lax
from jax.experimental import pallas as pl
from jax.experimental.pallas import tpu as pltpu
from jax.sharding import PartitionSpec as P

MESH = pl.DeviceIdType.MESH
CHIPS = (4, 4, 16)
C = 128
DIRS = ((1, 0), (-1, 0), (0, 1), (0, -1), (1, 1), (1, -1), (-1, 1), (-1, -1))
F32 = jnp.float32
BF16 = jnp.bfloat16


def dot(a, b):
    return jnp.dot(a, b, preferred_element_type=F32)


def kernel(
    chips,
    scale,
    feat_hbm,
    occ_hbm,
    kern_hbm,
    cot_hbm,
    out_ref,
    fgrad_ref,
    total,
    feat_v,
    cot_v,
    occ_v,
    kern_v,
    kern_t,
    mask_v,
    features_t,
    padded,
    wide_f,
    wide_g,
    send_face,
    send_corner,
    recv_face,
    recv_corner,
    acc,
    part,
    pair_buf,
    first_buf,
    second_buf,
    tiles,
    z_buf,
    z_all,
    out_v,
    fgrad_v,
    in_sem,
    out_sem,
    own_sem,
    known,
    halo_send,
    halo_recv,
    pair_send,
    pair_recv,
    first_send,
    first_recv,
    second_send,
    second_recv,
    z_send,
    z_recv,
    zg_send,
    zg_recv,
    sg_send,
    sg_recv,
    fg_send,
    fg_recv,
    pg_send,
    pg_recv,
):
    nx, ny, nz = chips
    n_space, n_tile = nx * nz, ny * 2
    space, tile = lax.axis_index("space"), lax.axis_index("tile")
    x, z = space // nz, space % nz
    y, core = tile // 2, tile % 2
    block = C // nx
    block_y = C // ny
    rows = C // (nx * ny)
    per_owner = -(-14 // nz)
    slots = nz * per_owner

    def at(px, py, pz, pc):
        return {"space": px * nz + pz, "tile": py * 2 + pc}

    def x_peer(d):
        return (x + d) % nx

    def y_peer(d):
        return (y + d) % ny

    def z_peer(d):
        return (z + d) % nz

    def halo_peer(i):
        ds, dt = DIRS[i]
        return {
            "space": (space + ds + n_space) % n_space,
            "tile": (tile + dt + n_tile) % n_tile,
        }

    sibling = at(x, y, z, 1 - core)

    loads = [
        pltpu.make_async_copy(src, dst, in_sem.at[i])
        for i, (src, dst) in enumerate(
            ((occ_hbm, occ_v), (cot_hbm, cot_v), (feat_hbm, feat_v), (kern_hbm, kern_v))
        )
    ]
    for load in loads:
        load.start()

    barrier = pltpu.get_barrier_semaphore()

    def greet(device):
        pl.semaphore_signal(barrier, inc=1, device_id=device, device_id_type=MESH)

    for i in range(8):
        greet(halo_peer(i))
    greet(sibling)
    for d in range(1, nx):
        greet(at(x_peer(d), y, z, core))
    for d in range(1, ny):
        greet(at(x, y_peer(d), z, core))

    for d in (1, -1):
        greet(at(x, y, z_peer(d + nz), core))

    def tell(step):
        d = 2**step
        if d < nz // 2:
            for side in (d, -d):
                pl.semaphore_signal(
                    known.at[step],
                    inc=1,
                    device_id=at(x, y, z_peer(side + nz), core),
                    device_id_type=MESH,
                )

    def hear(step):
        if 2**step < nz // 2:
            pl.semaphore_wait(known.at[step], 2)

    loads[0].wait()
    cells = occ_v[...].reshape(64, 8).astype(F32).astype(BF16)
    pick = lax.broadcasted_iota(jnp.int32, (512, 64), 0) // 8
    pick = (pick == lax.broadcasted_iota(jnp.int32, (512, 64), 1)).astype(F32)
    spread = dot(pick.astype(BF16), cells)
    own = lax.broadcasted_iota(jnp.int32, (512, 8), 0) % 8
    own = own == lax.broadcasted_iota(jnp.int32, (512, 8), 1)
    column = jnp.sum(jnp.where(own, spread, 0.0), axis=1, keepdims=True)
    mask_v[...] = jnp.broadcast_to(column, (512, C)).reshape(8, 8, 8, C)

    def masked_of(source):
        return source[...].astype(F32) * mask_v[...]

    def fill_halo(which, value):
        edge_x = {1: value[7], -1: value[0]}
        edge_y = {1: value[:, 7], -1: value[:, 0]}
        for i in range(2):
            send_face[which, i] = edge_x[DIRS[i][0]].reshape(64, C).astype(BF16)
        for i in range(2, 4):
            send_face[which, i] = edge_y[DIRS[i][1]].reshape(64, C).astype(BF16)
        for i in range(4, 8):
            corner = edge_x[DIRS[i][0]][7 if DIRS[i][1] == 1 else 0]
            send_corner[which, i - 4] = jnp.concatenate([corner, corner], axis=0).astype(BF16)

    def halo_copies(which):
        copies = []
        for i in range(8):
            if i < 4:
                source, target = send_face.at[which, i], recv_face.at[which, i]
            else:
                source, target = send_corner.at[which, i - 4], recv_corner.at[which, i - 4]
            copies.append(
                pltpu.make_async_remote_copy(
                    src_ref=source,
                    dst_ref=target,
                    send_sem=halo_send.at[which, i // 4],
                    recv_sem=halo_recv.at[which, i // 4],
                    device_id=halo_peer(i),
                    device_id_type=MESH,
                )
            )
        return copies

    def halo_whole(which):
        return [
            pltpu.make_async_remote_copy(
                src_ref=source.at[which],
                dst_ref=target.at[which],
                send_sem=halo_send.at[which, i],
                recv_sem=halo_recv.at[which, i],
                device_id=sibling,
                device_id_type=MESH,
            )
            for i, (source, target) in enumerate(((send_face, recv_face), (send_corner, recv_corner)))
        ]

    inside = {
        (0, 1): (space > 0).astype(F32),
        (0, -1): (space < n_space - 1).astype(F32),
        (1, 1): (tile > 0).astype(F32),
        (1, -1): (tile < n_tile - 1).astype(F32),
    }

    def place_halo(which):
        for i in range(8):
            ds, dt = DIRS[i]
            valid = 1.0
            if ds:
                valid = valid * inside[0, ds]
            if dt:
                valid = valid * inside[1, dt]
            row, col = {1: 0, -1: 9}.get(ds), {1: 0, -1: 9}.get(dt)
            if i < 4:
                value = recv_face[which, i].astype(F32).reshape(8, 8, C) * valid
            else:
                value = recv_corner[which, i - 4].astype(F32)[0:8] * valid
            if ds == 0:
                padded[1:9, col] = value
            elif dt == 0:
                padded[row, 1:9] = value
            else:
                padded[row, col] = value

    z_place = lax.broadcasted_iota(jnp.int32, (10, 8, C), 1)

    def widen(target):
        def slab(i, carry):
            value = padded[i]
            before = jnp.where(z_place == 0, 0.0, pltpu.roll(value, 1, 1))
            after = jnp.where(z_place == 7, 0.0, pltpu.roll(value, 7, 1))
            start = pl.multiple_of(i * 64, 64)
            for sy in range(3):
                for sz, shifted in enumerate((before, value, after)):
                    column = (3 * sy + sz) * C
                    target[pl.ds(start, 64), column : column + C] = (
                        shifted[sy : sy + 8].reshape(64, C).astype(BF16)
                    )
            return carry

        lax.fori_loop(0, 10, slab, 0)

    loads[1].wait()
    masked_grad = masked_of(cot_v)
    padded[1:9, 1:9] = masked_grad
    fill_halo(0, masked_grad)
    pl.semaphore_wait(barrier, 8 + 1 + (nx - 1) + (ny - 1) + 2)
    halo_g = halo_copies(0)
    for copy in halo_g:
        copy.start()
    tell(0)
    loads[2].wait()
    masked = masked_of(feat_v)
    fill_halo(1, masked)
    halo_f = halo_copies(1)
    for copy in halo_f:
        copy.start()
    hear(0)
    tell(1)
    features_t[...] = jnp.transpose(masked.reshape(512, C)).astype(BF16)

    for copy in halo_whole(0):
        copy.wait_recv()
    place_halo(0)
    widen(wide_g)

    def terms(first):
        def two(i, carry):
            for half in range(2):
                offset = first + 7 * half + i
                shift = (53 - offset) % 27
                start = pl.multiple_of((shift // 9) * 64, 64)
                column = pl.multiple_of((shift % 9) * C, C)
                part[offset] = dot(features_t[...], wide_g[pl.ds(start, 512), pl.ds(column, C)])
            return carry

        lax.fori_loop(0, 7, two, 0)

    mine = core * 14
    theirs = (1 - core) * 14

    def pair_copy(half):
        return pltpu.make_async_remote_copy(
            src_ref=part.at[pl.ds(theirs + 7 * half, 7)],
            dst_ref=pair_buf.at[pl.ds(7 * half, 7)],
            send_sem=pair_send.at[half],
            recv_sem=pair_recv.at[half],
            device_id=sibling,
            device_id_type=MESH,
        )

    hear(1)
    tell(2)

    pair = {}
    terms(theirs)
    for half in (1, 0):
        pair[half] = pair_copy(half)
        pair[half].start()

    first_size = {0: nx, 1: ny}
    second_size = {0: ny, 1: nx}
    first_block = {0: block, 1: block_y}
    first_place = {0: x * block, 1: y * block_y}
    second_place = {0: x * block + y * rows, 1: y * block_y + x * rows}

    def first_index(half, d):
        return x_peer(d + nx) if half == 0 else y_peer(d + ny)

    def first_device(half, d):
        if half == 0:
            return at(x_peer(d + nx), y, z, core)
        return at(x, y_peer(d + ny), z, core)

    def second_peer(half, d):
        return (x, y_peer(d)) if half == 0 else (x_peer(d), y)

    def first_copy(half, slot):
        sign = 1 if slot % 2 == 0 else -1
        upper = {0: 0, 1: 1, 2: 1, 3: 0, 4: 0, 5: 1}[slot]
        target = first_index(half, 2 if slot < 2 else sign)
        size = first_block[half] // 2
        start = pl.multiple_of(target * first_block[half] + upper * size, 8)
        return pltpu.make_async_remote_copy(
            src_ref=part.at[pl.ds(mine + 7 * half, 7), pl.ds(start, size)],
            dst_ref=first_buf.at[half, slot, :, 0:size],
            send_sem=first_send.at[half, slot],
            recv_sem=first_recv.at[half, slot],
            device_id=first_device(half, sign),
            device_id_type=MESH,
        )

    def first_start(half):
        ring = first_size[half] > 2
        firsts[half] = {slot: first_copy(half, slot) for slot in ((0, 1, 2, 3) if ring else (2, 3))}
        for copy in firsts[half].values():
            copy.start()

    def first_relay(half):
        if first_size[half] == 2:
            return
        size = first_block[half] // 2
        for slot in (0, 1):
            firsts[half][slot].wait_recv()
            target = first_index(half, 1 if slot == 0 else -1)
            where = pl.ds(pl.multiple_of(target * first_block[half] + slot * size, 8), size)
            part[pl.ds(mine + 7 * half, 7), where] = (
                part[pl.ds(mine + 7 * half, 7), where] + first_buf[half, slot, :, 0:size]
            )
            firsts[half][slot + 4] = first_copy(half, slot + 4)
            firsts[half][slot + 4].start()

    def second_copies(half):
        copies = []
        base = first_place[half]
        for d in range(1, second_size[half]):
            px, py = second_peer(half, d)
            index = py if half == 0 else px
            start = pl.multiple_of(base + index * rows, 8)
            copies.append(
                pltpu.make_async_remote_copy(
                    src_ref=part.at[pl.ds(mine + 7 * half, 7), pl.ds(start, rows)],
                    dst_ref=second_buf.at[half, d - 1],
                    send_sem=second_send.at[half, d - 1],
                    recv_sem=second_recv.at[half, d - 1],
                    device_id=at(px, py, z, core),
                    device_id_type=MESH,
                )
            )
        return copies

    def add_pair(half):
        pair[half].wait_recv()

        def one(i, carry):
            part[mine + 7 * half + i] = part[mine + 7 * half + i] + pair_buf[7 * half + i]
            return carry

        lax.fori_loop(0, 7, one, 0)

    def add_first(half):
        size = first_block[half] // 2
        for upper, slots_of in ((0, (3, 4)), (1, (2, 5))):
            where = pl.ds(pl.multiple_of(first_place[half] + upper * size, 8), size)
            value = part[pl.ds(mine + 7 * half, 7), where]
            for slot in slots_of:
                if slot in firsts[half]:
                    firsts[half][slot].wait_recv()
                    value = value + first_buf[half, slot, :, 0:size]
            part[pl.ds(mine + 7 * half, 7), where] = value

    def add_second(half, copies):
        for copy in copies:
            copy.wait_recv()
        where = pl.ds(pl.multiple_of(second_place[half], 8), rows)
        value = part[pl.ds(mine + 7 * half, 7), where]
        for d in range(1, second_size[half]):
            value = value + second_buf[half, d - 1]
        for i in range(7):
            tiles[i // per_owner, half, i % per_owner] = value[i]

    firsts, seconds = {}, {}
    terms(mine)
    for half in (1, 0):
        add_pair(half)
        first_start(half)

    padded[1:9, 1:9] = masked_of(feat_v)
    for copy in halo_whole(1):
        copy.wait_recv()
    place_halo(1)
    widen(wide_f)
    for half in (1, 0):
        first_relay(half)

    def convolved(wide, weight, target):
        acc[...] = jnp.zeros((512, C), F32)

        def add(a, carry):
            start = pl.multiple_of(a * 64, 64)
            acc[...] = acc[...] + dot(wide[pl.ds(start, 512), :], weight(a))
            return carry

        lax.fori_loop(0, 3, add, 0)
        value = acc[...].reshape(8, 8, 8, C) * mask_v[...]
        target[...] = value.astype(BF16)

    loads[3].wait()
    convolved(wide_f, lambda a: kern_v[pl.ds(9 * a, 9)].reshape(9 * C, C), out_v)
    out_copy = pltpu.make_async_copy(out_v, out_ref, out_sem.at[0])
    out_copy.start()

    for half in (1, 0):
        add_first(half)
        seconds[half] = second_copies(half)
        for copy in seconds[half]:
            copy.start()
    def z_part(ref, owner):
        return ref.at[owner // 2, owner % 2]

    def z_copy(d):
        return pltpu.make_async_remote_copy(
            src_ref=z_part(tiles, z_peer(d)),
            dst_ref=z_buf.at[pl.ds((d - 1) * per_owner, per_owner)],
            send_sem=z_send,
            recv_sem=z_recv,
            device_id=at(x, y, z_peer(d), core),
            device_id_type=MESH,
        )

    def zg_copy(d):
        return pltpu.make_async_remote_copy(
            src_ref=z_part(z_all, z),
            dst_ref=z_part(z_all, z),
            send_sem=zg_send,
            recv_sem=zg_recv.at[z % 2],
            device_id=at(x, y, z_peer(d), core),
            device_id_type=MESH,
        )

    def z_bytes(count, sends, receives):
        return pltpu.make_async_remote_copy(
            src_ref=z_buf.at[0 : count * per_owner],
            dst_ref=z_buf.at[0 : count * per_owner],
            send_sem=sends,
            recv_sem=receives,
            device_id=sibling,
            device_id_type=MESH,
        )

    z_whole = z_bytes(nz - 1, z_send, z_recv)
    zg_whole = z_bytes(nz - 1, zg_send, zg_recv.at[0])

    def zg_arrived(half):
        @pl.when(z % 2 != half)
        def _():
            z_bytes(nz // 2, zg_send, zg_recv.at[half]).wait_recv()

        if nz > 2:

            @pl.when(z % 2 == half)
            def _():
                z_bytes(nz // 2 - 1, zg_send, zg_recv.at[half]).wait_recv()

    hear(2)
    if slots > 14:
        tiles[nz // 2 - 1] = jnp.zeros((2, per_owner, rows, C), F32)
    for half in (1, 0):
        add_second(half, seconds[half])

        def z_start(k, carry):
            d = 2 * k + (z + half) % 2

            @pl.when(d > 0)
            def _():
                z_copy(d).start()

            return carry

        lax.fori_loop(0, nz // 2, z_start, 0)

    def flip(s, carry):
        start = pl.multiple_of(s * C, C)
        kern_t[pl.ds(start, C), :] = jnp.transpose(kern_v[26 - s].astype(F32)).astype(BF16)
        return carry

    lax.fori_loop(0, 27, flip, 0)

    z_whole.wait_recv()
    value = tiles[z // 2, z % 2]
    for d in range(1, nz):
        value = value + z_buf[(d - 1) * per_owner : d * per_owner]
    z_all[z // 2, z % 2] = value * scale

    def zg_start(d, carry):
        zg_copy(d).start()
        return carry

    lax.fori_loop(1, nz, zg_start, 0)

    for copy in halo_whole(0) + halo_whole(1) + [pair[0], pair[1]]:
        copy.wait_send()
    for half in (1, 0):
        for copy in list(firsts[half].values()) + seconds[half]:
            copy.wait_send()
    z_whole.wait_send()

    def gathered(half, offsets, row, size):
        return total.at[pl.ds(offsets + 7 * half, 7), pl.ds(pl.multiple_of(row, 8), size)]

    def z_half(half):
        return z_all.at[0:7, half, 0] if per_owner == 1 else z_all.at[0, half]

    def second_back(half, d, row):
        return pltpu.make_async_remote_copy(
            src_ref=z_half(half),
            dst_ref=gathered(half, mine, row, rows),
            send_sem=sg_send.at[half, d - 1],
            recv_sem=sg_recv.at[half, d - 1],
            device_id=at(*second_peer(half, d), z, core),
            device_id_type=MESH,
        )

    def first_back(half, slot, target):
        sign = 1 if slot % 2 == 0 else -1
        upper = {0: 0, 1: 1, 2: 1, 3: 0, 4: 0, 5: 1}[slot]
        size = first_block[half] // 2
        row = target * first_block[half] + upper * size
        return pltpu.make_async_remote_copy(
            src_ref=gathered(half, mine, row, size),
            dst_ref=gathered(half, mine, row, size),
            send_sem=fg_send.at[half, slot],
            recv_sem=fg_recv.at[half, slot],
            device_id=first_device(half, sign),
            device_id_type=MESH,
        )

    def source_of(half, slot):
        sign = 1 if slot % 2 == 0 else -1
        return first_index(half, -sign if slot < 4 else 2)

    def pair_back(half, slot, offsets):
        size = first_block[half]
        if slot == 6:
            row = first_index(half, 0) * size
        else:
            size = size // 2
            upper = {0: 0, 1: 1, 2: 1, 3: 0, 4: 0, 5: 1}[slot]
            row = source_of(half, slot) * 2 * size + upper * size
        return pltpu.make_async_remote_copy(
            src_ref=gathered(half, offsets, row, size),
            dst_ref=gathered(half, offsets, row, size),
            send_sem=pg_send.at[half, slot],
            recv_sem=pg_recv.at[half, slot],
            device_id=sibling,
            device_id_type=MESH,
        )

    convolved(wide_g, lambda a: kern_t[pl.ds(pl.multiple_of(a * 9 * C, C), 9 * C), :], fgrad_v)
    fgrad_copy = pltpu.make_async_copy(fgrad_v, fgrad_ref, out_sem.at[1])
    fgrad_copy.start()

    sent = []
    keeps = {}
    for half in (1, 0):
        zg_arrived(half)
        for d in range(1, second_size[half]):
            copy = second_back(half, d, second_place[half])
            copy.start()
            sent.append(copy)
        keeps[half] = pltpu.make_async_copy(
            z_half(half),
            gathered(half, mine, second_place[half], rows),
            own_sem.at[half],
        )
        keeps[half].start()
    for half in (1, 0):
        n = second_size[half]
        for d in range(1, n):
            from_index = ((y if half == 0 else x) - d + n) % n
            second_back(half, d, first_place[half] + from_index * rows).wait_recv()
        keeps[half].wait()
        for slot in (0, 1, 2, 3) if first_size[half] > 2 else (0, 1):
            copy = first_back(half, slot, first_index(half, 0))
            copy.start()
            sent.append(copy)
        copy = pair_back(half, 6, mine)
        copy.start()
        sent.append(copy)

    forwarded = []
    for slot in range(6):
        for half in (1, 0):
            if first_size[half] > 2 or slot < 2:
                first_back(half, slot, source_of(half, slot)).wait_recv()
                if first_size[half] > 2 and slot < 2:
                    copy = first_back(half, slot + 4, source_of(half, slot))
                    copy.start()
                    sent.append(copy)
                copy = pair_back(half, slot, mine)
                copy.start()
                forwarded.append(copy)
    zg_whole.wait_send()
    for copy in sent:
        copy.wait_send()
    out_copy.wait()
    fgrad_copy.wait()
    for slot in (6, 0, 1, 2, 3, 4, 5):
        for half in (1, 0):
            if first_size[half] > 2 or slot in (6, 0, 1):
                pair_back(half, slot, theirs).wait_recv()
    for copy in forwarded:
        copy.wait_send()


def shards(chips, features, occupancy, weights, cotangent):
    nx, ny, nz = chips
    voxels = 512 * nx * ny * nz * 2
    scale = 1.0 / math.sqrt(voxels)
    rows = C // (nx * ny)
    per_owner = -(-14 // nz)
    most = max(nx, ny)
    dma = pltpu.SemaphoreType.DMA
    results = pl.pallas_call(
        functools.partial(kernel, chips, scale),
        out_shape=(
            jax.ShapeDtypeStruct((8, 8, 8, C), BF16),
            jax.ShapeDtypeStruct((8, 8, 8, C), BF16),
            jax.ShapeDtypeStruct((28, C, C), F32),
        ),
        in_specs=[pl.BlockSpec(memory_space=pltpu.HBM)] * 4,
        out_specs=[pl.BlockSpec(memory_space=pl.ANY)] * 3,
        scratch_shapes=[
            pltpu.VMEM((8, 8, 8, C), BF16),
            pltpu.VMEM((8, 8, 8, C), BF16),
            pltpu.VMEM((8, 8, 8), jnp.int32),
            pltpu.VMEM((27, C, C), BF16),
            pltpu.VMEM((27 * C, C), BF16),
            pltpu.VMEM((8, 8, 8, C), F32),
            pltpu.VMEM((C, 512), BF16),
            pltpu.VMEM((10, 10, 8, C), F32),
            pltpu.VMEM((640, 9 * C), BF16),
            pltpu.VMEM((640, 9 * C), BF16),
            pltpu.VMEM((2, 4, 64, C), BF16),
            pltpu.VMEM((2, 4, 16, C), BF16),
            pltpu.VMEM((2, 4, 64, C), BF16),
            pltpu.VMEM((2, 4, 16, C), BF16),
            pltpu.VMEM((512, C), F32),
            pltpu.VMEM((28, C, C), F32),
            pltpu.VMEM((14, C, C), F32),
            pltpu.VMEM((2, 6, 7, C // (2 * min(nx, ny)), C), F32),
            pltpu.VMEM((2, most - 1, 7, rows, C), F32),
            pltpu.VMEM((nz // 2, 2, per_owner, rows, C), F32),
            pltpu.VMEM(((nz - 1) * per_owner, rows, C), F32),
            pltpu.VMEM((nz // 2, 2, per_owner, rows, C), F32),
            pltpu.VMEM((8, 8, 8, C), BF16),
            pltpu.VMEM((8, 8, 8, C), BF16),
            dma((4,)),
            dma((2,)),
            dma((2,)),
            pltpu.SemaphoreType.REGULAR((3,)),
            dma((2, 2)),
            dma((2, 2)),
            dma((2,)),
            dma((2,)),
            dma((2, 6)),
            dma((2, 6)),
            dma((2, most - 1)),
            dma((2, most - 1)),
            dma,
            dma,
            dma,
            dma((2,)),
            dma((2, most - 1)),
            dma((2, most - 1)),
            dma((2, 6)),
            dma((2, 6)),
            dma((2, 7)),
            dma((2, 7)),
        ],
        compiler_params=pltpu.CompilerParams(
            collective_id=0, has_side_effects=True, vmem_limit_bytes=48 * 1024 * 1024
        ),
        cost_estimate=pl.CostEstimate(
            flops=3 * 2 * 512 * 27 * C * C, bytes_accessed=4_000_000, transcendentals=0
        ),
    )(*(pltpu.with_memory_space_constraint(a, pltpu.HBM) for a in (features, occupancy, weights, cotangent)))
    return results[0], results[1], results[2][:27]


def solution(mesh, chips=CHIPS):
    in_specs = (
        P("space", "tile", None, None),
        P("space", "tile", None),
        P(),
        P("space", "tile", None, None),
    )
    out_specs = (P("space", "tile", None, None), P("space", "tile", None, None), P())
    return jax.shard_map(
        functools.partial(shards, chips),
        mesh=mesh,
        in_specs=in_specs,
        out_specs=out_specs,
        check_vma=False,
    )
```

```python
import functools
import math

import jax
import jax.numpy as jnp
from jax import lax
from jax.experimental import pallas as pl
from jax.experimental.pallas import tpu as pltpu
from jax.sharding import PartitionSpec as P

MESH = pl.DeviceIdType.MESH
CHIPS = (4, 4, 16)
C = 128
DIRS = ((1, 0), (-1, 0), (0, 1), (0, -1), (1, 1), (1, -1), (-1, 1), (-1, -1))
F32 = jnp.float32
BF16 = jnp.bfloat16


def dot(a, b):
    return jnp.dot(a, b, preferred_element_type=F32)


def kernel(
    chips,
    scale,
    feat_hbm,
    occ_hbm,
    kern_hbm,
    cot_hbm,
    out_ref,
    fgrad_ref,
    total,
    feat_v,
    cot_v,
    occ_v,
    kern_v,
    kern_t,
    mask_v,
    features_t,
    padded,
    wide_f,
    wide_g,
    send_face,
    send_corner,
    recv_face,
    recv_corner,
    part,
    pair_buf,
    first_buf,
    second_buf,
    tiles,
    z_buf,
    z_sum,
    z_all,
    out_v,
    fgrad_v,
    in_sem,
    out_sem,
    own_sem,
    known,
    halo_send,
    halo_recv,
    pair_send,
    pair_recv,
    first_send,
    first_recv,
    second_send,
    second_recv,
    z_send,
    z_recv,
    zs_send,
    zs_recv,
    zg_send,
    zg_recv,
    sg_send,
    sg_recv,
    fg_send,
    fg_recv,
    pg_send,
    pg_recv,
):
    nx, ny, nz = chips
    n_space, n_tile = nx * nz, ny * 2
    space, tile = lax.axis_index("space"), lax.axis_index("tile")
    x, z = space // nz, space % nz
    y, core = tile // 2, tile % 2
    block = C // nx
    block_y = C // ny
    rows = C // (nx * ny)
    near = min(4, nz)
    groups = nz // near
    per_owner = 16 // near
    z_group, z_near = z // near, z % near

    def at(px, py, pz, pc):
        return {"space": px * nz + pz, "tile": py * 2 + pc}

    def x_peer(d):
        return (x + d) % nx

    def y_peer(d):
        return (y + d) % ny

    def z_peer(d):
        return (z + d) % nz

    def halo_peer(i):
        ds, dt = DIRS[i]
        return {
            "space": (space + ds + n_space) % n_space,
            "tile": (tile + dt + n_tile) % n_tile,
        }

    sibling = at(x, y, z, 1 - core)

    loads = [
        pltpu.make_async_copy(src, dst, in_sem.at[i])
        for i, (src, dst) in enumerate(
            ((occ_hbm, occ_v), (cot_hbm, cot_v), (feat_hbm, feat_v), (kern_hbm, kern_v))
        )
    ]
    for load in loads:
        load.start()

    barrier = pltpu.get_barrier_semaphore()

    def greet(device):
        pl.semaphore_signal(barrier, inc=1, device_id=device, device_id_type=MESH)

    for i in range(8):
        greet(halo_peer(i))
    greet(sibling)
    for d in range(1, nx):
        greet(at(x_peer(d), y, z, core))
    for d in range(1, ny):
        greet(at(x, y_peer(d), z, core))

    for d in (1, -1):
        greet(at(x, y, z_peer(d + nz), core))

    def tell(step):
        d = 2**step
        if d < nz // 2:
            for side in (d, -d):
                pl.semaphore_signal(
                    known.at[step],
                    inc=1,
                    device_id=at(x, y, z_peer(side + nz), core),
                    device_id_type=MESH,
                )

    def hear(step):
        if 2**step < nz // 2:
            pl.semaphore_wait(known.at[step], 2)

    loads[0].wait()
    cells = occ_v[...].reshape(64, 8).astype(F32).astype(BF16)
    pick = lax.broadcasted_iota(jnp.int32, (512, 64), 0) // 8
    pick = (pick == lax.broadcasted_iota(jnp.int32, (512, 64), 1)).astype(F32)
    spread = dot(pick.astype(BF16), cells)
    own = lax.broadcasted_iota(jnp.int32, (512, 8), 0) % 8
    own = own == lax.broadcasted_iota(jnp.int32, (512, 8), 1)
    column = jnp.sum(jnp.where(own, spread, 0.0), axis=1, keepdims=True)
    mask_v[...] = jnp.broadcast_to(column, (512, C)).reshape(8, 8, 8, C)

    def masked_of(source):
        return source[...].astype(F32) * mask_v[...]

    def fill_halo(which, value):
        edge_x = {1: value[7], -1: value[0]}
        edge_y = {1: value[:, 7], -1: value[:, 0]}
        for i in range(2):
            send_face[which, i] = edge_x[DIRS[i][0]].reshape(64, C).astype(BF16)
        for i in range(2, 4):
            send_face[which, i] = edge_y[DIRS[i][1]].reshape(64, C).astype(BF16)
        for i in range(4, 8):
            corner = edge_x[DIRS[i][0]][7 if DIRS[i][1] == 1 else 0]
            send_corner[which, i - 4] = jnp.concatenate([corner, corner], axis=0).astype(BF16)

    def halo_copies(which):
        copies = []
        for i in range(8):
            if i < 4:
                source, target = send_face.at[which, i], recv_face.at[which, i]
            else:
                source, target = send_corner.at[which, i - 4], recv_corner.at[which, i - 4]
            copies.append(
                pltpu.make_async_remote_copy(
                    src_ref=source,
                    dst_ref=target,
                    send_sem=halo_send.at[which, i],
                    recv_sem=halo_recv.at[which, i],
                    device_id=halo_peer(i),
                    device_id_type=MESH,
                )
            )
        return copies

    inside = {
        (0, 1): (space > 0).astype(F32),
        (0, -1): (space < n_space - 1).astype(F32),
        (1, 1): (tile > 0).astype(F32),
        (1, -1): (tile < n_tile - 1).astype(F32),
    }

    def place_halo(which):
        for i in range(8):
            ds, dt = DIRS[i]
            valid = 1.0
            if ds:
                valid = valid * inside[0, ds]
            if dt:
                valid = valid * inside[1, dt]
            row, col = {1: 0, -1: 9}.get(ds), {1: 0, -1: 9}.get(dt)
            if i < 4:
                value = recv_face[which, i].astype(F32).reshape(8, 8, C) * valid
            else:
                value = recv_corner[which, i - 4].astype(F32)[0:8] * valid
            if ds == 0:
                padded[1:9, col] = value
            elif dt == 0:
                padded[row, 1:9] = value
            else:
                padded[row, col] = value

    z_place = lax.broadcasted_iota(jnp.int32, (10, 8, C), 1)

    def widen(target):
        def slab(i, carry):
            value = padded[i]
            before = jnp.where(z_place == 0, 0.0, pltpu.roll(value, 1, 1))
            after = jnp.where(z_place == 7, 0.0, pltpu.roll(value, 7, 1))
            start = pl.multiple_of(i * 64, 64)
            for sy in range(3):
                for sz, shifted in enumerate((before, value, after)):
                    column = (3 * sy + sz) * C
                    target[pl.ds(start, 64), column : column + C] = (
                        shifted[sy : sy + 8].reshape(64, C).astype(BF16)
                    )
            return carry

        lax.fori_loop(0, 10, slab, 0)

    loads[1].wait()
    masked_grad = masked_of(cot_v)
    padded[1:9, 1:9] = masked_grad
    fill_halo(0, masked_grad)
    pl.semaphore_wait(barrier, 8 + 1 + (nx - 1) + (ny - 1) + 2)
    halo_g = halo_copies(0)
    for copy in halo_g:
        copy.start()
    tell(0)
    loads[2].wait()
    masked = masked_of(feat_v)
    fill_halo(1, masked)
    halo_f = halo_copies(1)
    for copy in halo_f:
        copy.start()
    hear(0)
    tell(1)
    features_t[...] = jnp.transpose(masked.reshape(512, C)).astype(BF16)

    for copy in halo_g:
        copy.wait_recv()
    place_halo(0)
    widen(wide_g)

    def terms(sx, first, last):
        for q in range(first, last, 2):
            end = min(q + 2, last)
            result = dot(features_t[...], wide_g[sx * 64 : sx * 64 + 512, q * C : end * C])
            for j in range(q, end):
                part[26 - (9 * sx + j)] = result[:, (j - q) * C : (j - q + 1) * C]

    mine = core * 14
    theirs = (1 - core) * 14

    def pair_copy(half):
        return pltpu.make_async_remote_copy(
            src_ref=part.at[pl.ds(theirs + 7 * half, 7)],
            dst_ref=pair_buf.at[pl.ds(7 * half, 7)],
            send_sem=pair_send.at[half],
            recv_sem=pair_recv.at[half],
            device_id=sibling,
            device_id_type=MESH,
        )

    hear(1)
    tell(2)

    def offset_terms(first):
        for sx in range(3):
            inside_sx = [26 - o - 9 * sx for o in range(first, min(first + 7, 27)) if (26 - o) // 9 == sx]
            if inside_sx:
                terms(sx, min(inside_sx), max(inside_sx) + 1)

    def for_core(first, second):
        @pl.when(core == 0)
        def _():
            offset_terms(first)

        @pl.when(core == 1)
        def _():
            offset_terms(second)

    part[27] = jnp.zeros((C, C), F32)
    pair = {}
    for half in (1, 0):
        for_core(14 + 7 * half, 7 * half)
        pair[half] = pair_copy(half)
        pair[half].start()

    first_size = {0: nx, 1: ny}
    second_size = {0: ny, 1: nx}
    first_block = {0: block, 1: block_y}
    first_place = {0: x * block, 1: y * block_y}
    second_place = {0: x * block + y * rows, 1: y * block_y + x * rows}

    def first_index(half, d):
        return x_peer(d + nx) if half == 0 else y_peer(d + ny)

    def first_device(half, d):
        if half == 0:
            return at(x_peer(d + nx), y, z, core)
        return at(x, y_peer(d + ny), z, core)

    def second_peer(half, d):
        return (x, y_peer(d)) if half == 0 else (x_peer(d), y)

    def first_copy(half, slot):
        sign = 1 if slot % 2 == 0 else -1
        upper = {0: 0, 1: 1, 2: 1, 3: 0, 4: 0, 5: 1}[slot]
        target = first_index(half, 2 if slot < 2 else sign)
        size = first_block[half] // 2
        start = pl.multiple_of(target * first_block[half] + upper * size, 8)
        return pltpu.make_async_remote_copy(
            src_ref=part.at[pl.ds(mine + 7 * half, 7), pl.ds(start, size)],
            dst_ref=first_buf.at[half, slot, :, 0:size],
            send_sem=first_send.at[half, slot],
            recv_sem=first_recv.at[half, slot],
            device_id=first_device(half, sign),
            device_id_type=MESH,
        )

    def first_start(half):
        ring = first_size[half] > 2
        firsts[half] = {slot: first_copy(half, slot) for slot in ((0, 1, 2, 3) if ring else (2, 3))}
        for copy in firsts[half].values():
            copy.start()

    def first_relay(half):
        if first_size[half] == 2:
            return
        size = first_block[half] // 2
        for slot in (0, 1):
            firsts[half][slot].wait_recv()
            target = first_index(half, 1 if slot == 0 else -1)
            where = pl.ds(pl.multiple_of(target * first_block[half] + slot * size, 8), size)
            part[pl.ds(mine + 7 * half, 7), where] = (
                part[pl.ds(mine + 7 * half, 7), where] + first_buf[half, slot, :, 0:size]
            )
            firsts[half][slot + 4] = first_copy(half, slot + 4)
            firsts[half][slot + 4].start()

    def second_copies(half):
        copies = []
        base = first_place[half]
        for d in range(1, second_size[half]):
            px, py = second_peer(half, d)
            index = py if half == 0 else px
            start = pl.multiple_of(base + index * rows, 8)
            copies.append(
                pltpu.make_async_remote_copy(
                    src_ref=part.at[pl.ds(mine + 7 * half, 7), pl.ds(start, rows)],
                    dst_ref=second_buf.at[half, d - 1],
                    send_sem=second_send.at[half, d - 1],
                    recv_sem=second_recv.at[half, d - 1],
                    device_id=at(px, py, z, core),
                    device_id_type=MESH,
                )
            )
        return copies

    def add_pair(half):
        pair[half].wait_recv()

        def one(i, carry):
            part[mine + 7 * half + i] = part[mine + 7 * half + i] + pair_buf[7 * half + i]
            return carry

        lax.fori_loop(0, 7, one, 0)

    def add_first(half):
        size = first_block[half] // 2
        for upper, slots_of in ((0, (3, 4)), (1, (2, 5))):
            where = pl.ds(pl.multiple_of(first_place[half] + upper * size, 8), size)
            value = part[pl.ds(mine + 7 * half, 7), where]
            for slot in slots_of:
                if slot in firsts[half]:
                    firsts[half][slot].wait_recv()
                    value = value + first_buf[half, slot, :, 0:size]
            part[pl.ds(mine + 7 * half, 7), where] = value

    def add_second(half, copies):
        for copy in copies:
            copy.wait_recv()
        where = pl.ds(pl.multiple_of(second_place[half], 8), rows)
        value = part[pl.ds(mine + 7 * half, 7), where]
        for d in range(1, second_size[half]):
            value = value + second_buf[half, d - 1]
        tiles[8 * half : 8 * half + 7] = value

    firsts, seconds = {}, {}
    for half in (1, 0):
        for_core(7 * half, 14 + 7 * half)
        add_pair(half)
        first_start(half)

    padded[1:9, 1:9] = masked_of(feat_v)
    for copy in halo_f:
        copy.wait_recv()
    place_halo(1)
    widen(wide_f)
    for half in (1, 0):
        first_relay(half)

    def convolved(wide, weight, target):
        value = dot(wide[0:512, :], weight(0))
        value = value + dot(wide[64:576, :], weight(1))
        value = value + dot(wide[128:640, :], weight(2))
        value = value.reshape(8, 8, 8, C) * mask_v[...]
        target[...] = value.astype(BF16)

    loads[3].wait()
    convolved(wide_f, lambda a: kern_v[9 * a : 9 * a + 9].reshape(9 * C, C), out_v)
    out_copy = pltpu.make_async_copy(out_v, out_ref, out_sem.at[0])
    out_copy.start()

    for half in (1, 0):
        add_first(half)
        seconds[half] = second_copies(half)
        for copy in seconds[half]:
            copy.start()
    def z_part(ref, owner):
        return ref.at[pl.ds(owner * per_owner, per_owner)]

    def near_device(d):
        return at(x, y, z_group * near + (z_near + d) % near, core)

    def z_copy(d):
        return pltpu.make_async_remote_copy(
            src_ref=z_part(tiles, (z_near + d) % near),
            dst_ref=z_part(z_buf, d - 1),
            send_sem=z_send,
            recv_sem=z_recv,
            device_id=near_device(d),
            device_id_type=MESH,
        )

    def zs_copy(d):
        return pltpu.make_async_remote_copy(
            src_ref=z_sum.at[z_group],
            dst_ref=z_sum.at[z_group],
            send_sem=zs_send,
            recv_sem=zs_recv,
            device_id=at(x, y, (z_group + d) % groups * near + z_near, core),
            device_id_type=MESH,
        )

    def zg_copy(d):
        return pltpu.make_async_remote_copy(
            src_ref=z_part(z_all, z_near),
            dst_ref=z_part(z_all, z_near),
            send_sem=zg_send,
            recv_sem=zg_recv,
            device_id=near_device(d),
            device_id_type=MESH,
        )

    def whole(ref, sends, receives):
        return pltpu.make_async_remote_copy(
            src_ref=ref,
            dst_ref=ref,
            send_sem=sends,
            recv_sem=receives,
            device_id=sibling,
            device_id_type=MESH,
        )

    z_whole = whole(z_buf, z_send, z_recv)
    zs_whole = whole(z_sum.at[0 : groups - 1], zs_send, zs_recv) if groups > 1 else None
    zg_whole = whole(z_buf, zg_send, zg_recv)

    hear(2)
    for half in (1, 0):
        tiles[8 * half + 7] = jnp.zeros((rows, C), F32)
        add_second(half, seconds[half])
        for d in range(1, near):

            @pl.when((z_near + d) % near * 2 // near == half)
            def _():
                z_copy(d).start()

    def flip(s, carry):
        start = pl.multiple_of(s * C, C)
        kern_t[pl.ds(start, C), :] = jnp.transpose(kern_v[26 - s].astype(F32)).astype(BF16)
        return carry

    lax.fori_loop(0, 27, flip, 0)

    z_whole.wait_recv()
    value = tiles[pl.ds(z_near * per_owner, per_owner)]
    for d in range(1, near):
        value = value + z_buf[(d - 1) * per_owner : d * per_owner]
    z_sum[z_group] = value
    for d in range(1, groups):
        zs_copy(d).start()

    for copy in halo_g + halo_f + [pair[0], pair[1]]:
        copy.wait_send()
    for half in (1, 0):
        for copy in list(firsts[half].values()) + seconds[half]:
            copy.wait_send()
    z_whole.wait_send()

    convolved(wide_g, lambda a: kern_t[a * 9 * C : (a + 1) * 9 * C, :], fgrad_v)
    fgrad_copy = pltpu.make_async_copy(fgrad_v, fgrad_ref, out_sem.at[1])
    fgrad_copy.start()

    if groups > 1:
        zs_whole.wait_recv()
    value = z_sum[0]
    for i in range(1, groups):
        value = value + z_sum[i]
    z_all[pl.ds(z_near * per_owner, per_owner)] = value * scale
    for d in range(1, near):
        zg_copy(d).start()

    def gathered(half, offsets, row, size):
        return total.at[pl.ds(offsets + 7 * half, 7), pl.ds(pl.multiple_of(row, 8), size)]

    def z_half(half):
        return z_all.at[8 * half : 8 * half + 7]

    def second_back(half, d, row):
        return pltpu.make_async_remote_copy(
            src_ref=z_half(half),
            dst_ref=gathered(half, mine, row, rows),
            send_sem=sg_send.at[half, d - 1],
            recv_sem=sg_recv.at[half, d - 1],
            device_id=at(*second_peer(half, d), z, core),
            device_id_type=MESH,
        )

    def first_back(half, slot, target):
        sign = 1 if slot % 2 == 0 else -1
        upper = {0: 0, 1: 1, 2: 1, 3: 0, 4: 0, 5: 1}[slot]
        size = first_block[half] // 2
        row = target * first_block[half] + upper * size
        return pltpu.make_async_remote_copy(
            src_ref=gathered(half, mine, row, size),
            dst_ref=gathered(half, mine, row, size),
            send_sem=fg_send.at[half, slot],
            recv_sem=fg_recv.at[half, slot],
            device_id=first_device(half, sign),
            device_id_type=MESH,
        )

    def source_of(half, slot):
        sign = 1 if slot % 2 == 0 else -1
        return first_index(half, -sign if slot < 4 else 2)

    def pair_back(half, slot, offsets):
        size = first_block[half]
        if slot == 6:
            row = first_index(half, 0) * size
        else:
            size = size // 2
            upper = {0: 0, 1: 1, 2: 1, 3: 0, 4: 0, 5: 1}[slot]
            row = source_of(half, slot) * 2 * size + upper * size
        return pltpu.make_async_remote_copy(
            src_ref=gathered(half, offsets, row, size),
            dst_ref=gathered(half, offsets, row, size),
            send_sem=pg_send.at[half, slot],
            recv_sem=pg_recv.at[half, slot],
            device_id=sibling,
            device_id_type=MESH,
        )

    sent = []
    keeps = {}
    zg_whole.wait_recv()
    for half in (1, 0):
        for d in range(1, second_size[half]):
            copy = second_back(half, d, second_place[half])
            copy.start()
            sent.append(copy)
        keeps[half] = pltpu.make_async_copy(
            z_half(half),
            gathered(half, mine, second_place[half], rows),
            own_sem.at[half],
        )
        keeps[half].start()
    for half in (1, 0):
        n = second_size[half]
        for d in range(1, n):
            from_index = ((y if half == 0 else x) - d + n) % n
            second_back(half, d, first_place[half] + from_index * rows).wait_recv()
        keeps[half].wait()
        for slot in (0, 1, 2, 3) if first_size[half] > 2 else (0, 1):
            copy = first_back(half, slot, first_index(half, 0))
            copy.start()
            sent.append(copy)
        copy = pair_back(half, 6, mine)
        copy.start()
        sent.append(copy)

    forwarded = []
    for slot in range(6):
        for half in (1, 0):
            if first_size[half] > 2 or slot < 2:
                first_back(half, slot, source_of(half, slot)).wait_recv()
                if first_size[half] > 2 and slot < 2:
                    copy = first_back(half, slot + 4, source_of(half, slot))
                    copy.start()
                    sent.append(copy)
                copy = pair_back(half, slot, mine)
                copy.start()
                forwarded.append(copy)
    zg_whole.wait_send()
    if groups > 1:
        zs_whole.wait_send()
    for copy in sent:
        copy.wait_send()
    out_copy.wait()
    fgrad_copy.wait()
    for slot in (6, 0, 1, 2, 3, 4, 5):
        for half in (1, 0):
            if first_size[half] > 2 or slot in (6, 0, 1):
                pair_back(half, slot, theirs).wait_recv()
    for copy in forwarded:
        copy.wait_send()


def shards(chips, features, occupancy, weights, cotangent):
    nx, ny, nz = chips
    voxels = 512 * nx * ny * nz * 2
    scale = 1.0 / math.sqrt(voxels)
    rows = C // (nx * ny)
    near = min(4, nz)
    per_owner = 16 // near
    most = max(nx, ny)
    dma = pltpu.SemaphoreType.DMA
    results = pl.pallas_call(
        functools.partial(kernel, chips, scale),
        out_shape=(
            jax.ShapeDtypeStruct((8, 8, 8, C), BF16),
            jax.ShapeDtypeStruct((8, 8, 8, C), BF16),
            jax.ShapeDtypeStruct((28, C, C), F32),
        ),
        in_specs=[pl.BlockSpec(memory_space=pltpu.HBM)] * 4,
        out_specs=[pl.BlockSpec(memory_space=pl.ANY)] * 3,
        scratch_shapes=[
            pltpu.VMEM((8, 8, 8, C), BF16),
            pltpu.VMEM((8, 8, 8, C), BF16),
            pltpu.VMEM((8, 8, 8), jnp.int32),
            pltpu.VMEM((27, C, C), BF16),
            pltpu.VMEM((27 * C, C), BF16),
            pltpu.VMEM((8, 8, 8, C), F32),
            pltpu.VMEM((C, 512), BF16),
            pltpu.VMEM((10, 10, 8, C), F32),
            pltpu.VMEM((640, 9 * C), BF16),
            pltpu.VMEM((640, 9 * C), BF16),
            pltpu.VMEM((2, 4, 64, C), BF16),
            pltpu.VMEM((2, 4, 16, C), BF16),
            pltpu.VMEM((2, 4, 64, C), BF16),
            pltpu.VMEM((2, 4, 16, C), BF16),
            pltpu.VMEM((28, C, C), F32),
            pltpu.VMEM((14, C, C), F32),
            pltpu.VMEM((2, 6, 7, C // (2 * min(nx, ny)), C), F32),
            pltpu.VMEM((2, most - 1, 7, rows, C), F32),
            pltpu.VMEM((16, rows, C), F32),
            pltpu.VMEM(((near - 1) * per_owner, rows, C), F32),
            pltpu.VMEM((nz // near, per_owner, rows, C), F32),
            pltpu.VMEM((16, rows, C), F32),
            pltpu.VMEM((8, 8, 8, C), BF16),
            pltpu.VMEM((8, 8, 8, C), BF16),
            dma((4,)),
            dma((2,)),
            dma((2,)),
            pltpu.SemaphoreType.REGULAR((3,)),
            dma((2, 8)),
            dma((2, 8)),
            dma((2,)),
            dma((2,)),
            dma((2, 6)),
            dma((2, 6)),
            dma((2, most - 1)),
            dma((2, most - 1)),
            dma,
            dma,
            dma,
            dma,
            dma,
            dma,
            dma((2, most - 1)),
            dma((2, most - 1)),
            dma((2, 6)),
            dma((2, 6)),
            dma((2, 7)),
            dma((2, 7)),
        ],
        compiler_params=pltpu.CompilerParams(
            collective_id=0, has_side_effects=True, vmem_limit_bytes=48 * 1024 * 1024
        ),
        cost_estimate=pl.CostEstimate(
            flops=3 * 2 * 512 * 27 * C * C, bytes_accessed=4_000_000, transcendentals=0
        ),
    )(*(pltpu.with_memory_space_constraint(a, pltpu.HBM) for a in (features, occupancy, weights, cotangent)))
    return results[0], results[1], results[2][:27]


def solution(mesh, chips=CHIPS):
    in_specs = (
        P("space", "tile", None, None),
        P("space", "tile", None),
        P(),
        P("space", "tile", None, None),
    )
    out_specs = (P("space", "tile", None, None), P("space", "tile", None, None), P())
    return jax.shard_map(
        functools.partial(shards, chips),
        mesh=mesh,
        in_specs=in_specs,
        out_specs=out_specs,
        check_vma=False,
    )
```

```python
import functools
import math

import jax
import jax.numpy as jnp
from jax import lax
from jax.experimental import pallas as pl
from jax.experimental.pallas import tpu as pltpu
from jax.sharding import PartitionSpec as P

MESH = pl.DeviceIdType.MESH
CHIPS = (4, 4, 16)
C = 128
DIRS = ((1, 0), (-1, 0), (0, 1), (0, -1), (1, 1), (1, -1), (-1, 1), (-1, -1))
F32 = jnp.float32
BF16 = jnp.bfloat16


def dot(a, b):
    return jnp.dot(a, b, preferred_element_type=F32)


def kernel(
    chips,
    scale,
    feat_hbm,
    occ_hbm,
    kern_hbm,
    cot_hbm,
    out_ref,
    fgrad_ref,
    total,
    feat_v,
    cot_v,
    occ_v,
    kern_v,
    kern_t,
    mask_v,
    features_t,
    padded,
    wide_f,
    wide_g,
    send_face,
    send_corner,
    recv_face,
    recv_corner,
    part,
    pair_buf,
    first_buf,
    second_buf,
    tiles,
    z_buf,
    z_sum,
    z_all,
    out_v,
    fgrad_v,
    in_sem,
    out_sem,
    own_sem,
    known,
    halo_send,
    halo_recv,
    pair_send,
    pair_recv,
    first_send,
    first_recv,
    second_send,
    second_recv,
    z_send,
    z_recv,
    zs_send,
    zs_recv,
    zg_send,
    zg_recv,
    sg_send,
    sg_recv,
    fg_send,
    fg_recv,
    pg_send,
    pg_recv,
):
    nx, ny, nz = chips
    n_space, n_tile = nx * nz, ny * 2
    space, tile = lax.axis_index("space"), lax.axis_index("tile")
    x, z = space // nz, space % nz
    y, core = tile // 2, tile % 2
    block = C // nx
    block_y = C // ny
    rows = C // (nx * ny)
    near = min(4, nz)
    groups = nz // near
    per_owner = 16 // near
    z_group, z_near = z // near, z % near

    def at(px, py, pz, pc):
        return {"space": px * nz + pz, "tile": py * 2 + pc}

    def x_peer(d):
        return (x + d) % nx

    def y_peer(d):
        return (y + d) % ny

    def z_peer(d):
        return (z + d) % nz

    def halo_peer(i):
        ds, dt = DIRS[i]
        return {
            "space": (space + ds + n_space) % n_space,
            "tile": (tile + dt + n_tile) % n_tile,
        }

    sibling = at(x, y, z, 1 - core)

    loads = [
        pltpu.make_async_copy(src, dst, in_sem.at[i])
        for i, (src, dst) in enumerate(
            ((occ_hbm, occ_v), (cot_hbm, cot_v), (feat_hbm, feat_v), (kern_hbm, kern_v))
        )
    ]
    for load in loads:
        load.start()

    barrier = pltpu.get_barrier_semaphore()

    def greet(device):
        pl.semaphore_signal(barrier, inc=1, device_id=device, device_id_type=MESH)

    for i in range(8):
        greet(halo_peer(i))
    greet(sibling)
    for d in range(1, nx):
        greet(at(x_peer(d), y, z, core))
    for d in range(1, ny):
        greet(at(x, y_peer(d), z, core))

    for d in (1, -1):
        greet(at(x, y, z_peer(d + nz), core))

    def tell(step):
        d = 2**step
        if d < nz // 2:
            for side in (d, -d):
                pl.semaphore_signal(
                    known.at[step],
                    inc=1,
                    device_id=at(x, y, z_peer(side + nz), core),
                    device_id_type=MESH,
                )

    def hear(step):
        if 2**step < nz // 2:
            pl.semaphore_wait(known.at[step], 2)

    loads[0].wait()
    cells = occ_v[...].reshape(64, 8).astype(F32).astype(BF16)
    pick = lax.broadcasted_iota(jnp.int32, (512, 64), 0) // 8
    pick = (pick == lax.broadcasted_iota(jnp.int32, (512, 64), 1)).astype(F32)
    spread = dot(pick.astype(BF16), cells)
    own = lax.broadcasted_iota(jnp.int32, (512, 8), 0) % 8
    own = own == lax.broadcasted_iota(jnp.int32, (512, 8), 1)
    column = jnp.sum(jnp.where(own, spread, 0.0), axis=1, keepdims=True)
    mask_v[...] = jnp.broadcast_to(column, (512, C)).reshape(8, 8, 8, C)

    def masked_of(source):
        return source[...].astype(F32) * mask_v[...]

    def fill_halo(which, value):
        edge_x = {1: value[7], -1: value[0]}
        edge_y = {1: value[:, 7], -1: value[:, 0]}
        for i in range(2):
            send_face[which, i] = edge_x[DIRS[i][0]].reshape(64, C).astype(BF16)
        for i in range(2, 4):
            send_face[which, i] = edge_y[DIRS[i][1]].reshape(64, C).astype(BF16)
        for i in range(4, 8):
            corner = edge_x[DIRS[i][0]][7 if DIRS[i][1] == 1 else 0]
            send_corner[which, i - 4] = jnp.concatenate([corner, corner], axis=0).astype(BF16)

    def halo_copies(which):
        copies = []
        for i in range(8):
            if i < 4:
                source, target = send_face.at[which, i], recv_face.at[which, i]
            else:
                source, target = send_corner.at[which, i - 4], recv_corner.at[which, i - 4]
            copies.append(
                pltpu.make_async_remote_copy(
                    src_ref=source,
                    dst_ref=target,
                    send_sem=halo_send.at[which, i],
                    recv_sem=halo_recv.at[which, i],
                    device_id=halo_peer(i),
                    device_id_type=MESH,
                )
            )
        return copies

    inside = {
        (0, 1): (space > 0).astype(F32),
        (0, -1): (space < n_space - 1).astype(F32),
        (1, 1): (tile > 0).astype(F32),
        (1, -1): (tile < n_tile - 1).astype(F32),
    }

    def place_halo(which):
        for i in range(8):
            ds, dt = DIRS[i]
            valid = 1.0
            if ds:
                valid = valid * inside[0, ds]
            if dt:
                valid = valid * inside[1, dt]
            row, col = {1: 0, -1: 9}.get(ds), {1: 0, -1: 9}.get(dt)
            if i < 4:
                value = recv_face[which, i].astype(F32).reshape(8, 8, C) * valid
            else:
                value = recv_corner[which, i - 4].astype(F32)[0:8] * valid
            if ds == 0:
                padded[1:9, col] = value
            elif dt == 0:
                padded[row, 1:9] = value
            else:
                padded[row, col] = value

    z_place = lax.broadcasted_iota(jnp.int32, (10, 8, C), 1)

    def widen(target):
        def slab(i, carry):
            value = padded[i]
            before = jnp.where(z_place == 0, 0.0, pltpu.roll(value, 1, 1))
            after = jnp.where(z_place == 7, 0.0, pltpu.roll(value, 7, 1))
            start = pl.multiple_of(i * 64, 64)
            for sy in range(3):
                for sz, shifted in enumerate((before, value, after)):
                    column = (3 * sy + sz) * C
                    target[pl.ds(start, 64), column : column + C] = (
                        shifted[sy : sy + 8].reshape(64, C).astype(BF16)
                    )
            return carry

        lax.fori_loop(0, 10, slab, 0)

    loads[1].wait()
    masked_grad = masked_of(cot_v)
    padded[1:9, 1:9] = masked_grad
    fill_halo(0, masked_grad)
    pl.semaphore_wait(barrier, 8 + 1 + (nx - 1) + (ny - 1) + 2)
    halo_g = halo_copies(0)
    for copy in halo_g:
        copy.start()
    tell(0)
    loads[2].wait()
    masked = masked_of(feat_v)
    fill_halo(1, masked)
    halo_f = halo_copies(1)
    for copy in halo_f:
        copy.start()
    hear(0)
    tell(1)
    features_t[...] = jnp.transpose(masked.reshape(512, C)).astype(BF16)

    for copy in halo_g:
        copy.wait_recv()
    place_halo(0)
    widen(wide_g)

    def terms(sx, first, last):
        for q in range(first, last, 2):
            end = min(q + 2, last)
            result = dot(features_t[...], wide_g[sx * 64 : sx * 64 + 512, q * C : end * C])
            for j in range(q, end):
                part[26 - (9 * sx + j)] = result[:, (j - q) * C : (j - q + 1) * C]

    mine = core * 14
    theirs = (1 - core) * 14

    def pair_copy(half):
        return pltpu.make_async_remote_copy(
            src_ref=part.at[pl.ds(theirs + 7 * half, 7)],
            dst_ref=pair_buf.at[pl.ds(7 * half, 7)],
            send_sem=pair_send.at[half],
            recv_sem=pair_recv.at[half],
            device_id=sibling,
            device_id_type=MESH,
        )

    hear(1)
    tell(2)

    def offset_terms(first):
        for sx in range(3):
            inside_sx = [26 - o - 9 * sx for o in range(first, min(first + 7, 27)) if (26 - o) // 9 == sx]
            if inside_sx:
                terms(sx, min(inside_sx), max(inside_sx) + 1)

    def for_core(first, second):
        @pl.when(core == 0)
        def _():
            offset_terms(first)

        @pl.when(core == 1)
        def _():
            offset_terms(second)

    part[27] = jnp.zeros((C, C), F32)
    pair = {}
    for half in (1, 0):
        for_core(14 + 7 * half, 7 * half)
        pair[half] = pair_copy(half)
        pair[half].start()

    first_size = {0: nx, 1: ny}
    second_size = {0: ny, 1: nx}
    first_block = {0: block, 1: block_y}
    first_place = {0: x * block, 1: y * block_y}
    second_place = {0: x * block + y * rows, 1: y * block_y + x * rows}

    def first_index(half, d):
        return x_peer(d + nx) if half == 0 else y_peer(d + ny)

    def first_device(half, d):
        if half == 0:
            return at(x_peer(d + nx), y, z, core)
        return at(x, y_peer(d + ny), z, core)

    def second_peer(half, d):
        return (x, y_peer(d)) if half == 0 else (x_peer(d), y)

    def first_copy(half, slot):
        sign = 1 if slot % 2 == 0 else -1
        upper = {0: 0, 1: 1, 2: 1, 3: 0, 4: 0, 5: 1}[slot]
        target = first_index(half, 2 if slot < 2 else sign)
        size = first_block[half] // 2
        start = pl.multiple_of(target * first_block[half] + upper * size, 8)
        return pltpu.make_async_remote_copy(
            src_ref=part.at[pl.ds(mine + 7 * half, 7), pl.ds(start, size)],
            dst_ref=first_buf.at[half, slot, :, 0:size],
            send_sem=first_send.at[half, slot],
            recv_sem=first_recv.at[half, slot],
            device_id=first_device(half, sign),
            device_id_type=MESH,
        )

    def first_start(half):
        ring = first_size[half] > 2
        firsts[half] = {slot: first_copy(half, slot) for slot in ((0, 1, 2, 3) if ring else (2, 3))}
        for copy in firsts[half].values():
            copy.start()

    def first_relay(half):
        if first_size[half] == 2:
            return
        size = first_block[half] // 2
        for slot in (0, 1):
            firsts[half][slot].wait_recv()
            target = first_index(half, 1 if slot == 0 else -1)
            where = pl.ds(pl.multiple_of(target * first_block[half] + slot * size, 8), size)
            part[pl.ds(mine + 7 * half, 7), where] = (
                part[pl.ds(mine + 7 * half, 7), where] + first_buf[half, slot, :, 0:size]
            )
            firsts[half][slot + 4] = first_copy(half, slot + 4)
            firsts[half][slot + 4].start()

    def second_copies(half):
        copies = []
        base = first_place[half]
        for d in range(1, second_size[half]):
            px, py = second_peer(half, d)
            index = py if half == 0 else px
            start = pl.multiple_of(base + index * rows, 8)
            copies.append(
                pltpu.make_async_remote_copy(
                    src_ref=part.at[pl.ds(mine + 7 * half, 7), pl.ds(start, rows)],
                    dst_ref=second_buf.at[half, d - 1],
                    send_sem=second_send.at[half, d - 1],
                    recv_sem=second_recv.at[half, d - 1],
                    device_id=at(px, py, z, core),
                    device_id_type=MESH,
                )
            )
        return copies

    def add_pair(half):
        pair[half].wait_recv()

        def one(i, carry):
            part[mine + 7 * half + i] = part[mine + 7 * half + i] + pair_buf[7 * half + i]
            return carry

        lax.fori_loop(0, 7, one, 0)

    def add_first(half):
        size = first_block[half] // 2
        for upper, slots_of in ((0, (3, 4)), (1, (2, 5))):
            where = pl.ds(pl.multiple_of(first_place[half] + upper * size, 8), size)
            value = part[pl.ds(mine + 7 * half, 7), where]
            for slot in slots_of:
                if slot in firsts[half]:
                    firsts[half][slot].wait_recv()
                    value = value + first_buf[half, slot, :, 0:size]
            part[pl.ds(mine + 7 * half, 7), where] = value

    def add_second(half, copies):
        for copy in copies:
            copy.wait_recv()
        where = pl.ds(pl.multiple_of(second_place[half], 8), rows)
        value = part[pl.ds(mine + 7 * half, 7), where]
        for d in range(1, second_size[half]):
            value = value + second_buf[half, d - 1]
        tiles[8 * half : 8 * half + 7] = value

    firsts, seconds = {}, {}
    for half in (1, 0):
        for_core(7 * half, 14 + 7 * half)
        add_pair(half)
        first_start(half)

    padded[1:9, 1:9] = masked_of(feat_v)
    for copy in halo_f:
        copy.wait_recv()
    place_halo(1)
    for half in (1, 0):
        first_relay(half)
    widen(wide_f)

    def convolved(wide, weight, target):
        value = dot(wide[0:512, :], weight(0))
        value = value + dot(wide[64:576, :], weight(1))
        value = value + dot(wide[128:640, :], weight(2))
        value = value.reshape(8, 8, 8, C) * mask_v[...]
        target[...] = value.astype(BF16)

    def flip(s, carry):
        start = pl.multiple_of(s * C, C)
        kern_t[pl.ds(start, C), :] = jnp.transpose(kern_v[26 - s].astype(F32)).astype(BF16)
        return carry

    def flips(part_of):
        lax.fori_loop(9 * part_of, 9 * part_of + 9, flip, 0, unroll=3)

    for half in (1, 0):
        add_first(half)
        seconds[half] = second_copies(half)
        for copy in seconds[half]:
            copy.start()
    def z_part(ref, owner):
        return ref.at[pl.ds(owner * per_owner, per_owner)]

    def near_device(d):
        return at(x, y, z_group * near + (z_near + d) % near, core)

    def z_copy(d):
        return pltpu.make_async_remote_copy(
            src_ref=z_part(tiles, (z_near + d) % near),
            dst_ref=z_part(z_buf, d - 1),
            send_sem=z_send,
            recv_sem=z_recv,
            device_id=near_device(d),
            device_id_type=MESH,
        )

    def zs_copy(d):
        return pltpu.make_async_remote_copy(
            src_ref=z_sum.at[z_group],
            dst_ref=z_sum.at[z_group],
            send_sem=zs_send,
            recv_sem=zs_recv,
            device_id=at(x, y, (z_group + d) % groups * near + z_near, core),
            device_id_type=MESH,
        )

    def zg_copy(d):
        return pltpu.make_async_remote_copy(
            src_ref=z_part(z_all, z_near),
            dst_ref=z_part(z_all, z_near),
            send_sem=zg_send,
            recv_sem=zg_recv,
            device_id=near_device(d),
            device_id_type=MESH,
        )

    def whole(ref, sends, receives):
        return pltpu.make_async_remote_copy(
            src_ref=ref,
            dst_ref=ref,
            send_sem=sends,
            recv_sem=receives,
            device_id=sibling,
            device_id_type=MESH,
        )

    z_whole = whole(z_buf, z_send, z_recv)
    zs_whole = whole(z_sum.at[0 : groups - 1], zs_send, zs_recv) if groups > 1 else None
    zg_whole = whole(z_buf, zg_send, zg_recv)

    hear(2)
    loads[3].wait()
    flips(0)
    for half in (1, 0):
        tiles[8 * half + 7] = jnp.zeros((rows, C), F32)
        add_second(half, seconds[half])
        for d in range(1, near):

            @pl.when((z_near + d) % near * 2 // near == half)
            def _():
                z_copy(d).start()

    flips(1)
    z_whole.wait_recv()
    value = tiles[pl.ds(z_near * per_owner, per_owner)]
    for d in range(1, near):
        value = value + z_buf[(d - 1) * per_owner : d * per_owner]
    z_sum[z_group] = value
    for d in range(1, groups):
        zs_copy(d).start()

    for copy in halo_g + halo_f + [pair[0], pair[1]]:
        copy.wait_send()
    for half in (1, 0):
        for copy in list(firsts[half].values()) + seconds[half]:
            copy.wait_send()
    z_whole.wait_send()

    convolved(wide_f, lambda a: kern_v[9 * a : 9 * a + 9].reshape(9 * C, C), out_v)
    out_copy = pltpu.make_async_copy(out_v, out_ref, out_sem.at[0])
    out_copy.start()

    if groups > 1:
        zs_whole.wait_recv()
    value = z_sum[0]
    for i in range(1, groups):
        value = value + z_sum[i]
    z_all[pl.ds(z_near * per_owner, per_owner)] = value * scale
    for d in range(1, near):
        zg_copy(d).start()

    def gathered(half, offsets, row, size):
        return total.at[pl.ds(offsets + 7 * half, 7), pl.ds(pl.multiple_of(row, 8), size)]

    def z_half(half):
        return z_all.at[8 * half : 8 * half + 7]

    def second_back(half, d, row):
        return pltpu.make_async_remote_copy(
            src_ref=z_half(half),
            dst_ref=gathered(half, mine, row, rows),
            send_sem=sg_send.at[half, d - 1],
            recv_sem=sg_recv.at[half, d - 1],
            device_id=at(*second_peer(half, d), z, core),
            device_id_type=MESH,
        )

    def first_back(half, slot, target):
        sign = 1 if slot % 2 == 0 else -1
        upper = {0: 0, 1: 1, 2: 1, 3: 0, 4: 0, 5: 1}[slot]
        size = first_block[half] // 2
        row = target * first_block[half] + upper * size
        return pltpu.make_async_remote_copy(
            src_ref=gathered(half, mine, row, size),
            dst_ref=gathered(half, mine, row, size),
            send_sem=fg_send.at[half, slot],
            recv_sem=fg_recv.at[half, slot],
            device_id=first_device(half, sign),
            device_id_type=MESH,
        )

    def source_of(half, slot):
        sign = 1 if slot % 2 == 0 else -1
        return first_index(half, -sign if slot < 4 else 2)

    def pair_back(half, slot, offsets):
        size = first_block[half]
        if slot == 6:
            row = first_index(half, 0) * size
        else:
            size = size // 2
            upper = {0: 0, 1: 1, 2: 1, 3: 0, 4: 0, 5: 1}[slot]
            row = source_of(half, slot) * 2 * size + upper * size
        return pltpu.make_async_remote_copy(
            src_ref=gathered(half, offsets, row, size),
            dst_ref=gathered(half, offsets, row, size),
            send_sem=pg_send.at[half, slot],
            recv_sem=pg_recv.at[half, slot],
            device_id=sibling,
            device_id_type=MESH,
        )

    sent = []
    keeps = {}
    flips(2)
    zg_whole.wait_recv()
    for half in (1, 0):
        for d in range(1, second_size[half]):
            copy = second_back(half, d, second_place[half])
            copy.start()
            sent.append(copy)
        keeps[half] = pltpu.make_async_copy(
            z_half(half),
            gathered(half, mine, second_place[half], rows),
            own_sem.at[half],
        )
        keeps[half].start()
    for half in (1, 0):
        n = second_size[half]
        for d in range(1, n):
            from_index = ((y if half == 0 else x) - d + n) % n
            second_back(half, d, first_place[half] + from_index * rows).wait_recv()
        keeps[half].wait()
        for slot in (0, 1, 2, 3) if first_size[half] > 2 else (0, 1):
            copy = first_back(half, slot, first_index(half, 0))
            copy.start()
            sent.append(copy)
        copy = pair_back(half, 6, mine)
        copy.start()
        sent.append(copy)

    forwarded = []
    for slot in range(6):
        if slot == 2:
            convolved(wide_g, lambda a: kern_t[a * 9 * C : (a + 1) * 9 * C, :], fgrad_v)
            fgrad_copy = pltpu.make_async_copy(fgrad_v, fgrad_ref, out_sem.at[1])
            fgrad_copy.start()

        for half in (1, 0):
            if first_size[half] > 2 or slot < 2:
                first_back(half, slot, source_of(half, slot)).wait_recv()
                if first_size[half] > 2 and slot < 2:
                    copy = first_back(half, slot + 4, source_of(half, slot))
                    copy.start()
                    sent.append(copy)
                copy = pair_back(half, slot, mine)
                copy.start()
                forwarded.append(copy)
    zg_whole.wait_send()
    if groups > 1:
        zs_whole.wait_send()
    for copy in sent:
        copy.wait_send()
    out_copy.wait()
    fgrad_copy.wait()
    for slot in (6, 0, 1, 2, 3, 4, 5):
        for half in (1, 0):
            if first_size[half] > 2 or slot in (6, 0, 1):
                pair_back(half, slot, theirs).wait_recv()
    for copy in forwarded:
        copy.wait_send()


def shards(chips, features, occupancy, weights, cotangent):
    nx, ny, nz = chips
    voxels = 512 * nx * ny * nz * 2
    scale = 1.0 / math.sqrt(voxels)
    rows = C // (nx * ny)
    near = min(4, nz)
    per_owner = 16 // near
    most = max(nx, ny)
    dma = pltpu.SemaphoreType.DMA
    results = pl.pallas_call(
        functools.partial(kernel, chips, scale),
        out_shape=(
            jax.ShapeDtypeStruct((8, 8, 8, C), BF16),
            jax.ShapeDtypeStruct((8, 8, 8, C), BF16),
            jax.ShapeDtypeStruct((28, C, C), F32),
        ),
        in_specs=[pl.BlockSpec(memory_space=pltpu.HBM)] * 4,
        out_specs=[pl.BlockSpec(memory_space=pl.ANY)] * 3,
        scratch_shapes=[
            pltpu.VMEM((8, 8, 8, C), BF16),
            pltpu.VMEM((8, 8, 8, C), BF16),
            pltpu.VMEM((8, 8, 8), jnp.int32),
            pltpu.VMEM((27, C, C), BF16),
            pltpu.VMEM((27 * C, C), BF16),
            pltpu.VMEM((8, 8, 8, C), F32),
            pltpu.VMEM((C, 512), BF16),
            pltpu.VMEM((10, 10, 8, C), F32),
            pltpu.VMEM((640, 9 * C), BF16),
            pltpu.VMEM((640, 9 * C), BF16),
            pltpu.VMEM((2, 4, 64, C), BF16),
            pltpu.VMEM((2, 4, 16, C), BF16),
            pltpu.VMEM((2, 4, 64, C), BF16),
            pltpu.VMEM((2, 4, 16, C), BF16),
            pltpu.VMEM((28, C, C), F32),
            pltpu.VMEM((14, C, C), F32),
            pltpu.VMEM((2, 6, 7, C // (2 * min(nx, ny)), C), F32),
            pltpu.VMEM((2, most - 1, 7, rows, C), F32),
            pltpu.VMEM((16, rows, C), F32),
            pltpu.VMEM(((near - 1) * per_owner, rows, C), F32),
            pltpu.VMEM((nz // near, per_owner, rows, C), F32),
            pltpu.VMEM((16, rows, C), F32),
            pltpu.VMEM((8, 8, 8, C), BF16),
            pltpu.VMEM((8, 8, 8, C), BF16),
            dma((4,)),
            dma((2,)),
            dma((2,)),
            pltpu.SemaphoreType.REGULAR((3,)),
            dma((2, 8)),
            dma((2, 8)),
            dma((2,)),
            dma((2,)),
            dma((2, 6)),
            dma((2, 6)),
            dma((2, most - 1)),
            dma((2, most - 1)),
            dma,
            dma,
            dma,
            dma,
            dma,
            dma,
            dma((2, most - 1)),
            dma((2, most - 1)),
            dma((2, 6)),
            dma((2, 6)),
            dma((2, 7)),
            dma((2, 7)),
        ],
        compiler_params=pltpu.CompilerParams(
            collective_id=0, has_side_effects=True, vmem_limit_bytes=48 * 1024 * 1024
        ),
        cost_estimate=pl.CostEstimate(
            flops=3 * 2 * 512 * 27 * C * C, bytes_accessed=4_000_000, transcendentals=0
        ),
    )(*(pltpu.with_memory_space_constraint(a, pltpu.HBM) for a in (features, occupancy, weights, cotangent)))
    return results[0], results[1], results[2][:27]


def solution(mesh, chips=CHIPS):
    in_specs = (
        P("space", "tile", None, None),
        P("space", "tile", None),
        P(),
        P("space", "tile", None, None),
    )
    out_specs = (P("space", "tile", None, None), P("space", "tile", None, None), P())
    return jax.shard_map(
        functools.partial(shards, chips),
        mesh=mesh,
        in_specs=in_specs,
        out_specs=out_specs,
        check_vma=False,
    )
```

```python
import functools
import math

import jax
import jax.numpy as jnp
from jax import lax
from jax.experimental import pallas as pl
from jax.experimental.pallas import tpu as pltpu
from jax.sharding import PartitionSpec as P

MESH = pl.DeviceIdType.MESH
CHIPS = (4, 4, 16)
C = 128
DIRS = ((1, 0), (-1, 0), (0, 1), (0, -1), (1, 1), (1, -1), (-1, 1), (-1, -1))
F32 = jnp.float32
BF16 = jnp.bfloat16


def dot(a, b):
    return jnp.dot(a, b, preferred_element_type=F32)


def kernel(
    chips,
    scale,
    feat_hbm,
    occ_hbm,
    kern_hbm,
    cot_hbm,
    out_ref,
    fgrad_ref,
    total,
    feat_v,
    cot_v,
    occ_v,
    kern_v,
    kern_t,
    mask_v,
    features_t,
    padded,
    wide_f,
    wide_g,
    send_face,
    send_corner,
    recv_face,
    recv_corner,
    part,
    pair_buf,
    first_buf,
    second_buf,
    tiles,
    z_buf,
    z_sum,
    z_all,
    out_v,
    fgrad_v,
    in_sem,
    out_sem,
    own_sem,
    known,
    halo_send,
    halo_recv,
    pair_send,
    pair_recv,
    first_send,
    first_recv,
    second_send,
    second_recv,
    z_send,
    z_recv,
    zs_send,
    zs_recv,
    zg_send,
    zg_recv,
    sg_send,
    sg_recv,
    fg_send,
    fg_recv,
    pg_send,
    pg_recv,
):
    nx, ny, nz = chips
    n_space, n_tile = nx * nz, ny * 2
    space, tile = lax.axis_index("space"), lax.axis_index("tile")
    x, z = space // nz, space % nz
    y, core = tile // 2, tile % 2
    block = C // nx
    block_y = C // ny
    rows = C // (nx * ny)
    near = min(4, nz)
    groups = nz // near
    per_owner = 16 // near
    z_group, z_near = z // near, z % near

    def at(px, py, pz, pc):
        return {"space": px * nz + pz, "tile": py * 2 + pc}

    def x_peer(d):
        return (x + d) % nx

    def y_peer(d):
        return (y + d) % ny

    def z_peer(d):
        return (z + d) % nz

    def halo_peer(i):
        ds, dt = DIRS[i]
        return {
            "space": (space + ds + n_space) % n_space,
            "tile": (tile + dt + n_tile) % n_tile,
        }

    sibling = at(x, y, z, 1 - core)

    loads = [
        pltpu.make_async_copy(src, dst, in_sem.at[i])
        for i, (src, dst) in enumerate(
            ((occ_hbm, occ_v), (cot_hbm, cot_v), (feat_hbm, feat_v), (kern_hbm, kern_v))
        )
    ]
    for load in loads:
        load.start()

    barrier = pltpu.get_barrier_semaphore()

    def greet(device):
        pl.semaphore_signal(barrier, inc=1, device_id=device, device_id_type=MESH)

    for i in range(8):
        greet(halo_peer(i))
    greet(sibling)
    for d in range(1, nx):
        greet(at(x_peer(d), y, z, core))
    for d in range(1, ny):
        greet(at(x, y_peer(d), z, core))

    for d in (1, -1):
        greet(at(x, y, z_peer(d + nz), core))

    def tell(step):
        d = 2**step
        if d < nz // 2:
            for side in (d, -d):
                pl.semaphore_signal(
                    known.at[step],
                    inc=1,
                    device_id=at(x, y, z_peer(side + nz), core),
                    device_id_type=MESH,
                )

    def hear(step):
        if 2**step < nz // 2:
            pl.semaphore_wait(known.at[step], 2)

    loads[0].wait()
    cells = occ_v[...].reshape(64, 8).astype(F32).astype(BF16)
    pick = lax.broadcasted_iota(jnp.int32, (512, 64), 0) // 8
    pick = (pick == lax.broadcasted_iota(jnp.int32, (512, 64), 1)).astype(F32)
    spread = dot(pick.astype(BF16), cells)
    own = lax.broadcasted_iota(jnp.int32, (512, 8), 0) % 8
    own = own == lax.broadcasted_iota(jnp.int32, (512, 8), 1)
    column = jnp.sum(jnp.where(own, spread, 0.0), axis=1, keepdims=True)
    mask_v[...] = jnp.broadcast_to(column, (512, C)).reshape(8, 8, 8, C)

    def masked_of(source):
        return source[...].astype(F32) * mask_v[...]

    def fill_halo(which, value):
        edge_x = {1: value[7], -1: value[0]}
        edge_y = {1: value[:, 7], -1: value[:, 0]}
        for i in range(2):
            send_face[which, i] = edge_x[DIRS[i][0]].reshape(64, C).astype(BF16)
        for i in range(2, 4):
            send_face[which, i] = edge_y[DIRS[i][1]].reshape(64, C).astype(BF16)
        for i in range(4, 8):
            corner = edge_x[DIRS[i][0]][7 if DIRS[i][1] == 1 else 0]
            send_corner[which, i - 4] = jnp.concatenate([corner, corner], axis=0).astype(BF16)

    def halo_copies(which):
        copies = []
        for i in range(8):
            if i < 4:
                source, target = send_face.at[which, i], recv_face.at[which, i]
            else:
                source, target = send_corner.at[which, i - 4], recv_corner.at[which, i - 4]
            copies.append(
                pltpu.make_async_remote_copy(
                    src_ref=source,
                    dst_ref=target,
                    send_sem=halo_send.at[which, i],
                    recv_sem=halo_recv.at[which, i],
                    device_id=halo_peer(i),
                    device_id_type=MESH,
                )
            )
        return copies

    inside = {
        (0, 1): (space > 0).astype(F32),
        (0, -1): (space < n_space - 1).astype(F32),
        (1, 1): (tile > 0).astype(F32),
        (1, -1): (tile < n_tile - 1).astype(F32),
    }

    def place_halo(which):
        for i in range(8):
            ds, dt = DIRS[i]
            valid = 1.0
            if ds:
                valid = valid * inside[0, ds]
            if dt:
                valid = valid * inside[1, dt]
            row, col = {1: 0, -1: 9}.get(ds), {1: 0, -1: 9}.get(dt)
            if i < 4:
                value = recv_face[which, i].astype(F32).reshape(8, 8, C) * valid
            else:
                value = recv_corner[which, i - 4].astype(F32)[0:8] * valid
            if ds == 0:
                padded[1:9, col] = value
            elif dt == 0:
                padded[row, 1:9] = value
            else:
                padded[row, col] = value

    z_place = lax.broadcasted_iota(jnp.int32, (10, 8, C), 1)

    def widen(target):
        def slab(i, carry):
            value = padded[i]
            before = jnp.where(z_place == 0, 0.0, pltpu.roll(value, 1, 1))
            after = jnp.where(z_place == 7, 0.0, pltpu.roll(value, 7, 1))
            start = pl.multiple_of(i * 64, 64)
            for sy in range(3):
                for sz, shifted in enumerate((before, value, after)):
                    column = (3 * sy + sz) * C
                    target[pl.ds(start, 64), column : column + C] = (
                        shifted[sy : sy + 8].reshape(64, C).astype(BF16)
                    )
            return carry

        lax.fori_loop(0, 10, slab, 0)

    loads[1].wait()
    masked_grad = masked_of(cot_v)
    padded[1:9, 1:9] = masked_grad
    fill_halo(0, masked_grad)
    pl.semaphore_wait(barrier, 8 + 1 + (nx - 1) + (ny - 1) + 2)
    halo_g = halo_copies(0)
    for copy in halo_g:
        copy.start()
    tell(0)
    loads[2].wait()
    masked = masked_of(feat_v)
    fill_halo(1, masked)
    halo_f = halo_copies(1)
    for copy in halo_f:
        copy.start()
    hear(0)
    tell(1)
    features_t[...] = jnp.transpose(masked.reshape(512, C)).astype(BF16)

    for copy in halo_g:
        copy.wait_recv()
    place_halo(0)
    widen(wide_g)

    def terms(sx, first, last):
        for q in range(first, last, 2):
            end = min(q + 2, last)
            result = dot(features_t[...], wide_g[sx * 64 : sx * 64 + 512, q * C : end * C])
            for j in range(q, end):
                part[26 - (9 * sx + j)] = result[:, (j - q) * C : (j - q + 1) * C]

    mine = core * 14
    theirs = (1 - core) * 14

    def pair_copy(half):
        return pltpu.make_async_remote_copy(
            src_ref=part.at[pl.ds(theirs + 7 * half, 7)],
            dst_ref=pair_buf.at[pl.ds(7 * half, 7)],
            send_sem=pair_send.at[half],
            recv_sem=pair_recv.at[half],
            device_id=sibling,
            device_id_type=MESH,
        )

    hear(1)
    tell(2)

    def offset_terms(first):
        for sx in range(3):
            inside_sx = [26 - o - 9 * sx for o in range(first, min(first + 7, 27)) if (26 - o) // 9 == sx]
            if inside_sx:
                terms(sx, min(inside_sx), max(inside_sx) + 1)

    def for_core(first, second):
        @pl.when(core == 0)
        def _():
            offset_terms(first)

        @pl.when(core == 1)
        def _():
            offset_terms(second)

    part[27] = jnp.zeros((C, C), F32)
    pair = {}
    for half in (1, 0):
        for_core(14 + 7 * half, 7 * half)
        pair[half] = pair_copy(half)
        pair[half].start()

    first_size = {0: nx, 1: ny}
    second_size = {0: ny, 1: nx}
    first_block = {0: block, 1: block_y}
    first_place = {0: x * block, 1: y * block_y}
    second_place = {0: x * block + y * rows, 1: y * block_y + x * rows}

    def first_index(half, d):
        return x_peer(d + nx) if half == 0 else y_peer(d + ny)

    def first_device(half, d):
        if half == 0:
            return at(x_peer(d + nx), y, z, core)
        return at(x, y_peer(d + ny), z, core)

    def second_peer(half, d):
        return (x, y_peer(d)) if half == 0 else (x_peer(d), y)

    def first_start(half):
        size = first_block[half]
        for d in range(1, first_size[half]):
            start = pl.multiple_of(first_index(half, d) * size, 8)
            firsts[half, d] = pltpu.make_async_remote_copy(
                src_ref=part.at[pl.ds(mine + 7 * half, 7), pl.ds(start, size)],
                dst_ref=first_buf.at[half, d - 1, :, 0:size],
                send_sem=first_send.at[half, d - 1],
                recv_sem=first_recv.at[half, d - 1],
                device_id=first_device(half, d),
                device_id_type=MESH,
            )
            firsts[half, d].start()

    def second_copies(half):
        copies = []
        base = first_place[half]
        for d in range(1, second_size[half]):
            px, py = second_peer(half, d)
            index = py if half == 0 else px
            start = pl.multiple_of(base + index * rows, 8)
            copies.append(
                pltpu.make_async_remote_copy(
                    src_ref=part.at[pl.ds(mine + 7 * half, 7), pl.ds(start, rows)],
                    dst_ref=second_buf.at[half, d - 1],
                    send_sem=second_send.at[half, d - 1],
                    recv_sem=second_recv.at[half, d - 1],
                    device_id=at(px, py, z, core),
                    device_id_type=MESH,
                )
            )
        return copies

    def add_pair(half):
        pair[half].wait_recv()

        def one(i, carry):
            part[mine + 7 * half + i] = part[mine + 7 * half + i] + pair_buf[7 * half + i]
            return carry

        lax.fori_loop(0, 7, one, 0)

    def add_first(half):
        size = first_block[half]
        where = pl.ds(pl.multiple_of(first_place[half], 8), size)
        value = part[pl.ds(mine + 7 * half, 7), where]
        for d in range(1, first_size[half]):
            firsts[half, d].wait_recv()
            value = value + first_buf[half, d - 1, :, 0:size]
        part[pl.ds(mine + 7 * half, 7), where] = value

    def add_second(half, copies):
        for copy in copies:
            copy.wait_recv()
        where = pl.ds(pl.multiple_of(second_place[half], 8), rows)
        value = part[pl.ds(mine + 7 * half, 7), where]
        for d in range(1, second_size[half]):
            value = value + second_buf[half, d - 1]
        tiles[8 * half : 8 * half + 7] = value

    firsts, seconds = {}, {}
    for half in (1, 0):
        for_core(7 * half, 14 + 7 * half)
        add_pair(half)
        first_start(half)

    padded[1:9, 1:9] = masked_of(feat_v)
    for copy in halo_f:
        copy.wait_recv()
    place_halo(1)
    widen(wide_f)

    def convolved(wide, weight, target):
        value = dot(wide[0:512, :], weight(0))
        value = value + dot(wide[64:576, :], weight(1))
        value = value + dot(wide[128:640, :], weight(2))
        value = value.reshape(8, 8, 8, C) * mask_v[...]
        target[...] = value.astype(BF16)

    def flip(s, carry):
        start = pl.multiple_of(s * C, C)
        kern_t[pl.ds(start, C), :] = jnp.transpose(kern_v[26 - s].astype(F32)).astype(BF16)
        return carry

    def flips(part_of):
        lax.fori_loop(9 * part_of, 9 * part_of + 9, flip, 0, unroll=3)

    for half in (1, 0):
        add_first(half)
        seconds[half] = second_copies(half)
        for copy in seconds[half]:
            copy.start()
    def z_part(ref, owner):
        return ref.at[pl.ds(owner * per_owner, per_owner)]

    def near_device(d):
        return at(x, y, z_group * near + (z_near + d) % near, core)

    def z_copy(d):
        return pltpu.make_async_remote_copy(
            src_ref=z_part(tiles, (z_near + d) % near),
            dst_ref=z_part(z_buf, d - 1),
            send_sem=z_send,
            recv_sem=z_recv,
            device_id=near_device(d),
            device_id_type=MESH,
        )

    def zs_copy(d):
        return pltpu.make_async_remote_copy(
            src_ref=z_sum.at[z_group],
            dst_ref=z_sum.at[z_group],
            send_sem=zs_send,
            recv_sem=zs_recv,
            device_id=at(x, y, (z_group + d) % groups * near + z_near, core),
            device_id_type=MESH,
        )

    def zg_copy(d):
        return pltpu.make_async_remote_copy(
            src_ref=z_part(z_all, z_near),
            dst_ref=z_part(z_all, z_near),
            send_sem=zg_send,
            recv_sem=zg_recv,
            device_id=near_device(d),
            device_id_type=MESH,
        )

    def whole(ref, sends, receives):
        return pltpu.make_async_remote_copy(
            src_ref=ref,
            dst_ref=ref,
            send_sem=sends,
            recv_sem=receives,
            device_id=sibling,
            device_id_type=MESH,
        )

    z_whole = whole(z_buf, z_send, z_recv)
    zs_whole = whole(z_sum.at[0 : groups - 1], zs_send, zs_recv) if groups > 1 else None
    zg_whole = whole(z_buf, zg_send, zg_recv)

    hear(2)
    loads[3].wait()
    flips(0)
    for half in (1, 0):
        tiles[8 * half + 7] = jnp.zeros((rows, C), F32)
        add_second(half, seconds[half])
        for d in range(1, near):

            @pl.when((z_near + d) % near * 2 // near == half)
            def _():
                z_copy(d).start()

    flips(1)
    z_whole.wait_recv()
    value = tiles[pl.ds(z_near * per_owner, per_owner)]
    for d in range(1, near):
        value = value + z_buf[(d - 1) * per_owner : d * per_owner]
    z_sum[z_group] = value
    for d in range(1, groups):
        zs_copy(d).start()

    for copy in halo_g + halo_f + [pair[0], pair[1]]:
        copy.wait_send()
    for half in (1, 0):
        for copy in seconds[half]:
            copy.wait_send()
    for copy in firsts.values():
        copy.wait_send()
    z_whole.wait_send()

    convolved(wide_f, lambda a: kern_v[9 * a : 9 * a + 9].reshape(9 * C, C), out_v)
    out_copy = pltpu.make_async_copy(out_v, out_ref, out_sem.at[0])
    out_copy.start()

    if groups > 1:
        zs_whole.wait_recv()
    value = z_sum[0]
    for i in range(1, groups):
        value = value + z_sum[i]
    z_all[pl.ds(z_near * per_owner, per_owner)] = value * scale
    for d in range(1, near):
        zg_copy(d).start()

    def gathered(half, offsets, row, size):
        return total.at[pl.ds(offsets + 7 * half, 7), pl.ds(pl.multiple_of(row, 8), size)]

    def z_half(half):
        return z_all.at[8 * half : 8 * half + 7]

    def second_back(half, d, row):
        return pltpu.make_async_remote_copy(
            src_ref=z_half(half),
            dst_ref=gathered(half, mine, row, rows),
            send_sem=sg_send.at[half, d - 1],
            recv_sem=sg_recv.at[half, d - 1],
            device_id=at(*second_peer(half, d), z, core),
            device_id_type=MESH,
        )

    def first_back(half, d, index):
        size = first_block[half]
        return pltpu.make_async_remote_copy(
            src_ref=gathered(half, mine, index * size, size),
            dst_ref=gathered(half, mine, index * size, size),
            send_sem=fg_send.at[half, d - 1],
            recv_sem=fg_recv.at[half, d - 1],
            device_id=first_device(half, d),
            device_id_type=MESH,
        )

    def pair_back(half, d, offsets):
        size = first_block[half]
        row = first_index(half, -d) * size
        return pltpu.make_async_remote_copy(
            src_ref=gathered(half, offsets, row, size),
            dst_ref=gathered(half, offsets, row, size),
            send_sem=pg_send.at[half, d],
            recv_sem=pg_recv.at[half, d],
            device_id=sibling,
            device_id_type=MESH,
        )

    sent = []
    keeps = {}
    flips(2)
    zg_whole.wait_recv()
    for half in (1, 0):
        for d in range(1, second_size[half]):
            copy = second_back(half, d, second_place[half])
            copy.start()
            sent.append(copy)
        keeps[half] = pltpu.make_async_copy(
            z_half(half),
            gathered(half, mine, second_place[half], rows),
            own_sem.at[half],
        )
        keeps[half].start()
    for half in (1, 0):
        n = second_size[half]
        for d in range(1, n):
            from_index = ((y if half == 0 else x) - d + n) % n
            second_back(half, d, first_place[half] + from_index * rows).wait_recv()
        keeps[half].wait()
        for d in range(1, first_size[half]):
            copy = first_back(half, d, first_index(half, 0))
            copy.start()
            sent.append(copy)
        copy = pair_back(half, 0, mine)
        copy.start()
        sent.append(copy)

    convolved(wide_g, lambda a: kern_t[a * 9 * C : (a + 1) * 9 * C, :], fgrad_v)
    fgrad_copy = pltpu.make_async_copy(fgrad_v, fgrad_ref, out_sem.at[1])
    fgrad_copy.start()

    forwarded = []
    for d in (1, 3, 2):
        for half in (1, 0):
            if d < first_size[half]:
                first_back(half, d, first_index(half, -d)).wait_recv()
                copy = pair_back(half, d, mine)
                copy.start()
                forwarded.append(copy)
    zg_whole.wait_send()
    if groups > 1:
        zs_whole.wait_send()
    for copy in sent:
        copy.wait_send()
    out_copy.wait()
    fgrad_copy.wait()
    for d in (0, 1, 3, 2):
        for half in (1, 0):
            if d < first_size[half]:
                pair_back(half, d, theirs).wait_recv()
    for copy in forwarded:
        copy.wait_send()


def shards(chips, features, occupancy, weights, cotangent):
    nx, ny, nz = chips
    voxels = 512 * nx * ny * nz * 2
    scale = 1.0 / math.sqrt(voxels)
    rows = C // (nx * ny)
    near = min(4, nz)
    per_owner = 16 // near
    most = max(nx, ny)
    dma = pltpu.SemaphoreType.DMA
    results = pl.pallas_call(
        functools.partial(kernel, chips, scale),
        out_shape=(
            jax.ShapeDtypeStruct((8, 8, 8, C), BF16),
            jax.ShapeDtypeStruct((8, 8, 8, C), BF16),
            jax.ShapeDtypeStruct((28, C, C), F32),
        ),
        in_specs=[pl.BlockSpec(memory_space=pltpu.HBM)] * 4,
        out_specs=[pl.BlockSpec(memory_space=pl.ANY)] * 3,
        scratch_shapes=[
            pltpu.VMEM((8, 8, 8, C), BF16),
            pltpu.VMEM((8, 8, 8, C), BF16),
            pltpu.VMEM((8, 8, 8), jnp.int32),
            pltpu.VMEM((27, C, C), BF16),
            pltpu.VMEM((27 * C, C), BF16),
            pltpu.VMEM((8, 8, 8, C), F32),
            pltpu.VMEM((C, 512), BF16),
            pltpu.VMEM((10, 10, 8, C), F32),
            pltpu.VMEM((640, 9 * C), BF16),
            pltpu.VMEM((640, 9 * C), BF16),
            pltpu.VMEM((2, 4, 64, C), BF16),
            pltpu.VMEM((2, 4, 16, C), BF16),
            pltpu.VMEM((2, 4, 64, C), BF16),
            pltpu.VMEM((2, 4, 16, C), BF16),
            pltpu.VMEM((28, C, C), F32),
            pltpu.VMEM((14, C, C), F32),
            pltpu.VMEM((2, most - 1, 7, C // min(nx, ny), C), F32),
            pltpu.VMEM((2, most - 1, 7, rows, C), F32),
            pltpu.VMEM((16, rows, C), F32),
            pltpu.VMEM(((near - 1) * per_owner, rows, C), F32),
            pltpu.VMEM((nz // near, per_owner, rows, C), F32),
            pltpu.VMEM((16, rows, C), F32),
            pltpu.VMEM((8, 8, 8, C), BF16),
            pltpu.VMEM((8, 8, 8, C), BF16),
            dma((4,)),
            dma((2,)),
            dma((2,)),
            pltpu.SemaphoreType.REGULAR((3,)),
            dma((2, 8)),
            dma((2, 8)),
            dma((2,)),
            dma((2,)),
            dma((2, 6)),
            dma((2, 6)),
            dma((2, most - 1)),
            dma((2, most - 1)),
            dma,
            dma,
            dma,
            dma,
            dma,
            dma,
            dma((2, most - 1)),
            dma((2, most - 1)),
            dma((2, 6)),
            dma((2, 6)),
            dma((2, 7)),
            dma((2, 7)),
        ],
        compiler_params=pltpu.CompilerParams(
            collective_id=0, has_side_effects=True, vmem_limit_bytes=48 * 1024 * 1024
        ),
        cost_estimate=pl.CostEstimate(
            flops=3 * 2 * 512 * 27 * C * C, bytes_accessed=4_000_000, transcendentals=0
        ),
    )(*(pltpu.with_memory_space_constraint(a, pltpu.HBM) for a in (features, occupancy, weights, cotangent)))
    return results[0], results[1], results[2][:27]


def solution(mesh, chips=CHIPS):
    in_specs = (
        P("space", "tile", None, None),
        P("space", "tile", None),
        P(),
        P("space", "tile", None, None),
    )
    out_specs = (P("space", "tile", None, None), P("space", "tile", None, None), P())
    return jax.shard_map(
        functools.partial(shards, chips),
        mesh=mesh,
        in_specs=in_specs,
        out_specs=out_specs,
        check_vma=False,
    )
```

```python
import functools
import math

import jax
import jax.numpy as jnp
from jax import lax
from jax.experimental import pallas as pl
from jax.experimental.pallas import tpu as pltpu
from jax.sharding import PartitionSpec as P

MESH = pl.DeviceIdType.MESH
CHIPS = (4, 4, 16)
C = 128
DIRS = ((1, 0), (-1, 0), (0, 1), (0, -1), (1, 1), (1, -1), (-1, 1), (-1, -1))
F32 = jnp.float32
BF16 = jnp.bfloat16


def dot(a, b):
    return jnp.dot(a, b, preferred_element_type=F32)


def kernel(
    chips,
    scale,
    feat_hbm,
    occ_hbm,
    kern_hbm,
    cot_hbm,
    out_ref,
    fgrad_ref,
    total,
    feat_v,
    cot_v,
    occ_v,
    kern_v,
    kern_t,
    mask_v,
    features_t,
    padded,
    wide_f,
    wide_g,
    send_face,
    send_corner,
    recv_face,
    recv_corner,
    part,
    pair_buf,
    first_buf,
    second_buf,
    tiles,
    z_buf,
    z_sum,
    z_all,
    out_v,
    fgrad_v,
    in_sem,
    out_sem,
    own_sem,
    known,
    halo_send,
    halo_recv,
    pair_send,
    pair_recv,
    first_send,
    first_recv,
    second_send,
    second_recv,
    z_send,
    z_recv,
    zs_send,
    zs_recv,
    zg_send,
    zg_recv,
    sg_send,
    sg_recv,
    fg_send,
    fg_recv,
    pg_send,
    pg_recv,
):
    nx, ny, nz = chips
    n_space, n_tile = nx * nz, ny * 2
    space, tile = lax.axis_index("space"), lax.axis_index("tile")
    x, z = space // nz, space % nz
    y, core = tile // 2, tile % 2
    block = C // nx
    block_y = C // ny
    rows = C // (nx * ny)
    near = min(4, nz)
    groups = nz // near
    per_owner = 16 // near
    z_group, z_near = z // near, z % near

    def at(px, py, pz, pc):
        return {"space": px * nz + pz, "tile": py * 2 + pc}

    def x_peer(d):
        return (x + d) % nx

    def y_peer(d):
        return (y + d) % ny

    def z_peer(d):
        return (z + d) % nz

    def halo_peer(i):
        ds, dt = DIRS[i]
        return {
            "space": (space + ds + n_space) % n_space,
            "tile": (tile + dt + n_tile) % n_tile,
        }

    sibling = at(x, y, z, 1 - core)

    loads = [
        pltpu.make_async_copy(src, dst, in_sem.at[i])
        for i, (src, dst) in enumerate(
            ((occ_hbm, occ_v), (cot_hbm, cot_v), (feat_hbm, feat_v), (kern_hbm, kern_v))
        )
    ]
    for load in loads:
        load.start()

    barrier = pltpu.get_barrier_semaphore()

    def greet(device):
        pl.semaphore_signal(barrier, inc=1, device_id=device, device_id_type=MESH)

    for i in range(8):
        greet(halo_peer(i))
    greet(sibling)
    for d in range(1, nx):
        greet(at(x_peer(d), y, z, core))
    for d in range(1, ny):
        greet(at(x, y_peer(d), z, core))

    for d in (1, -1):
        greet(at(x, y, z_peer(d + nz), core))

    def tell(step):
        d = 2**step
        if d < nz // 2:
            for side in (d, -d):
                pl.semaphore_signal(
                    known.at[step],
                    inc=1,
                    device_id=at(x, y, z_peer(side + nz), core),
                    device_id_type=MESH,
                )

    def hear(step):
        if 2**step < nz // 2:
            pl.semaphore_wait(known.at[step], 2)

    loads[0].wait()
    cells = occ_v[...].reshape(64, 8).astype(F32).astype(BF16)
    pick = lax.broadcasted_iota(jnp.int32, (512, 64), 0) // 8
    pick = (pick == lax.broadcasted_iota(jnp.int32, (512, 64), 1)).astype(F32)
    spread = dot(pick.astype(BF16), cells)
    own = lax.broadcasted_iota(jnp.int32, (512, 8), 0) % 8
    own = own == lax.broadcasted_iota(jnp.int32, (512, 8), 1)
    column = jnp.sum(jnp.where(own, spread, 0.0), axis=1, keepdims=True)
    mask_v[...] = jnp.broadcast_to(column, (512, C)).reshape(8, 8, 8, C)

    def masked_of(source):
        return source[...].astype(F32) * mask_v[...]

    def fill_halo(which, value):
        edge_x = {1: value[7], -1: value[0]}
        edge_y = {1: value[:, 7], -1: value[:, 0]}
        for i in range(2):
            send_face[which, i] = edge_x[DIRS[i][0]].reshape(64, C).astype(BF16)
        for i in range(2, 4):
            send_face[which, i] = edge_y[DIRS[i][1]].reshape(64, C).astype(BF16)
        for i in range(4, 8):
            corner = edge_x[DIRS[i][0]][7 if DIRS[i][1] == 1 else 0]
            send_corner[which, i - 4] = jnp.concatenate([corner, corner], axis=0).astype(BF16)

    def halo_copies(which):
        copies = []
        for i in range(8):
            if i < 4:
                source, target = send_face.at[which, i], recv_face.at[which, i]
            else:
                source, target = send_corner.at[which, i - 4], recv_corner.at[which, i - 4]
            copies.append(
                pltpu.make_async_remote_copy(
                    src_ref=source,
                    dst_ref=target,
                    send_sem=halo_send.at[which, i],
                    recv_sem=halo_recv.at[which, i],
                    device_id=halo_peer(i),
                    device_id_type=MESH,
                )
            )
        return copies

    inside = {
        (0, 1): (space > 0).astype(F32),
        (0, -1): (space < n_space - 1).astype(F32),
        (1, 1): (tile > 0).astype(F32),
        (1, -1): (tile < n_tile - 1).astype(F32),
    }

    def place_halo(which):
        for i in range(8):
            ds, dt = DIRS[i]
            valid = 1.0
            if ds:
                valid = valid * inside[0, ds]
            if dt:
                valid = valid * inside[1, dt]
            row, col = {1: 0, -1: 9}.get(ds), {1: 0, -1: 9}.get(dt)
            if i < 4:
                value = recv_face[which, i].astype(F32).reshape(8, 8, C) * valid
            else:
                value = recv_corner[which, i - 4].astype(F32)[0:8] * valid
            if ds == 0:
                padded[1:9, col] = value
            elif dt == 0:
                padded[row, 1:9] = value
            else:
                padded[row, col] = value

    z_place = lax.broadcasted_iota(jnp.int32, (10, 8, C), 1)

    def widen(target):
        def slab(i, carry):
            value = padded[i]
            before = jnp.where(z_place == 0, 0.0, pltpu.roll(value, 1, 1))
            after = jnp.where(z_place == 7, 0.0, pltpu.roll(value, 7, 1))
            start = pl.multiple_of(i * 64, 64)
            for sy in range(3):
                for sz, shifted in enumerate((before, value, after)):
                    column = (3 * sy + sz) * C
                    target[pl.ds(start, 64), column : column + C] = (
                        shifted[sy : sy + 8].reshape(64, C).astype(BF16)
                    )
            return carry

        lax.fori_loop(0, 10, slab, 0)

    loads[1].wait()
    masked_grad = masked_of(cot_v)
    padded[1:9, 1:9] = masked_grad
    fill_halo(0, masked_grad)
    pl.semaphore_wait(barrier, 8 + 1 + (nx - 1) + (ny - 1) + 2)
    halo_g = halo_copies(0)
    for copy in halo_g:
        copy.start()
    tell(0)
    loads[2].wait()
    masked = masked_of(feat_v)
    fill_halo(1, masked)
    halo_f = halo_copies(1)
    for copy in halo_f:
        copy.start()
    features_t[...] = jnp.transpose(masked.reshape(512, C)).astype(BF16)

    for copy in halo_g:
        copy.wait_recv()
    hear(0)
    tell(1)
    place_halo(0)
    widen(wide_g)

    def terms(sx, first, last):
        for q in range(first, last, 2):
            end = min(q + 2, last)
            result = dot(features_t[...], wide_g[sx * 64 : sx * 64 + 512, q * C : end * C])
            for j in range(q, end):
                part[26 - (9 * sx + j)] = result[:, (j - q) * C : (j - q + 1) * C]

    mine = core * 14
    theirs = (1 - core) * 14

    def pair_copy(half):
        return pltpu.make_async_remote_copy(
            src_ref=part.at[pl.ds(theirs + 7 * half, 7)],
            dst_ref=pair_buf.at[pl.ds(7 * half, 7)],
            send_sem=pair_send.at[half],
            recv_sem=pair_recv.at[half],
            device_id=sibling,
            device_id_type=MESH,
        )

    def offset_terms(first):
        for sx in range(3):
            inside_sx = [26 - o - 9 * sx for o in range(first, min(first + 7, 27)) if (26 - o) // 9 == sx]
            if inside_sx:
                terms(sx, min(inside_sx), max(inside_sx) + 1)

    def for_core(first, second):
        @pl.when(core == 0)
        def _():
            offset_terms(first)

        @pl.when(core == 1)
        def _():
            offset_terms(second)

    part[27] = jnp.zeros((C, C), F32)
    pair = {}
    for half in (1, 0):
        for_core(14 + 7 * half, 7 * half)
        pair[half] = pair_copy(half)
        pair[half].start()

    first_size = {0: nx, 1: ny}
    second_size = {0: ny, 1: nx}
    first_block = {0: block, 1: block_y}
    first_place = {0: x * block, 1: y * block_y}
    second_place = {0: x * block + y * rows, 1: y * block_y + x * rows}

    def first_index(half, d):
        return x_peer(d + nx) if half == 0 else y_peer(d + ny)

    def first_device(half, d):
        if half == 0:
            return at(x_peer(d + nx), y, z, core)
        return at(x, y_peer(d + ny), z, core)

    def second_peer(half, d):
        return (x, y_peer(d)) if half == 0 else (x_peer(d), y)

    def first_start(half):
        size = first_block[half]
        for d in range(1, first_size[half]):
            start = pl.multiple_of(first_index(half, d) * size, 8)
            firsts[half, d] = pltpu.make_async_remote_copy(
                src_ref=part.at[pl.ds(mine + 7 * half, 7), pl.ds(start, size)],
                dst_ref=first_buf.at[half, d - 1, :, 0:size],
                send_sem=first_send.at[half, d - 1],
                recv_sem=first_recv.at[half, d - 1],
                device_id=first_device(half, d),
                device_id_type=MESH,
            )
            firsts[half, d].start()

    def second_copies(half):
        copies = []
        base = first_place[half]
        for d in range(1, second_size[half]):
            px, py = second_peer(half, d)
            index = py if half == 0 else px
            start = pl.multiple_of(base + index * rows, 8)
            copies.append(
                pltpu.make_async_remote_copy(
                    src_ref=part.at[pl.ds(mine + 7 * half, 7), pl.ds(start, rows)],
                    dst_ref=second_buf.at[half, d - 1],
                    send_sem=second_send.at[half, d - 1],
                    recv_sem=second_recv.at[half, d - 1],
                    device_id=at(px, py, z, core),
                    device_id_type=MESH,
                )
            )
        return copies

    def add_pair(half):
        pair[half].wait_recv()

        def one(i, carry):
            part[mine + 7 * half + i] = part[mine + 7 * half + i] + pair_buf[7 * half + i]
            return carry

        lax.fori_loop(0, 7, one, 0)

    def add_first(half):
        size = first_block[half]
        where = pl.ds(pl.multiple_of(first_place[half], 8), size)
        value = part[pl.ds(mine + 7 * half, 7), where]
        for d in range(1, first_size[half]):
            firsts[half, d].wait_recv()
            value = value + first_buf[half, d - 1, :, 0:size]
        part[pl.ds(mine + 7 * half, 7), where] = value

    def add_second(half, copies):
        for copy in copies:
            copy.wait_recv()
        where = pl.ds(pl.multiple_of(second_place[half], 8), rows)
        value = part[pl.ds(mine + 7 * half, 7), where]
        for d in range(1, second_size[half]):
            value = value + second_buf[half, d - 1]
        tiles[8 * half : 8 * half + 7] = value

    firsts, seconds = {}, {}
    for half in (1, 0):
        for_core(7 * half, 14 + 7 * half)
        if half == 1:
            hear(1)
            tell(2)
        add_pair(half)
        first_start(half)

    padded[1:9, 1:9] = masked_of(feat_v)
    for copy in halo_f:
        copy.wait_recv()
    place_halo(1)
    widen(wide_f)

    def convolved(wide, weight, target):
        value = dot(wide[0:512, :], weight(0))
        value = value + dot(wide[64:576, :], weight(1))
        value = value + dot(wide[128:640, :], weight(2))
        value = value.reshape(8, 8, 8, C) * mask_v[...]
        target[...] = value.astype(BF16)

    def flip(s, carry):
        start = pl.multiple_of(s * C, C)
        kern_t[pl.ds(start, C), :] = jnp.transpose(kern_v[26 - s].astype(F32)).astype(BF16)
        return carry

    def flips(part_of):
        lax.fori_loop(9 * part_of, 9 * part_of + 9, flip, 0, unroll=3)

    for half in (1, 0):
        add_first(half)
        seconds[half] = second_copies(half)
        for copy in seconds[half]:
            copy.start()
    def z_part(ref, owner):
        return ref.at[pl.ds(owner * per_owner, per_owner)]

    def near_device(d):
        return at(x, y, z_group * near + (z_near + d) % near, core)

    def z_copy(d):
        return pltpu.make_async_remote_copy(
            src_ref=z_part(tiles, (z_near + d) % near),
            dst_ref=z_part(z_buf, d - 1),
            send_sem=z_send,
            recv_sem=z_recv,
            device_id=near_device(d),
            device_id_type=MESH,
        )

    def zs_copy(d):
        return pltpu.make_async_remote_copy(
            src_ref=z_sum.at[z_group],
            dst_ref=z_sum.at[z_group],
            send_sem=zs_send,
            recv_sem=zs_recv,
            device_id=at(x, y, (z_group + d) % groups * near + z_near, core),
            device_id_type=MESH,
        )

    def zg_copy(d):
        return pltpu.make_async_remote_copy(
            src_ref=z_part(z_all, z_near),
            dst_ref=z_part(z_all, z_near),
            send_sem=zg_send,
            recv_sem=zg_recv,
            device_id=near_device(d),
            device_id_type=MESH,
        )

    def whole(ref, sends, receives):
        return pltpu.make_async_remote_copy(
            src_ref=ref,
            dst_ref=ref,
            send_sem=sends,
            recv_sem=receives,
            device_id=sibling,
            device_id_type=MESH,
        )

    z_whole = whole(z_buf, z_send, z_recv)
    zs_whole = whole(z_sum.at[0 : groups - 1], zs_send, zs_recv) if groups > 1 else None
    zg_whole = whole(z_buf, zg_send, zg_recv)

    hear(2)
    loads[3].wait()
    flips(0)
    for half in (1, 0):
        tiles[8 * half + 7] = jnp.zeros((rows, C), F32)
        add_second(half, seconds[half])
        for d in range(1, near):

            @pl.when((z_near + d) % near * 2 // near == half)
            def _():
                z_copy(d).start()

    flips(1)
    z_whole.wait_recv()
    value = tiles[pl.ds(z_near * per_owner, per_owner)]
    for d in range(1, near):
        value = value + z_buf[(d - 1) * per_owner : d * per_owner]
    z_sum[z_group] = value
    for d in range(1, groups):
        zs_copy(d).start()

    for copy in halo_g + halo_f + [pair[0], pair[1]]:
        copy.wait_send()
    for half in (1, 0):
        for copy in seconds[half]:
            copy.wait_send()
    for copy in firsts.values():
        copy.wait_send()
    z_whole.wait_send()

    convolved(wide_f, lambda a: kern_v[9 * a : 9 * a + 9].reshape(9 * C, C), out_v)
    out_copy = pltpu.make_async_copy(out_v, out_ref, out_sem.at[0])
    out_copy.start()

    if groups > 1:
        zs_whole.wait_recv()
    value = z_sum[0]
    for i in range(1, groups):
        value = value + z_sum[i]
    z_all[pl.ds(z_near * per_owner, per_owner)] = value * scale
    for d in range(1, near):
        zg_copy(d).start()

    def gathered(half, offsets, row, size):
        return total.at[pl.ds(offsets + 7 * half, 7), pl.ds(pl.multiple_of(row, 8), size)]

    def z_half(half):
        return z_all.at[8 * half : 8 * half + 7]

    def second_back(half, d, row):
        return pltpu.make_async_remote_copy(
            src_ref=z_half(half),
            dst_ref=gathered(half, mine, row, rows),
            send_sem=sg_send.at[half, d - 1],
            recv_sem=sg_recv.at[half, d - 1],
            device_id=at(*second_peer(half, d), z, core),
            device_id_type=MESH,
        )

    def first_back(half, d, index):
        size = first_block[half]
        return pltpu.make_async_remote_copy(
            src_ref=gathered(half, mine, index * size, size),
            dst_ref=gathered(half, mine, index * size, size),
            send_sem=fg_send.at[half, d - 1],
            recv_sem=fg_recv.at[half, d - 1],
            device_id=first_device(half, d),
            device_id_type=MESH,
        )

    def pair_back(half, d, offsets):
        size = first_block[half]
        row = first_index(half, -d) * size
        return pltpu.make_async_remote_copy(
            src_ref=gathered(half, offsets, row, size),
            dst_ref=gathered(half, offsets, row, size),
            send_sem=pg_send.at[half, d],
            recv_sem=pg_recv.at[half, d],
            device_id=sibling,
            device_id_type=MESH,
        )

    sent = []
    keeps = {}
    flips(2)
    zg_whole.wait_recv()
    for half in (1, 0):
        for d in range(1, second_size[half]):
            copy = second_back(half, d, second_place[half])
            copy.start()
            sent.append(copy)
        keeps[half] = pltpu.make_async_copy(
            z_half(half),
            gathered(half, mine, second_place[half], rows),
            own_sem.at[half],
        )
        keeps[half].start()
    for half in (1, 0):
        n = second_size[half]
        for d in range(1, n):
            from_index = ((y if half == 0 else x) - d + n) % n
            second_back(half, d, first_place[half] + from_index * rows).wait_recv()
        keeps[half].wait()
        for d in range(1, first_size[half]):
            copy = first_back(half, d, first_index(half, 0))
            copy.start()
            sent.append(copy)
        copy = pair_back(half, 0, mine)
        copy.start()
        sent.append(copy)

    convolved(wide_g, lambda a: kern_t[a * 9 * C : (a + 1) * 9 * C, :], fgrad_v)
    fgrad_copy = pltpu.make_async_copy(fgrad_v, fgrad_ref, out_sem.at[1])
    fgrad_copy.start()

    forwarded = []
    for d in (1, 3, 2):
        for half in (1, 0):
            if d < first_size[half]:
                first_back(half, d, first_index(half, -d)).wait_recv()
                copy = pair_back(half, d, mine)
                copy.start()
                forwarded.append(copy)
    zg_whole.wait_send()
    if groups > 1:
        zs_whole.wait_send()
    for copy in sent:
        copy.wait_send()
    out_copy.wait()
    fgrad_copy.wait()
    for d in (0, 1, 3, 2):
        for half in (1, 0):
            if d < first_size[half]:
                pair_back(half, d, theirs).wait_recv()
    for copy in forwarded:
        copy.wait_send()


def shards(chips, features, occupancy, weights, cotangent):
    nx, ny, nz = chips
    voxels = 512 * nx * ny * nz * 2
    scale = 1.0 / math.sqrt(voxels)
    rows = C // (nx * ny)
    near = min(4, nz)
    per_owner = 16 // near
    most = max(nx, ny)
    dma = pltpu.SemaphoreType.DMA
    results = pl.pallas_call(
        functools.partial(kernel, chips, scale),
        out_shape=(
            jax.ShapeDtypeStruct((8, 8, 8, C), BF16),
            jax.ShapeDtypeStruct((8, 8, 8, C), BF16),
            jax.ShapeDtypeStruct((28, C, C), F32),
        ),
        in_specs=[pl.BlockSpec(memory_space=pltpu.HBM)] * 4,
        out_specs=[pl.BlockSpec(memory_space=pl.ANY)] * 3,
        scratch_shapes=[
            pltpu.VMEM((8, 8, 8, C), BF16),
            pltpu.VMEM((8, 8, 8, C), BF16),
            pltpu.VMEM((8, 8, 8), jnp.int32),
            pltpu.VMEM((27, C, C), BF16),
            pltpu.VMEM((27 * C, C), BF16),
            pltpu.VMEM((8, 8, 8, C), F32),
            pltpu.VMEM((C, 512), BF16),
            pltpu.VMEM((10, 10, 8, C), F32),
            pltpu.VMEM((640, 9 * C), BF16),
            pltpu.VMEM((640, 9 * C), BF16),
            pltpu.VMEM((2, 4, 64, C), BF16),
            pltpu.VMEM((2, 4, 16, C), BF16),
            pltpu.VMEM((2, 4, 64, C), BF16),
            pltpu.VMEM((2, 4, 16, C), BF16),
            pltpu.VMEM((28, C, C), F32),
            pltpu.VMEM((14, C, C), F32),
            pltpu.VMEM((2, most - 1, 7, C // min(nx, ny), C), F32),
            pltpu.VMEM((2, most - 1, 7, rows, C), F32),
            pltpu.VMEM((16, rows, C), F32),
            pltpu.VMEM(((near - 1) * per_owner, rows, C), F32),
            pltpu.VMEM((nz // near, per_owner, rows, C), F32),
            pltpu.VMEM((16, rows, C), F32),
            pltpu.VMEM((8, 8, 8, C), BF16),
            pltpu.VMEM((8, 8, 8, C), BF16),
            dma((4,)),
            dma((2,)),
            dma((2,)),
            pltpu.SemaphoreType.REGULAR((3,)),
            dma((2, 8)),
            dma((2, 8)),
            dma((2,)),
            dma((2,)),
            dma((2, 6)),
            dma((2, 6)),
            dma((2, most - 1)),
            dma((2, most - 1)),
            dma,
            dma,
            dma,
            dma,
            dma,
            dma,
            dma((2, most - 1)),
            dma((2, most - 1)),
            dma((2, 6)),
            dma((2, 6)),
            dma((2, 7)),
            dma((2, 7)),
        ],
        compiler_params=pltpu.CompilerParams(
            collective_id=0, has_side_effects=True, vmem_limit_bytes=48 * 1024 * 1024
        ),
        cost_estimate=pl.CostEstimate(
            flops=3 * 2 * 512 * 27 * C * C, bytes_accessed=4_000_000, transcendentals=0
        ),
    )(*(pltpu.with_memory_space_constraint(a, pltpu.HBM) for a in (features, occupancy, weights, cotangent)))
    return results[0], results[1], results[2][:27]


def solution(mesh, chips=CHIPS):
    in_specs = (
        P("space", "tile", None, None),
        P("space", "tile", None),
        P(),
        P("space", "tile", None, None),
    )
    out_specs = (P("space", "tile", None, None), P("space", "tile", None, None), P())
    return jax.shard_map(
        functools.partial(shards, chips),
        mesh=mesh,
        in_specs=in_specs,
        out_specs=out_specs,
        check_vma=False,
    )
```

```python
import functools
import math

import jax
import jax.numpy as jnp
from jax import lax
from jax.experimental import pallas as pl
from jax.experimental.pallas import tpu as pltpu
from jax.sharding import PartitionSpec as P

MESH = pl.DeviceIdType.MESH
CHIPS = (4, 4, 16)
C = 128
DIRS = ((1, 0), (-1, 0), (0, 1), (0, -1), (1, 1), (1, -1), (-1, 1), (-1, -1))
F32 = jnp.float32
BF16 = jnp.bfloat16


def dot(a, b):
    return jnp.dot(a, b, preferred_element_type=F32)


def kernel(
    chips,
    scale,
    feat_hbm,
    occ_hbm,
    kern_hbm,
    cot_hbm,
    out_ref,
    fgrad_ref,
    total,
    feat_v,
    cot_v,
    occ_v,
    kern_v,
    kern_t,
    mask_v,
    features_t,
    padded,
    wide_f,
    wide_g,
    send_face,
    send_corner,
    recv_face,
    recv_corner,
    part,
    pair_buf,
    first_buf,
    second_buf,
    tiles,
    z_buf,
    z_sum,
    z_all,
    out_v,
    fgrad_v,
    in_sem,
    out_sem,
    own_sem,
    known,
    halo_send,
    halo_recv,
    pair_send,
    pair_recv,
    first_send,
    first_recv,
    second_send,
    second_recv,
    z_send,
    z_recv,
    zs_send,
    zs_recv,
    zg_send,
    zg_recv,
    sg_send,
    sg_recv,
    fg_send,
    fg_recv,
    pg_send,
    pg_recv,
):
    nx, ny, nz = chips
    n_space, n_tile = nx * nz, ny * 2
    space, tile = lax.axis_index("space"), lax.axis_index("tile")
    x, z = space // nz, space % nz
    y, core = tile // 2, tile % 2
    block = C // nx
    block_y = C // ny
    rows = C // (nx * ny)
    near = min(4, nz)
    groups = nz // near
    per_owner = 16 // near
    z_group, z_near = z // near, z % near

    def at(px, py, pz, pc):
        return {"space": px * nz + pz, "tile": py * 2 + pc}

    def x_peer(d):
        return (x + d) % nx

    def y_peer(d):
        return (y + d) % ny

    def z_peer(d):
        return (z + d) % nz

    def halo_peer(i):
        ds, dt = DIRS[i]
        return {
            "space": (space + ds + n_space) % n_space,
            "tile": (tile + dt + n_tile) % n_tile,
        }

    sibling = at(x, y, z, 1 - core)

    loads = [
        pltpu.make_async_copy(src, dst, in_sem.at[i])
        for i, (src, dst) in enumerate(
            ((occ_hbm, occ_v), (cot_hbm, cot_v), (feat_hbm, feat_v), (kern_hbm, kern_v))
        )
    ]
    for load in loads:
        load.start()

    barrier = pltpu.get_barrier_semaphore()

    def greet(device):
        pl.semaphore_signal(barrier, inc=1, device_id=device, device_id_type=MESH)

    for i in range(8):
        greet(halo_peer(i))
    greet(sibling)
    for d in range(1, nx):
        greet(at(x_peer(d), y, z, core))
    for d in range(1, ny):
        greet(at(x, y_peer(d), z, core))

    for d in (1, -1):
        greet(at(x, y, z_peer(d + nz), core))

    def tell(step):
        d = 2**step
        if d < nz // 2:
            for side in (d, -d):
                pl.semaphore_signal(
                    known.at[step],
                    inc=1,
                    device_id=at(x, y, z_peer(side + nz), core),
                    device_id_type=MESH,
                )

    def hear(step):
        if 2**step < nz // 2:
            pl.semaphore_wait(known.at[step], 2)

    loads[0].wait()
    cells = occ_v[...].reshape(64, 8).astype(F32).astype(BF16)
    pick = lax.broadcasted_iota(jnp.int32, (512, 64), 0) // 8
    pick = (pick == lax.broadcasted_iota(jnp.int32, (512, 64), 1)).astype(F32)
    spread = dot(pick.astype(BF16), cells)
    own = lax.broadcasted_iota(jnp.int32, (512, 8), 0) % 8
    own = own == lax.broadcasted_iota(jnp.int32, (512, 8), 1)
    column = jnp.sum(jnp.where(own, spread, 0.0), axis=1, keepdims=True)
    mask_v[...] = jnp.broadcast_to(column, (512, C)).reshape(8, 8, 8, C)

    def masked_of(source):
        return source[...].astype(F32) * mask_v[...]

    def fill_halo(which, value):
        edge_x = {1: value[7], -1: value[0]}
        edge_y = {1: value[:, 7], -1: value[:, 0]}
        for i in range(2):
            send_face[which, i] = edge_x[DIRS[i][0]].reshape(64, C).astype(BF16)
        for i in range(2, 4):
            send_face[which, i] = edge_y[DIRS[i][1]].reshape(64, C).astype(BF16)
        for i in range(4, 8):
            corner = edge_x[DIRS[i][0]][7 if DIRS[i][1] == 1 else 0]
            send_corner[which, i - 4] = jnp.concatenate([corner, corner], axis=0).astype(BF16)

    def halo_copies(which):
        copies = []
        for i in range(8):
            if i < 4:
                source, target = send_face.at[which, i], recv_face.at[which, i]
            else:
                source, target = send_corner.at[which, i - 4], recv_corner.at[which, i - 4]
            copies.append(
                pltpu.make_async_remote_copy(
                    src_ref=source,
                    dst_ref=target,
                    send_sem=halo_send.at[which, i],
                    recv_sem=halo_recv.at[which, i],
                    device_id=halo_peer(i),
                    device_id_type=MESH,
                )
            )
        return copies

    inside = {
        (0, 1): (space > 0).astype(F32),
        (0, -1): (space < n_space - 1).astype(F32),
        (1, 1): (tile > 0).astype(F32),
        (1, -1): (tile < n_tile - 1).astype(F32),
    }

    def place_halo(which):
        for i in range(8):
            ds, dt = DIRS[i]
            valid = 1.0
            if ds:
                valid = valid * inside[0, ds]
            if dt:
                valid = valid * inside[1, dt]
            row, col = {1: 0, -1: 9}.get(ds), {1: 0, -1: 9}.get(dt)
            if i < 4:
                value = recv_face[which, i].astype(F32).reshape(8, 8, C) * valid
            else:
                value = recv_corner[which, i - 4].astype(F32)[0:8] * valid
            if ds == 0:
                padded[1:9, col] = value
            elif dt == 0:
                padded[row, 1:9] = value
            else:
                padded[row, col] = value

    z_place = lax.broadcasted_iota(jnp.int32, (10, 8, C), 1)

    def widen(target):
        def slab(i, carry):
            value = padded[i]
            before = jnp.where(z_place == 0, 0.0, pltpu.roll(value, 1, 1))
            after = jnp.where(z_place == 7, 0.0, pltpu.roll(value, 7, 1))
            start = pl.multiple_of(i * 64, 64)
            for sy in range(3):
                for sz, shifted in enumerate((before, value, after)):
                    column = (3 * sy + sz) * C
                    target[pl.ds(start, 64), column : column + C] = (
                        shifted[sy : sy + 8].reshape(64, C).astype(BF16)
                    )
            return carry

        lax.fori_loop(0, 10, slab, 0)

    loads[1].wait()
    masked_grad = masked_of(cot_v)
    padded[1:9, 1:9] = masked_grad
    fill_halo(0, masked_grad)
    pl.semaphore_wait(barrier, 8 + 1 + (nx - 1) + (ny - 1) + 2)
    halo_g = halo_copies(0)
    for copy in halo_g:
        copy.start()
    tell(0)
    loads[2].wait()
    masked = masked_of(feat_v)
    fill_halo(1, masked)
    halo_f = halo_copies(1)
    for copy in halo_f:
        copy.start()
    hear(0)
    tell(1)
    features_t[...] = jnp.transpose(masked.reshape(512, C)).astype(BF16)

    for copy in halo_g:
        copy.wait_recv()
    place_halo(0)
    widen(wide_g)

    def terms(sx, first, last):
        for q in range(first, last, 2):
            end = min(q + 2, last)
            result = dot(features_t[...], wide_g[sx * 64 : sx * 64 + 512, q * C : end * C])
            for j in range(q, end):
                part[26 - (9 * sx + j)] = result[:, (j - q) * C : (j - q + 1) * C]

    mine = core * 14
    theirs = (1 - core) * 14

    def pair_copy(half):
        return pltpu.make_async_remote_copy(
            src_ref=part.at[pl.ds(theirs + 7 * half, 7)],
            dst_ref=pair_buf.at[pl.ds(7 * half, 7)],
            send_sem=pair_send.at[half],
            recv_sem=pair_recv.at[half],
            device_id=sibling,
            device_id_type=MESH,
        )

    hear(1)
    tell(2)

    def offset_terms(first):
        for sx in range(3):
            inside_sx = [26 - o - 9 * sx for o in range(first, min(first + 7, 27)) if (26 - o) // 9 == sx]
            if inside_sx:
                terms(sx, min(inside_sx), max(inside_sx) + 1)

    def for_core(first, second):
        @pl.when(core == 0)
        def _():
            offset_terms(first)

        @pl.when(core == 1)
        def _():
            offset_terms(second)

    part[27] = jnp.zeros((C, C), F32)
    pair = {}
    for half in (1, 0):
        for_core(14 + 7 * half, 7 * half)
        pair[half] = pair_copy(half)
        pair[half].start()

    first_size = {0: nx, 1: ny}
    second_size = {0: ny, 1: nx}
    first_order = {h: (2, 1, 3) if n == 4 else tuple(range(1, n)) for h, n in first_size.items()}
    first_block = {0: block, 1: block_y}
    first_place = {0: x * block, 1: y * block_y}
    second_place = {0: x * block + y * rows, 1: y * block_y + x * rows}

    def first_index(half, d):
        return x_peer(d + nx) if half == 0 else y_peer(d + ny)

    def first_device(half, d):
        if half == 0:
            return at(x_peer(d + nx), y, z, core)
        return at(x, y_peer(d + ny), z, core)

    def second_peer(half, d):
        return (x, y_peer(d)) if half == 0 else (x_peer(d), y)

    def first_start(half):
        size = first_block[half]
        for d in first_order[half]:
            start = pl.multiple_of(first_index(half, d) * size, 8)
            firsts[half, d] = pltpu.make_async_remote_copy(
                src_ref=part.at[pl.ds(mine + 7 * half, 7), pl.ds(start, size)],
                dst_ref=first_buf.at[half, d - 1, :, 0:size],
                send_sem=first_send.at[half, d - 1],
                recv_sem=first_recv.at[half, d - 1],
                device_id=first_device(half, d),
                device_id_type=MESH,
            )
            firsts[half, d].start()

    def second_copies(half):
        copies = []
        base = first_place[half]
        for d in range(1, second_size[half]):
            px, py = second_peer(half, d)
            index = py if half == 0 else px
            start = pl.multiple_of(base + index * rows, 8)
            copies.append(
                pltpu.make_async_remote_copy(
                    src_ref=part.at[pl.ds(mine + 7 * half, 7), pl.ds(start, rows)],
                    dst_ref=second_buf.at[half, d - 1],
                    send_sem=second_send.at[half, d - 1],
                    recv_sem=second_recv.at[half, d - 1],
                    device_id=at(px, py, z, core),
                    device_id_type=MESH,
                )
            )
        return copies

    def add_pair(half):
        pair[half].wait_recv()

        def one(i, carry):
            part[mine + 7 * half + i] = part[mine + 7 * half + i] + pair_buf[7 * half + i]
            return carry

        lax.fori_loop(0, 7, one, 0)

    def add_first(half):
        size = first_block[half]
        where = pl.ds(pl.multiple_of(first_place[half], 8), size)
        value = part[pl.ds(mine + 7 * half, 7), where]
        for d in range(1, first_size[half]):
            firsts[half, d].wait_recv()
            value = value + first_buf[half, d - 1, :, 0:size]
        part[pl.ds(mine + 7 * half, 7), where] = value

    def add_second(half, copies):
        for copy in copies:
            copy.wait_recv()
        where = pl.ds(pl.multiple_of(second_place[half], 8), rows)
        value = part[pl.ds(mine + 7 * half, 7), where]
        for d in range(1, second_size[half]):
            value = value + second_buf[half, d - 1]
        tiles[8 * half : 8 * half + 7] = value

    firsts, seconds = {}, {}
    for half in (1, 0):
        for_core(7 * half, 14 + 7 * half)
        add_pair(half)
        first_start(half)

    padded[1:9, 1:9] = masked_of(feat_v)
    for copy in halo_f:
        copy.wait_recv()
    place_halo(1)
    widen(wide_f)

    def convolved(wide, weight, target):
        value = dot(wide[0:512, :], weight(0))
        value = value + dot(wide[64:576, :], weight(1))
        value = value + dot(wide[128:640, :], weight(2))
        value = value.reshape(8, 8, 8, C) * mask_v[...]
        target[...] = value.astype(BF16)

    def flip(s, carry):
        start = pl.multiple_of(s * C, C)
        kern_t[pl.ds(start, C), :] = jnp.transpose(kern_v[26 - s].astype(F32)).astype(BF16)
        return carry

    def flips(part_of):
        lax.fori_loop(9 * part_of, 9 * part_of + 9, flip, 0, unroll=3)

    for half in (1, 0):
        add_first(half)
        seconds[half] = second_copies(half)
        for copy in seconds[half]:
            copy.start()
    def z_part(ref, owner):
        return ref.at[pl.ds(owner * per_owner, per_owner)]

    def near_device(d):
        return at(x, y, z_group * near + (z_near + d) % near, core)

    def z_copy(d):
        return pltpu.make_async_remote_copy(
            src_ref=z_part(tiles, (z_near + d) % near),
            dst_ref=z_part(z_buf, d - 1),
            send_sem=z_send,
            recv_sem=z_recv,
            device_id=near_device(d),
            device_id_type=MESH,
        )

    def zs_copy(d):
        return pltpu.make_async_remote_copy(
            src_ref=z_sum.at[z_group],
            dst_ref=z_sum.at[z_group],
            send_sem=zs_send,
            recv_sem=zs_recv,
            device_id=at(x, y, (z_group + d) % groups * near + z_near, core),
            device_id_type=MESH,
        )

    def zg_copy(d):
        return pltpu.make_async_remote_copy(
            src_ref=z_part(z_all, z_near),
            dst_ref=z_part(z_all, z_near),
            send_sem=zg_send,
            recv_sem=zg_recv,
            device_id=near_device(d),
            device_id_type=MESH,
        )

    def whole(ref, sends, receives):
        return pltpu.make_async_remote_copy(
            src_ref=ref,
            dst_ref=ref,
            send_sem=sends,
            recv_sem=receives,
            device_id=sibling,
            device_id_type=MESH,
        )

    z_whole = whole(z_buf, z_send, z_recv)
    zs_whole = whole(z_sum.at[0 : groups - 1], zs_send, zs_recv) if groups > 1 else None
    zg_whole = whole(z_buf, zg_send, zg_recv)

    hear(2)
    loads[3].wait()
    flips(0)
    for half in (1, 0):
        tiles[8 * half + 7] = jnp.zeros((rows, C), F32)
        add_second(half, seconds[half])
        for d in range(1, near):

            @pl.when((z_near + d) % near * 2 // near == half)
            def _():
                z_copy(d).start()

    flips(1)
    z_whole.wait_recv()
    value = tiles[pl.ds(z_near * per_owner, per_owner)]
    for d in range(1, near):
        value = value + z_buf[(d - 1) * per_owner : d * per_owner]
    z_sum[z_group] = value
    for d in range(1, groups):
        zs_copy(d).start()

    for copy in halo_g + halo_f + [pair[0], pair[1]]:
        copy.wait_send()
    for half in (1, 0):
        for copy in seconds[half]:
            copy.wait_send()
    for copy in firsts.values():
        copy.wait_send()
    z_whole.wait_send()

    convolved(wide_f, lambda a: kern_v[9 * a : 9 * a + 9].reshape(9 * C, C), out_v)
    out_copy = pltpu.make_async_copy(out_v, out_ref, out_sem.at[0])
    out_copy.start()

    if groups > 1:
        zs_whole.wait_recv()
    value = z_sum[0]
    for i in range(1, groups):
        value = value + z_sum[i]
    z_all[pl.ds(z_near * per_owner, per_owner)] = value * scale
    for d in range(1, near):
        zg_copy(d).start()

    def gathered(half, offsets, row, size):
        return total.at[pl.ds(offsets + 7 * half, 7), pl.ds(pl.multiple_of(row, 8), size)]

    def z_half(half):
        return z_all.at[8 * half : 8 * half + 7]

    def second_back(half, d, row):
        return pltpu.make_async_remote_copy(
            src_ref=z_half(half),
            dst_ref=gathered(half, mine, row, rows),
            send_sem=sg_send.at[half, d - 1],
            recv_sem=sg_recv.at[half, d - 1],
            device_id=at(*second_peer(half, d), z, core),
            device_id_type=MESH,
        )

    def first_back(half, d, index):
        size = first_block[half]
        return pltpu.make_async_remote_copy(
            src_ref=gathered(half, mine, index * size, size),
            dst_ref=gathered(half, mine, index * size, size),
            send_sem=fg_send.at[half, d - 1],
            recv_sem=fg_recv.at[half, d - 1],
            device_id=first_device(half, d),
            device_id_type=MESH,
        )

    def pair_back(half, d, offsets):
        size = first_block[half]
        row = first_index(half, -d) * size
        return pltpu.make_async_remote_copy(
            src_ref=gathered(half, offsets, row, size),
            dst_ref=gathered(half, offsets, row, size),
            send_sem=pg_send.at[half, d],
            recv_sem=pg_recv.at[half, d],
            device_id=sibling,
            device_id_type=MESH,
        )

    sent = []
    keeps = {}
    flips(2)
    zg_whole.wait_recv()
    for half in (1, 0):
        for d in range(1, second_size[half]):
            copy = second_back(half, d, second_place[half])
            copy.start()
            sent.append(copy)
        keeps[half] = pltpu.make_async_copy(
            z_half(half),
            gathered(half, mine, second_place[half], rows),
            own_sem.at[half],
        )
        keeps[half].start()
    for half in (1, 0):
        n = second_size[half]
        for d in range(1, n):
            from_index = ((y if half == 0 else x) - d + n) % n
            second_back(half, d, first_place[half] + from_index * rows).wait_recv()
        keeps[half].wait()
        for d in first_order[half]:
            copy = first_back(half, d, first_index(half, 0))
            copy.start()
            sent.append(copy)
        copy = pair_back(half, 0, mine)
        copy.start()
        sent.append(copy)

    convolved(wide_g, lambda a: kern_t[a * 9 * C : (a + 1) * 9 * C, :], fgrad_v)
    fgrad_copy = pltpu.make_async_copy(fgrad_v, fgrad_ref, out_sem.at[1])
    fgrad_copy.start()

    forwarded = []
    for d in (1, 3, 2):
        for half in (1, 0):
            if d < first_size[half]:
                first_back(half, d, first_index(half, -d)).wait_recv()
                copy = pair_back(half, d, mine)
                copy.start()
                forwarded.append(copy)
    zg_whole.wait_send()
    if groups > 1:
        zs_whole.wait_send()
    for copy in sent:
        copy.wait_send()
    out_copy.wait()
    fgrad_copy.wait()
    for d in (0, 1, 3, 2):
        for half in (1, 0):
            if d < first_size[half]:
                pair_back(half, d, theirs).wait_recv()
    for copy in forwarded:
        copy.wait_send()


def shards(chips, features, occupancy, weights, cotangent):
    nx, ny, nz = chips
    voxels = 512 * nx * ny * nz * 2
    scale = 1.0 / math.sqrt(voxels)
    rows = C // (nx * ny)
    near = min(4, nz)
    per_owner = 16 // near
    most = max(nx, ny)
    dma = pltpu.SemaphoreType.DMA
    results = pl.pallas_call(
        functools.partial(kernel, chips, scale),
        out_shape=(
            jax.ShapeDtypeStruct((8, 8, 8, C), BF16),
            jax.ShapeDtypeStruct((8, 8, 8, C), BF16),
            jax.ShapeDtypeStruct((28, C, C), F32),
        ),
        in_specs=[pl.BlockSpec(memory_space=pltpu.HBM)] * 4,
        out_specs=[pl.BlockSpec(memory_space=pl.ANY)] * 3,
        scratch_shapes=[
            pltpu.VMEM((8, 8, 8, C), BF16),
            pltpu.VMEM((8, 8, 8, C), BF16),
            pltpu.VMEM((8, 8, 8), jnp.int32),
            pltpu.VMEM((27, C, C), BF16),
            pltpu.VMEM((27 * C, C), BF16),
            pltpu.VMEM((8, 8, 8, C), F32),
            pltpu.VMEM((C, 512), BF16),
            pltpu.VMEM((10, 10, 8, C), F32),
            pltpu.VMEM((640, 9 * C), BF16),
            pltpu.VMEM((640, 9 * C), BF16),
            pltpu.VMEM((2, 4, 64, C), BF16),
            pltpu.VMEM((2, 4, 16, C), BF16),
            pltpu.VMEM((2, 4, 64, C), BF16),
            pltpu.VMEM((2, 4, 16, C), BF16),
            pltpu.VMEM((28, C, C), F32),
            pltpu.VMEM((14, C, C), F32),
            pltpu.VMEM((2, most - 1, 7, C // min(nx, ny), C), F32),
            pltpu.VMEM((2, most - 1, 7, rows, C), F32),
            pltpu.VMEM((16, rows, C), F32),
            pltpu.VMEM(((near - 1) * per_owner, rows, C), F32),
            pltpu.VMEM((nz // near, per_owner, rows, C), F32),
            pltpu.VMEM((16, rows, C), F32),
            pltpu.VMEM((8, 8, 8, C), BF16),
            pltpu.VMEM((8, 8, 8, C), BF16),
            dma((4,)),
            dma((2,)),
            dma((2,)),
            pltpu.SemaphoreType.REGULAR((3,)),
            dma((2, 8)),
            dma((2, 8)),
            dma((2,)),
            dma((2,)),
            dma((2, 6)),
            dma((2, 6)),
            dma((2, most - 1)),
            dma((2, most - 1)),
            dma,
            dma,
            dma,
            dma,
            dma,
            dma,
            dma((2, most - 1)),
            dma((2, most - 1)),
            dma((2, 6)),
            dma((2, 6)),
            dma((2, 7)),
            dma((2, 7)),
        ],
        compiler_params=pltpu.CompilerParams(
            collective_id=0, has_side_effects=True, vmem_limit_bytes=48 * 1024 * 1024
        ),
        cost_estimate=pl.CostEstimate(
            flops=3 * 2 * 512 * 27 * C * C, bytes_accessed=4_000_000, transcendentals=0
        ),
    )(*(pltpu.with_memory_space_constraint(a, pltpu.HBM) for a in (features, occupancy, weights, cotangent)))
    return results[0], results[1], results[2][:27]


def solution(mesh, chips=CHIPS):
    in_specs = (
        P("space", "tile", None, None),
        P("space", "tile", None),
        P(),
        P("space", "tile", None, None),
    )
    out_specs = (P("space", "tile", None, None), P("space", "tile", None, None), P())
    return jax.shard_map(
        functools.partial(shards, chips),
        mesh=mesh,
        in_specs=in_specs,
        out_specs=out_specs,
        check_vma=False,
    )
```
